32 devices in a mesh: dp: 16 (over z, y, x), mp: 2 (over core).
Axes of the slice: x: 2, y: 2, z: 4, core: 2. Of those that a mesh axis runs over, the one named last changes fastest.
Arguments:
- tokens: bfloat16 [65536, 128], P(('dp', 'mp')), may hold values from -6 to 6
- stem_norm: bfloat16 [128], replicated, may hold values from 0.5 to 1.5
- stem_latent: bfloat16 [16, 128], replicated, may hold values from -6 to 6
- stem_wq: bfloat16 [128, 128], P(None, 'mp'), may hold values from -0.5 to 0.5
- stem_wkv: bfloat16 [2, 128, 128], P(None, None, 'mp'), may hold values from -0.5 to 0.5
- stem_wo: bfloat16 [128, 128], P('mp'), may hold values from -2 to 2
- norm_attn: bfloat16 [2, 128], replicated, may hold values from 0.5 to 1.5
- w_qkv: bfloat16 [2, 3, 128, 128], P(None, None, None, 'mp'), may hold values from -0.5 to 0.5
- w_out: bfloat16 [2, 128, 128], P(None, 'mp'), may hold values from -1 to 1
- norm_mlp: bfloat16 [2, 128], replicated, may hold values from 0.5 to 1.5
- w_up: bfloat16 [2, 128, 512], P(None, None, 'mp'), may hold values from -0.5 to 0.5
- b_up: bfloat16 [2, 512], P(None, 'mp'), may hold values from -3 to 3
- w_down: bfloat16 [2, 512, 128], P(None, 'mp'), may hold values from -0.25 to 0.25
- b_down: bfloat16 [2, 128], replicated, may hold values from -2 to 2
- w_act: bfloat16 [128, 128], replicated, may hold values from -0.125 to 0.125
- b_act: bfloat16 [128], replicated, may hold values from -3 to 3
- span_len: int32 [256], P(('dp', 'mp')), may hold values from 4 to 16
- joint_mask: int32 [256, 8], P(('dp', 'mp')), may hold values 0 or 1
- targets: float32 [256, 128], P(('dp', 'mp')), may hold values from -6 to 6
Outputs:
- actions: float32 [256, 128], P(('dp', 'mp'))
- masked_loss: float32 [], replicated
- grad_tokens: float32 [65536, 128], P(('dp', 'mp'))
- grad_stem_norm: float32 [128], replicated
- grad_stem_latent: float32 [16, 128], replicated
- grad_stem_wq: float32 [128, 128], P(None, 'mp')
- grad_stem_wkv: float32 [2, 128, 128], P(None, None, 'mp')
- grad_stem_wo: float32 [128, 128], P('mp')
- grad_norm_attn: float32 [2, 128], replicated
- grad_w_qkv: float32 [2, 3, 128, 128], P(None, None, None, 'mp')
- grad_w_out: float32 [2, 128, 128], P(None, 'mp')
- grad_norm_mlp: float32 [2, 128], replicated
- grad_w_up: float32 [2, 128, 512], P(None, None, 'mp')
- grad_b_up: float32 [2, 512], P(None, 'mp')
- grad_w_down: float32 [2, 512, 128], P(None, 'mp')
- grad_b_down: float32 [2, 128], replicated
- grad_w_act: float32 [128, 128], replicated
- grad_b_act: float32 [128], replicated
The draws below stay inside these ranges and needn't reach their ends.
All inputs are finite; a program needn't handle non-finite values. No bound on the sum of `joint_mask` on one device may be relied on, other than what follows from the above.
Results may differ from the reference program's by a relative error of at most 0.019.
Values may be sent and summed in bfloat16 or wider, within the bound.
A program may use at most 64 MiB of HBM per device.

```python
import jax
import jax.numpy as jnp
from jax import lax

D = 128
HEADS = 8
HD = 16
FF = 512
LAT = 16
SEQ_LEN = 256
SPAN = 16
JOINTS = 8
LAYERS = 2
SEQS = 256
TOKENS = 65536
AC = 128


def with_ends(values, stream_key, smallest, top_value):
    longest = values.shape.index(max(values.shape))
    spots = []
    for shift in (0, 1):
        where = [jax.random.randint(jax.random.fold_in(stream_key, axis), (), 0, length) for axis, length in enumerate(values.shape)]
        where[longest] = (where[longest] + shift) % values.shape[longest]
        spots.append(tuple(where))
    return values.at[spots[0]].set(smallest).at[spots[1]].set(top_value)


def steps_of(stream_key, extent, shards, smallest, largest):
    level, own = 1.0, jax.random.fold_in(stream_key, 6)
    for position, blocks in shards:
        steps = jnp.exp(jax.random.uniform(jax.random.fold_in(own, position), (blocks,), jnp.float32, smallest / len(shards), largest / len(shards)))
        level = level * jnp.repeat(steps, extent[position] // blocks).reshape([-1 if axis == position else 1 for axis in range(len(extent))])
    return level


def noise(stream_key, extent, spread, reach, split=(), dtype=jnp.bfloat16):
    drawn = jax.random.normal(stream_key, extent, jnp.float32) * spread
    if len(split) > 0:
        drawn = steps_of(stream_key, extent, split, -0.22, 0.18) * drawn
    return jnp.clip(drawn, min=-reach, max=reach).astype(dtype)


def setup_inputs(seed: int = 0) -> dict:
    arg_keys = jax.random.split(jax.random.key(seed), 20)
    return {
        "tokens": noise(arg_keys[0], (TOKENS, D), 1.0, 6.0, ((0, 32),)),
        "stem_norm": jnp.clip(1.0 + 0.1 * jax.random.normal(arg_keys[1], (D,), jnp.float32), 0.5, 1.5).astype(jnp.bfloat16),
        "stem_latent": noise(arg_keys[2], (LAT, D), 1.0, 6.0),
        "stem_wq": noise(arg_keys[3], (D, D), D ** -0.5, 0.5, ((1, 2),)),
        "stem_wkv": noise(arg_keys[4], (2, D, D), D ** -0.5, 0.5, ((2, 2),)),
        "stem_wo": noise(arg_keys[5], (D, D), (D // 16) ** -0.5, 2.0, ((0, 2),)),
        "norm_attn": jnp.clip(1.0 + 0.1 * jax.random.normal(arg_keys[6], (LAYERS, D), jnp.float32), 0.5, 1.5).astype(jnp.bfloat16),
        "w_qkv": noise(arg_keys[7], (LAYERS, 3, D, D), D ** -0.5, 0.5, ((3, 2),)),
        "w_out": noise(arg_keys[8], (LAYERS, D, D), (D // 4) ** -0.5, 1.0, ((1, 2),)),
        "norm_mlp": jnp.clip(1.0 + 0.1 * jax.random.normal(arg_keys[9], (LAYERS, D), jnp.float32), 0.5, 1.5).astype(jnp.bfloat16),
        "w_up": noise(arg_keys[10], (LAYERS, D, FF), D ** -0.5, 0.5, ((2, 2),)),
        "b_up": noise(arg_keys[11], (LAYERS, FF), 0.5, 3.0, ((1, 2),)),
        "w_down": noise(arg_keys[12], (LAYERS, FF, D), FF ** -0.5, 0.25, ((1, 2),)),
        "b_down": noise(arg_keys[13], (LAYERS, D), 0.3, 2.0),
        "w_act": noise(arg_keys[14], (D, AC), (D * LAT) ** -0.5, 0.125),
        "b_act": noise(arg_keys[15], (AC,), 0.5, 3.0),
        "span_len": with_ends(jax.random.randint(arg_keys[16], (SEQS,), SPAN // 4, SPAN + 1), jax.random.fold_in(arg_keys[16], 1), SPAN // 4, SPAN).astype(jnp.int32),
        "joint_mask": with_ends((jax.random.randint(arg_keys[17], (SEQS, JOINTS), 0, 4) < 3).astype(jnp.int32), jax.random.fold_in(arg_keys[17], 1), 0, 1),
        "targets": noise(arg_keys[18], (SEQS, AC), 1.0, 6.0, ((0, 32),), jnp.float32),
    }


highest = lax.Precision.HIGHEST
epsilon = 1e-05

@jax.custom_vjp
def low(v):
    return lax.optimization_barrier(v.astype(jnp.bfloat16)).astype(jnp.float32)

@jax.custom_vjp
def low_back(v):
    return v

def low_keep(v):
    return (low(v), None)

def low_pass(kept, grad):
    return (grad,)

def back_keep(v):
    return (v, None)

def back_low(kept, grad):
    return (low(grad),)
low.defvjp(low_keep, low_pass)
low_back.defvjp(back_keep, back_low)

def matmul_high(left, right):
    return jnp.matmul(left, right, precision=highest)

def layer_norm(values_in, gain_vec):
    mean_rows = lax.optimization_barrier(jnp.mean(values_in, axis=-1, keepdims=True))
    centred = values_in - mean_rows
    variance = lax.optimization_barrier(jnp.mean(centred * centred, axis=-1, keepdims=True))
    return centred * lax.rsqrt(variance + epsilon) * gain_vec

def attention(queries, key_rows, value_rows):
    scores = low_back(jnp.einsum('bqhe,bkhe->bhqk', queries, key_rows, precision=highest) * HD ** (-0.5))
    attn_probs = jax.nn.softmax(scores, axis=-1)
    mixed_heads = jnp.einsum('bhqk,bkhe->bqhe', low(attn_probs), value_rows, precision=highest)
    return low_back(low(mixed_heads))

def forward(tokens, stem_norm, stem_latent, stem_wq, stem_wkv, stem_wo, norm_attn, w_qkv, w_out, norm_mlp, w_up, b_up, w_down, b_down, w_act, b_act):
    stem_queries = low(matmul_high(stem_latent, stem_wq)).reshape(1, LAT, HEADS, HD)

    def stem_block(seq_group):
        group_size = seq_group.shape[0]
        normed = low(layer_norm(seq_group, stem_norm))
        key_rows = low_back(low(matmul_high(normed, stem_wkv[0]))).reshape(group_size, SEQ_LEN, HEADS, HD)
        value_rows = low_back(low(matmul_high(normed, stem_wkv[1]))).reshape(group_size, SEQ_LEN, HEADS, HD)
        queries = jnp.broadcast_to(stem_queries, (group_size, LAT, HEADS, HD))
        mixed_heads = attention(queries, key_rows, value_rows).reshape(group_size, LAT, D)
        return low_back(matmul_high(mixed_heads, stem_wo))
    branch = lax.map(jax.checkpoint(stem_block), tokens.reshape(SEQS // 16, 16, SEQ_LEN, D))
    residual = (stem_latent + branch).reshape(SEQS * LAT, D)
    head_shape = (SEQS, LAT, HEADS, HD)
    for layer_idx in range(LAYERS):
        normed = low(layer_norm(residual, norm_attn[layer_idx]))
        queries = low_back(low(matmul_high(normed, w_qkv[layer_idx, 0]))).reshape(head_shape)
        key_rows = low_back(low(matmul_high(normed, w_qkv[layer_idx, 1]))).reshape(head_shape)
        value_rows = low_back(low(matmul_high(normed, w_qkv[layer_idx, 2]))).reshape(head_shape)
        mixed_heads = attention(queries, key_rows, value_rows).reshape(SEQS * LAT, D)
        residual = residual + low_back(matmul_high(mixed_heads, w_out[layer_idx]))
        normed = low(layer_norm(residual, norm_mlp[layer_idx]))
        up_rows = low_back(matmul_high(normed, w_up[layer_idx]) + b_up[layer_idx])
        hidden_act = low(jax.nn.gelu(up_rows, approximate=False))
        residual = residual + low_back(matmul_high(hidden_act, w_down[layer_idx]) + b_down[layer_idx])
    pooled = lax.optimization_barrier(jnp.sum(residual.reshape(SEQS, LAT, D), axis=1))
    return matmul_high(pooled, w_act) + b_act

def reference(tokens, stem_norm, stem_latent, stem_wq, stem_wkv, stem_wo, norm_attn, w_qkv, w_out, norm_mlp, w_up, b_up, w_down, b_down, w_act, b_act, span_len, joint_mask, targets):
    params = tuple((arg_val.astype(jnp.float32) for arg_val in (tokens, stem_norm, stem_latent, stem_wq, stem_wkv, stem_wo, norm_attn, w_qkv, w_out, norm_mlp, w_up, b_up, w_down, b_down, w_act, b_act)))
    pred, pullback = jax.vjp(forward, *params)
    steps_grid = lax.broadcasted_iota(jnp.int32, (SPAN, JOINTS), 0)
    valid_mask = ((steps_grid[None] < span_len[:, None, None]) & (joint_mask[:, None, :] > 0)).astype(jnp.float32).reshape(SEQS, AC)
    entries = jnp.sum(valid_mask)
    errors = pred - targets.astype(jnp.float32)
    squares = jnp.sum(valid_mask * errors * errors)
    grad_list = pullback(SEQS * AC / entries * valid_mask * errors)
    return (valid_mask * pred, squares / entries, grad_list[0], grad_list[1], grad_list[2], grad_list[3], grad_list[4], grad_list[5], grad_list[6], grad_list[7], grad_list[8], grad_list[9], grad_list[10], grad_list[11], grad_list[12], grad_list[13], grad_list[14], grad_list[15])
```

```python
import functools

import jax
import jax.numpy as jnp
from jax import lax
from jax.experimental import pallas as pl
from jax.experimental.pallas import tpu as pltpu
from jax.sharding import PartitionSpec as P

HD = 16
LAT = 16
SEQ_LEN = 256
SPAN = 16
JOINTS = 8
HEADS = 8
D = 128
FF = 512
AC = 128
LAYERS = 2

F32 = jnp.float32
BF = jnp.bfloat16
MESH = pl.DeviceIdType.MESH
epsilon = 1e-05
highest = lax.Precision.HIGHEST

CHUNKS = (640, 256, 512, 384)
TAIL = 112


def nn(left, right):
    return jnp.dot(left, right, preferred_element_type=F32)


def nt(left, right):
    return lax.dot_general(left, right, (((1,), (1,)), ((), ())), preferred_element_type=F32)


def tn(left, right):
    return lax.dot_general(left, right, (((0,), (0,)), ((), ())), preferred_element_type=F32)


def iota(shape, axis):
    return lax.broadcasted_iota(jnp.int32, shape, axis)


def radices_of(count):
    found = []
    while count > 1:
        radix = 4 if count % 4 == 0 else 2
        found.append(radix)
        count //= radix
    return found


def flip(digit, offset):
    if offset == 1:
        return digit + 1 - 2 * (digit % 2)
    if offset == 2:
        return (digit + 2) % 4
    return 3 - digit


def norm_rows(values_in, gain_vec):
    mean_rows = jnp.mean(values_in, axis=-1, keepdims=True)
    centred = values_in - mean_rows
    variance = jnp.mean(centred * centred, axis=-1, keepdims=True)
    inv_rows = lax.rsqrt(variance + epsilon)
    unit_rows = centred * inv_rows
    return unit_rows * gain_vec, unit_rows, inv_rows


def norm_back(upstream, unit_rows, inv_rows, gain_vec):
    scaled = upstream * gain_vec
    inner = (
        scaled
        - jnp.mean(scaled, axis=-1, keepdims=True)
        - unit_rows * jnp.mean(scaled * unit_rows, axis=-1, keepdims=True)
    )
    return inv_rows * inner


def split_rows(values_in):
    first = values_in.astype(BF).astype(F32)
    rest = values_in - first
    second = rest.astype(BF).astype(F32)
    return jnp.concatenate([first, second, rest - second], axis=0).astype(BF)


def main_kernel(
    radices,
    tokens_h,
    stem_norm_h,
    stem_latent_h,
    stem_wq_h,
    stem_wkv_h,
    stem_wo_h,
    norm_attn_h,
    w_qkv_h,
    w_out_h,
    norm_mlp_h,
    w_up_h,
    b_up_h,
    w_down_h,
    b_down_h,
    w_act_h,
    b_act_h,
    span_len_h,
    joint_mask_h,
    targets_h,
    grad_tokens,
    fin_a,
    fin_b,
    fin_c,
    fin_d,
    tail_out,
    wq_out,
    head_out,
    x_v,
    stem_norm_v,
    stem_latent_v,
    wq_v,
    wkv_v,
    wo_v,
    norm_attn_v,
    wqkv_v,
    wout_v,
    norm_mlp_v,
    wup_v,
    bup_v,
    wdn_v,
    b_down_v,
    w_act_v,
    b_act_v,
    span_s,
    joint_v,
    targets_v,
    next_v,
    unit_v,
    inv_v,
    e_v,
    ds_v,
    small_v,
    ent_v,
    ent_r,
    own,
    oth,
    rcv,
    snd,
    rs_r,
    part,
    full_r,
    tail_s,
    tail_r,
    in_sem,
    send_sem,
    recv_sem,
):
    dp, mp = lax.axis_index("dp"), lax.axis_index("mp")
    own_seqs = targets_h.shape[0]
    rows = own_seqs * LAT
    fins = (fin_a, fin_b, fin_c, fin_d)
    core = (dp, 1 - mp)
    strides, digits = [], []
    stride = 1
    for radix in radices:
        strides.append(stride)
        digits.append((dp // stride) % radix)
        stride *= radix

    def partner(level, offset):
        digit = digits[level]
        return (dp + (flip(digit, offset) - digit) * strides[level], mp)

    barrier = pltpu.get_barrier_semaphore()
    greeted = [core]
    for level, radix in enumerate(radices):
        greeted += [partner(level, offset) for offset in range(1, radix)]
    for device in greeted:
        pl.semaphore_signal(barrier, inc=1, device_id=device, device_id_type=MESH)

    slots = [0]
    sends = []

    def remote(src, dst, device):
        slot = slots[0]
        slots[0] += 1
        copy = pltpu.make_async_remote_copy(
            src_ref=src,
            dst_ref=dst,
            send_sem=send_sem.at[slot],
            recv_sem=recv_sem.at[slot],
            device_id=device,
            device_id_type=MESH,
        )
        copy.start()
        sends.append(copy)
        return copy

    local = {}
    pairs = (
        ("tokens", tokens_h, x_v),
        ("stem_norm", stem_norm_h, stem_norm_v),
        ("stem_latent", stem_latent_h, stem_latent_v),
        ("wq", stem_wq_h, wq_v.at[0]),
        ("wkv", stem_wkv_h, wkv_v.at[0]),
        ("wo", stem_wo_h, wo_v.at[0]),
        ("wqkv", w_qkv_h, wqkv_v.at[0]),
        ("wout", w_out_h, wout_v.at[0]),
        ("wup", w_up_h, wup_v.at[0]),
        ("wdn", w_down_h, wdn_v.at[0]),
        ("norm_attn", norm_attn_h, norm_attn_v),
        ("norm_mlp", norm_mlp_h, norm_mlp_v),
        ("bup", b_up_h, bup_v.at[0]),
        ("b_down", b_down_h, b_down_v),
        ("w_act", w_act_h, w_act_v),
        ("b_act", b_act_h, b_act_v),
        ("span", span_len_h, span_s),
        ("joint", joint_mask_h, joint_v),
        ("targets", targets_h, targets_v),
    )
    for place, (name, src, dst) in enumerate(pairs):
        local[name] = pltpu.make_async_copy(src, dst, in_sem.at[place])
        local[name].start()

    head_mask = (
        (iota((HEADS, D, D), 2) // HD == iota((HEADS, D, D), 0)).astype(F32).astype(BF)
    )
    row_mask = (iota((HEADS, D, D), 1) // HD == iota((HEADS, D, D), 0)).astype(F32).astype(BF)
    diag_heads = (iota((D, D), 0) // LAT == iota((D, D), 1) // HD).astype(F32)
    block_add = jnp.where(iota((rows, rows), 0) // LAT == iota((rows, rows), 1) // LAT, 0.0, -1e30)
    mean_mat = jnp.full((D, D), 1.0 / D, BF)
    mean_twice = jnp.full((2 * D, D), 1.0 / D, BF)

    pl.semaphore_wait(barrier, len(greeted))
    gathered = {}
    for name, src, dst in (
        ("wq", stem_wq_h, wq_v.at[1]),
        ("wkv", stem_wkv_h, wkv_v.at[1]),
        ("wo", stem_wo_h, wo_v.at[1]),
        ("wqkv", w_qkv_h, wqkv_v.at[1]),
        ("wout", w_out_h, wout_v.at[1]),
        ("wup", w_up_h, wup_v.at[1]),
        ("wdn", w_down_h, wdn_v.at[1]),
        ("bup", b_up_h, bup_v.at[1]),
    ):
        gathered[name] = remote(src, dst, core)

    local["span"].wait()
    local["joint"].wait()
    spans = jnp.zeros((own_seqs, AC), jnp.int32)
    for seq in range(own_seqs):
        spans = jnp.where(iota((own_seqs, AC), 0) == seq, span_s[seq], spans)
    joints = (joint_v[...] > 0).astype(F32).astype(BF)
    spread = (iota((JOINTS, AC), 1) % JOINTS == iota((JOINTS, AC), 0)).astype(F32).astype(BF)
    valid = jnp.where(iota((own_seqs, AC), 1) // JOINTS < spans, nn(joints, spread), 0.0)
    ent_v[0] = jnp.broadcast_to(jnp.sum(valid, axis=0, keepdims=True), (8, AC))
    pending = [remote(ent_v.at[0], ent_r.at[0], core)]

    def entries_step(level):
        for copy in pending:
            copy.wait_recv()
        if level == 0:
            total = ent_v[0] + ent_r[0]
        else:
            total = tree(ent_v[level], [ent_r[at] for at in ent_slots[-1]])
        if level == len(radices):
            return total
        ent_v[level + 1] = total
        pending.clear()
        places = []
        for offset in range(1, radices[level]):
            place = 1 + sum(radices[:level]) - level + offset - 1
            places.append(place)
            pending.append(remote(ent_v.at[level + 1], ent_r.at[place], partner(level, offset)))
        ent_slots.append(places)
        return None

    ent_slots = []

    def tree(mine, others):
        if len(others) == 1:
            return mine + others[0]
        return (mine + others[0]) + (others[1] + others[2])

    local["tokens"].wait()
    local["stem_norm"].wait()
    stem_gain = stem_norm_v[...].astype(F32).reshape(1, D)
    half = own_seqs * SEQ_LEN // 2
    for start in (0, half):
        at = pl.ds(start, half)
        raw = x_v[at, :]
        centred = raw.astype(F32) - nn(raw, mean_mat)
        square = centred * centred
        upper = square.astype(BF)
        lower = (square - upper.astype(F32)).astype(BF)
        inv = lax.rsqrt(nn(jnp.concatenate([upper, lower], axis=1), mean_twice) + epsilon)
        unit = centred * inv
        inv_v[at, :] = inv
        unit_v[at, :] = unit
        next_v[at, 0:D] = (unit * stem_gain).astype(BF)
        next_v[at, D : 2 * D] = jnp.ones((half, D), BF)

    def both(ref, *index):
        return jnp.concatenate([ref[(0,) + index], ref[(1,) + index]], axis=0)

    entries_step(0)
    local["stem_latent"].wait()
    for name in ("wq", "wkv"):
        local[name].wait()
        gathered[name].wait_recv()
    latent = stem_latent_v[...]
    wq_t = both(wq_v)
    wk_t, wv_t = both(wkv_v, 0), both(wkv_v, 1)
    stem_q = (nt(latent, wq_t).astype(BF).astype(F32) * HD ** (-0.5)).astype(BF)
    q_diag = (jnp.concatenate([stem_q] * HEADS, axis=0).astype(F32) * diag_heads).astype(BF)
    fold = nn(q_diag, wk_t)
    fold_b = fold.astype(BF)
    mixed, shares, tops = [], [], []
    for seq in range(own_seqs):
        at = pl.ds(seq * SEQ_LEN, SEQ_LEN)
        scores = nt(fold_b, next_v[at, 0:D])
        probs = jnp.exp(scores - jnp.max(scores, axis=1, keepdims=True)).astype(BF)
        e_v[:, seq * SEQ_LEN : (seq + 1) * SEQ_LEN] = probs
        both_sums = nn(probs, next_v[at, :])
        share = 1.0 / both_sums[:, D:]
        shares.append(share)
        mixed.append((both_sums[:, :D] * share).astype(BF))
    mixed_all = jnp.concatenate(mixed, axis=0)
    heads_out = nt(mixed_all, wv_t).reshape(own_seqs, D, D) * diag_heads[None]
    stem_out = jnp.sum(heads_out.reshape(own_seqs, HEADS, LAT, D), axis=1).reshape(rows, D)
    stem_out = stem_out.astype(BF)
    local["wo"].wait()
    gathered["wo"].wait_recv()
    stem_wo = both(wo_v)
    latent_f = latent.astype(F32)
    hidden = jnp.concatenate([latent_f] * own_seqs, axis=0) + nn(stem_out, stem_wo)
    entries_step(1)

    for name in ("norm_attn", "norm_mlp", "b_down", "w_act", "b_act", "targets"):
        local[name].wait()
    for name in ("wqkv", "wout", "wup", "wdn", "bup"):
        local[name].wait()
        gathered[name].wait_recv()
    gain_attn = norm_attn_v[...].astype(F32)
    gain_mlp = norm_mlp_v[...].astype(F32)
    down_bias = b_down_v[...].astype(F32)
    up_bias = jnp.concatenate([bup_v[0], bup_v[1]], axis=1).astype(F32)

    def heads_below(matrix):
        return (matrix[None] * head_mask).reshape(HEADS * rows, D)

    def heads_beside(matrix):
        return jnp.concatenate([matrix * row_mask[head] for head in range(HEADS)], axis=1)

    def lanes_beside(cube):
        return jnp.concatenate([cube[head] for head in range(HEADS)], axis=1)

    def trunk_forward(residual, layer):
        gain_a, gain_m = gain_attn[layer : layer + 1], gain_mlp[layer : layer + 1]
        qkv = jnp.concatenate([both(wqkv_v, layer, part_at) for part_at in range(3)], axis=0)
        out_mat = both(wout_v, layer)
        up_mat = jnp.concatenate([wup_v[0, layer], wup_v[1, layer]], axis=1)
        down_mat = both(wdn_v, layer)
        normed, unit_a, inv_a = norm_rows(residual, gain_a)
        rows_a = normed.astype(BF)
        flat = nt(rows_a, qkv).astype(BF)
        queries = flat[:, :D] * jnp.asarray(HD ** (-0.5), BF)
        keys, values = flat[:, D : 2 * D], flat[:, 2 * D :]
        keys_t = nt(qkv[D : 2 * D], rows_a).astype(BF) * jnp.asarray(HD ** (-0.5), BF)
        values_t = nt(qkv[2 * D :], rows_a).astype(BF)
        scores = nt(heads_below(keys), queries).reshape(HEADS, rows, rows) + block_add[None]
        exped = jnp.exp(scores - jnp.max(scores, axis=1, keepdims=True))
        probs = exped / jnp.sum(exped, axis=1, keepdims=True)
        probs_b = probs.astype(BF)
        out_t = nn(heads_beside(values_t), probs_b.reshape(HEADS * rows, rows))
        attended = out_t.T.astype(BF)
        middle = residual + nn(attended, out_mat)
        normed_m, unit_m, inv_m = norm_rows(middle, gain_m)
        rows_m = normed_m.astype(BF)
        up_rows = nn(rows_m, up_mat) + up_bias[layer : layer + 1]
        cdf = 0.5 + 0.5 * lax.erf(up_rows * (0.5**0.5))
        slope = cdf + up_rows * (jnp.exp(-0.5 * up_rows * up_rows) * 0.3989422804014327)
        hidden_act = (up_rows * cdf).astype(BF)
        output = middle + nn(hidden_act, down_mat) + down_bias[layer : layer + 1]
        saved = dict(
            gain_a=gain_a, gain_m=gain_m, qkv=qkv, out_mat=out_mat, up_mat=up_mat,
            down_mat=down_mat, unit_a=unit_a, inv_a=inv_a, rows_a=rows_a, queries=queries,
            keys_t=keys_t, values=values, probs=probs, probs_b=probs_b, attended=attended,
            unit_m=unit_m, inv_m=inv_m, rows_m=rows_m, slope=slope, hidden_act=hidden_act,
        )
        return output, saved

    kept = []
    for layer in range(LAYERS):
        hidden, saved = trunk_forward(hidden, layer)
        kept.append(saved)
        if layer + 2 < len(radices):
            entries_step(layer + 2)

    entries = jnp.sum(entries_step(len(radices))[0:1], axis=1, keepdims=True)
    total_seqs = own_seqs * lax.axis_size("dp") * lax.axis_size("mp")
    pooled = jnp.sum(hidden.reshape(own_seqs, LAT, D), axis=1)
    act_mat = w_act_v[...]

    def summed3(stacked):
        return stacked[0:own_seqs] + stacked[own_seqs : 2 * own_seqs] + stacked[2 * own_seqs :]

    pred = summed3(nn(split_rows(pooled), act_mat)) + b_act_v[...].astype(F32).reshape(1, AC)
    errors = pred - targets_v[...]
    squares = jnp.sum(valid * errors * errors, axis=0, keepdims=True)
    d_pred = (total_seqs * AC / entries) * (valid * errors)
    head_out[0:own_seqs] = valid * pred
    head_out[own_seqs : own_seqs + 8] = jnp.broadcast_to(entries, (8, AC))
    d_act = lax.dot_general(
        pooled, d_pred, (((0,), (0,)), ((), ())), precision=highest, preferred_element_type=F32
    ).astype(BF)
    d_pooled = summed3(nt(split_rows(d_pred), act_mat))
    upstream = jnp.broadcast_to(d_pooled[:, None, :], (own_seqs, LAT, D)).reshape(rows, D)

    first_row = [sum(CHUNKS[:chunk]) for chunk in range(len(CHUNKS))]
    first_piece = [begin // radices[0] for begin in first_row]
    live = [[] for _ in CHUNKS]

    def put(chunk, offset, mine, others):
        at = pl.ds(first_row[chunk] + offset, mine.shape[0])
        own[at, :] = mine.astype(BF)
        oth[at, :] = others.astype(BF)

    def core_send(chunk):
        at = pl.ds(first_row[chunk], CHUNKS[chunk])
        live[chunk] = [remote(oth.at[at], rcv.at[at], core)]

    def received(chunk):
        for copy in live[chunk]:
            copy.wait_recv()
        live[chunk] = []

    def scatter(chunk):
        received(chunk)
        at = pl.ds(first_row[chunk], CHUNKS[chunk])
        snd[at, :] = (own[at, :].astype(F32) + rcv[at, :].astype(F32)).astype(BF)
        size = CHUNKS[chunk] // radices[0]
        here = pl.ds(first_piece[chunk], size)
        for offset in range(1, radices[0]):
            begin = first_row[chunk] + flip(digits[0], offset) * size
            src = snd.at[pl.ds(pl.multiple_of(begin, 16), size)]
            live[chunk].append(remote(src, rs_r.at[offset - 1, here], partner(0, offset)))

    def share_on(chunk, level):
        received(chunk)
        size = CHUNKS[chunk] // radices[0]
        here = pl.ds(first_piece[chunk], size)
        if level == 1:
            begin = pl.multiple_of(first_row[chunk] + digits[0] * size, 16)
            mine = snd[pl.ds(begin, size), :].astype(F32)
            got = [rs_r[at, here, :].astype(F32) for at in range(radices[0] - 1)]
        else:
            mine = part[level - 2, here, :].astype(F32)
            got = [full_r[level - 2, at, here, :].astype(F32) for at in range(radices[level - 1] - 1)]
        total = tree(mine, got).astype(BF)
        if level < len(radices):
            part[level - 1, here, :] = total
            for offset in range(1, radices[level]):
                dst = full_r.at[level - 1, offset - 1, here]
                live[chunk].append(remote(part.at[level - 1, here], dst, partner(level, offset)))
            return
        mine_at = pl.ds(pl.multiple_of(digits[0] * size, 16), size)
        fins[chunk][mine_at, :] = total
        for offset in range(1, radices[0]):
            piece = fins[chunk].at[mine_at]
            live[chunk].append(remote(piece, piece, partner(0, offset)))

    last = len(radices)

    def back_mlp(upstream, layer, chunk):
        kv = kept[layer]
        grad_top = upstream.astype(BF)
        small_v[16 + 5 + layer : 16 + 6 + layer, :] = jnp.sum(
            grad_top.astype(F32), axis=0, keepdims=True
        )
        d_hidden = nt(grad_top, kv["down_mat"])
        d_upper = (kv["slope"] * d_hidden).astype(BF)
        d_rows = nt(d_upper, kv["up_mat"])
        d_middle = upstream + norm_back(d_rows, kv["unit_m"], kv["inv_m"], kv["gain_m"])
        small_v[16 + 3 + layer : 16 + 4 + layer, :] = jnp.sum(
            d_rows * kv["unit_m"], axis=0, keepdims=True
        )
        d_bias = jnp.sum(d_upper.astype(F32), axis=0, keepdims=True)
        for block in range(4):
            row = 32 + 4 * layer + block
            small_v[row : row + 1, :] = d_bias[:, block * D : (block + 1) * D]
        d_down = tn(kv["hidden_act"], grad_top)
        d_up = tn(kv["rows_m"], d_upper)
        put(chunk, 0, d_up[:, 0:128], d_up[:, 256:384])
        put(chunk, 128, d_up[:, 128:256], d_up[:, 384:512])
        put(chunk, 256, d_down[0:256], d_down[256:512])
        return d_middle

    def back_attn(d_middle, layer, chunk):
        kv = kept[layer]
        grad_attn = d_middle.astype(BF)
        d_mixed = nt(grad_attn, kv["out_mat"]).astype(BF)
        d_probs = nt(heads_below(kv["values"]), d_mixed).reshape(HEADS, rows, rows)
        probs = kv["probs"]
        weighted = probs * d_probs
        inner = jnp.sum(weighted, axis=1, keepdims=True)
        d_scores = (weighted - probs * inner).astype(BF)
        d_q_t = nn(heads_beside(kv["keys_t"]), d_scores.reshape(HEADS * rows, rows))
        d_keys = nn(lanes_beside(d_scores), heads_below(kv["queries"])).astype(BF)
        d_values = nn(lanes_beside(kv["probs_b"]), heads_below(d_mixed)).astype(BF)
        grads = jnp.concatenate([d_q_t.T.astype(BF), d_keys, d_values], axis=1)
        d_rows = nn(grads, kv["qkv"])
        small_v[16 + 1 + layer : 16 + 2 + layer, :] = jnp.sum(
            d_rows * kv["unit_a"], axis=0, keepdims=True
        )
        d_input = d_middle + norm_back(d_rows, kv["unit_a"], kv["inv_a"], kv["gain_a"])
        d_out = tn(kv["attended"], grad_attn)
        d_qkv = tn(grads, kv["rows_a"])
        for place in range(3):
            begin = place * D
            put(chunk, place * 64, d_qkv[begin : begin + 64], d_qkv[begin + 64 : begin + 128])
        put(chunk, 192, d_out[0:64], d_out[64:128])
        return d_input

    put(0, 512, d_act, d_act)
    upstream = back_mlp(upstream, 1, 0)
    core_send(0)
    upstream = back_attn(upstream, 1, 1)
    core_send(1)
    scatter(0)
    upstream = back_mlp(upstream, 0, 2)
    core_send(2)
    scatter(1)
    upstream = back_attn(upstream, 0, 3)
    share_on(0, 1)
    scatter(2)

    grad_stem = upstream.astype(BF)
    d_out_t = nt(stem_wo, grad_stem).astype(BF)
    d_out = nt(grad_stem, stem_wo).astype(BF)
    d_stem_wo = tn(stem_out, grad_stem)
    put(3, 256, d_stem_wo[0:64], d_stem_wo[64:128])
    mixed_heads = jnp.transpose(
        mixed_all.reshape(own_seqs, HEADS, LAT, D), (1, 0, 2, 3)
    ).reshape(HEADS * rows, D)
    d_wv = nn(heads_beside(d_out_t), mixed_heads)
    put(3, 320, d_wv[0:64], d_wv[64:128])
    core_send(3)
    diag_b = diag_heads.astype(BF).reshape(1, HEADS, LAT, D)
    d_diag = (d_out.reshape(own_seqs, 1, LAT, D) * diag_b).reshape(own_seqs, D, D)
    back_v = nn(d_diag.reshape(own_seqs * D, D), wv_t).reshape(own_seqs, D, D)
    d_fold = jnp.zeros((D, D), F32)
    gain_sum = jnp.zeros((D, D), F32)
    folds_v = []
    for seq in range(own_seqs):
        at = pl.ds(seq * SEQ_LEN, SEQ_LEN)
        lanes = slice(seq * SEQ_LEN, (seq + 1) * SEQ_LEN)
        gain_sum += back_v[seq] * mixed[seq].astype(F32)
        scaled_v = back_v[seq] * shares[seq]
        scaled_b = scaled_v.astype(BF)
        folds_v.append(scaled_b)
        d_probs = nt(scaled_b, next_v[at, 0:D])
        probs = e_v[:, lanes].astype(F32)
        weighted = probs * d_probs
        inner = jnp.sum(weighted, axis=1, keepdims=True) * shares[seq][:, 0:1]
        d_scores = (weighted - probs * inner).astype(BF)
        ds_v[:, lanes] = d_scores
        d_fold += nn(d_scores, next_v[at, 0:D])

    d_fold_b = d_fold.astype(BF)
    d_wk = nn(q_diag.astype(F32).T.astype(BF), d_fold_b)
    d_q = nt(d_fold_b, wk_t) * diag_heads
    d_q = jnp.sum(d_q.reshape(HEADS, LAT, D), axis=0) * HD ** (-0.5)
    d_latent = jnp.sum(upstream.reshape(own_seqs, LAT, D), axis=0) + nn(d_q.astype(BF), wq_t)
    small_v[0:16, :] = d_latent
    gain_rows = jnp.sum(gain_sum + d_fold * fold, axis=0, keepdims=True)
    small_v[16:17, :] = gain_rows / stem_gain
    small_v[23:24, :] = jnp.sum(d_pred, axis=0, keepdims=True)
    square_top = squares.astype(BF).astype(F32)
    small_v[24:25, :] = square_top
    small_v[25:26, :] = squares - square_top
    tail_s[0, 0:64, :] = d_wk[0:64].astype(BF)
    tail_s[0, 64:80, :] = d_q.astype(BF)
    tail_s[1, 0:64, :] = d_wk[64:128].astype(BF)
    tail_s[1, 64:80, :] = jnp.concatenate([d_q[:, 64:], d_q[:, :64]], axis=1).astype(BF)
    for place, begin in ((0, 0), (1, 2)):
        for layer in range(LAYERS):
            row = 26 + 2 * layer
            src = 32 + 4 * layer + begin
            small_v[row : row + 2, :] = small_v[src : src + 2, :]
        small_v[30:32, :] = jnp.zeros((2, D), F32)
        tail_s[place, 80:112, :] = small_v[0:32, :].astype(BF)
    tail_live = [remote(tail_s.at[1], tail_r.at[0], core)]

    def tail_step(level):
        for copy in tail_live:
            copy.wait_recv()
        tail_live.clear()
        first = 1 + sum(radices[: level - 1]) - (level - 1)
        count = 1 if level == 0 else radices[level - 1] - 1
        begin = 0 if level == 0 else first
        mine = tail_s[0 if level == 0 else level + 1].astype(F32)
        total = tree(mine, [tail_r[begin + at].astype(F32) for at in range(count)])
        if level == last:
            return total
        tail_s[level + 2] = total.astype(BF)
        nxt = 1 + sum(radices[:level]) - level
        for offset in range(1, radices[level]):
            dst = tail_r.at[nxt + offset - 1]
            tail_live.append(remote(tail_s.at[level + 2], dst, partner(level, offset)))
        return None

    fold_g = (fold * stem_gain).astype(BF)
    fold_side = jnp.concatenate([fold_g, nn(fold_g, mean_mat).astype(BF)], axis=1)

    def token_grads(seq):
        at = pl.ds(seq * SEQ_LEN, SEQ_LEN)
        lanes = slice(seq * SEQ_LEN, (seq + 1) * SEQ_LEN)
        left = jnp.concatenate([ds_v[:, lanes], e_v[:, lanes]], axis=0)
        value_g = (folds_v[seq].astype(F32) * stem_gain).astype(BF)
        value_side = jnp.concatenate([value_g, nn(value_g, mean_mat).astype(BF)], axis=1)
        both_grads = tn(left, jnp.concatenate([fold_side, value_side], axis=0))
        scaled = both_grads[:, :D]
        unit = unit_v[at, :]
        slope_mean = nn((scaled * unit).astype(BF), mean_mat)
        grad_tokens[at, :] = inv_v[at, :] * (scaled - both_grads[:, D:] - unit * slope_mean)

    steps = [
        lambda: share_on(1, 1),
        lambda: scatter(3),
        lambda: tail_step(0),
        lambda: share_on(2, 1),
        lambda: share_on(0, 2),
        lambda: share_on(3, 1),
        lambda: tail_step(1),
        lambda: share_on(1, 2),
    ]
    for seq in range(own_seqs):
        token_grads(seq)
        if seq < len(steps):
            steps[seq]()
    for step in steps[own_seqs:]:
        step()
    share_on(2, 2)
    share_on(3, 2)
    for level in range(3, last + 1):
        for chunk in range(len(CHUNKS)):
            share_on(chunk, level)
    for level in range(2, last):
        tail_step(level)
    total = tail_step(last)
    tail_out[...] = total
    wq_out[...] = tn(total[64:80, 0:64].astype(BF), latent)
    for chunk in range(len(CHUNKS)):
        received(chunk)
    for copy in sends:
        copy.wait_send()


def split_kernel(
    grad_tokens,
    fin_a,
    fin_b,
    fin_c,
    fin_d,
    tail,
    wq_in,
    head,
    actions,
    masked_loss,
    d_tokens,
    d_stem_norm,
    d_latent,
    d_stem_wq,
    d_stem_wkv,
    d_stem_wo,
    d_norm_attn,
    d_qkv,
    d_out,
    d_norm_mlp,
    d_up,
    d_b_up,
    d_down,
    d_b_down,
    d_act,
    d_b_act,
    sem,
):
    copy = pltpu.make_async_copy(grad_tokens, d_tokens, sem)
    copy.start()
    own_seqs = actions.shape[0]
    for layer, mlp, attn in ((1, fin_a, fin_b), (0, fin_c, fin_d)):
        d_up[layer, :, 0:128] = mlp[0:128, :].astype(F32)
        d_up[layer, :, 128:256] = mlp[128:256, :].astype(F32)
        d_down[layer] = mlp[256:512, :].astype(F32)
        for place in range(3):
            d_qkv[layer, place] = attn[64 * place : 64 * place + 64, :].astype(F32)
        d_out[layer] = attn[192:256, :].astype(F32)
        d_b_up[layer : layer + 1, 0:128] = tail[106 + 2 * layer : 107 + 2 * layer, :]
        d_b_up[layer : layer + 1, 128:256] = tail[107 + 2 * layer : 108 + 2 * layer, :]
    d_act[...] = fin_a[512:640, :].astype(F32)
    d_stem_wo[...] = fin_d[256:320, :].astype(F32)
    d_stem_wkv[1] = fin_d[320:384, :].astype(F32)
    d_stem_wkv[0] = tail[0:64, :]
    d_stem_wq[...] = wq_in[...]
    d_latent[...] = tail[80:96, :]
    d_stem_norm[...] = tail[96:97, :].reshape(D)
    d_norm_attn[...] = tail[97:99, :]
    d_norm_mlp[...] = tail[99:101, :]
    d_b_down[...] = tail[101:103, :]
    d_b_act[...] = tail[103:104, :].reshape(D)
    actions[...] = head[0:own_seqs, :]
    squares = jnp.sum(tail[104:105, :] + tail[105:106, :], axis=1, keepdims=True)
    loss = squares / head[own_seqs : own_seqs + 1, :]
    masked_loss[...] = loss.reshape(D)
    copy.wait()


def on_device(radices, *args):
    (
        tokens,
        stem_norm,
        stem_latent,
        stem_wq,
        stem_wkv,
        stem_wo,
        norm_attn,
        w_qkv,
        w_out,
        norm_mlp,
        w_up,
        b_up,
        w_down,
        b_down,
        w_act,
        b_act,
        span_len,
        joint_mask,
        targets,
    ) = args
    own_seqs = targets.shape[0]
    count = own_seqs * SEQ_LEN
    rows = own_seqs * LAT
    last = len(radices)
    spread = sum(radices) - last
    vmem = pl.BlockSpec(memory_space=pltpu.VMEM)
    hbm = pl.BlockSpec(memory_space=pltpu.HBM)
    total_rows = sum(CHUNKS)
    pieces = total_rows // radices[0]
    wide = max(radices) - 1
    n_remote = 8 + 1 + spread + len(CHUNKS) * (1 + spread + radices[0] - 1) + 1 + spread
    shape = jax.ShapeDtypeStruct
    main = pl.pallas_call(
        functools.partial(main_kernel, radices),
        out_shape=[
            shape((count, D), F32),
            *[shape((size, D), BF) for size in CHUNKS],
            shape((TAIL, D), F32),
            shape((64, D), F32),
            shape((own_seqs + 8, AC), F32),
        ],
        in_specs=[hbm] * len(args),
        out_specs=[vmem] * 8,
        scratch_shapes=[
            pltpu.VMEM((count, D), BF),
            pltpu.VMEM((D,), BF),
            pltpu.VMEM((LAT, D), BF),
            pltpu.VMEM((2, 64, D), BF),
            pltpu.VMEM((2, 2, 64, D), BF),
            pltpu.VMEM((2, 64, D), BF),
            pltpu.VMEM((LAYERS, D), BF),
            pltpu.VMEM((2, LAYERS, 3, 64, D), BF),
            pltpu.VMEM((2, LAYERS, 64, D), BF),
            pltpu.VMEM((LAYERS, D), BF),
            pltpu.VMEM((2, LAYERS, D, FF // 2), BF),
            pltpu.VMEM((2, LAYERS, FF // 2), BF),
            pltpu.VMEM((2, LAYERS, FF // 2, D), BF),
            pltpu.VMEM((LAYERS, D), BF),
            pltpu.VMEM((D, AC), BF),
            pltpu.VMEM((AC,), BF),
            pltpu.SMEM((own_seqs,), jnp.int32),
            pltpu.VMEM((own_seqs, JOINTS), jnp.int32),
            pltpu.VMEM((own_seqs, AC), F32),
            pltpu.VMEM((count, 2 * D), BF),
            pltpu.VMEM((count, D), F32),
            pltpu.VMEM((count, D), F32),
            pltpu.VMEM((D, count), BF),
            pltpu.VMEM((D, count), BF),
            pltpu.VMEM((40, D), F32),
            pltpu.VMEM((1 + last, 8, AC), F32),
            pltpu.VMEM((1 + spread, 8, AC), F32),
            pltpu.VMEM((total_rows, D), BF),
            pltpu.VMEM((total_rows, D), BF),
            pltpu.VMEM((total_rows, D), BF),
            pltpu.VMEM((total_rows, D), BF),
            pltpu.VMEM((wide, pieces, D), BF),
            pltpu.VMEM((last - 1, pieces, D), BF),
            pltpu.VMEM((last - 1, wide, pieces, D), BF),
            pltpu.VMEM((2 + last, TAIL, D), BF),
            pltpu.VMEM((1 + spread, TAIL, D), BF),
            pltpu.SemaphoreType.DMA((len(args),)),
            pltpu.SemaphoreType.DMA((n_remote,)),
            pltpu.SemaphoreType.DMA((n_remote,)),
        ],
        compiler_params=pltpu.CompilerParams(
            collective_id=0, has_side_effects=True, vmem_limit_bytes=40 * 2**20
        ),
        name="stem_trunk_head",
    )(
        tokens,
        stem_norm,
        stem_latent,
        jnp.transpose(stem_wq),
        jnp.transpose(stem_wkv, (0, 2, 1)),
        stem_wo,
        norm_attn,
        jnp.transpose(w_qkv, (0, 1, 3, 2)),
        w_out,
        norm_mlp,
        w_up,
        b_up,
        w_down,
        b_down,
        w_act,
        b_act,
        span_len,
        joint_mask,
        targets,
    )
    outs = [
        shape((own_seqs, AC), F32),
        shape((D,), F32),
        shape((count, D), F32),
        shape((D,), F32),
        shape((LAT, D), F32),
        shape((64, D), F32),
        shape((2, 64, D), F32),
        shape((64, D), F32),
        shape((LAYERS, D), F32),
        shape((LAYERS, 3, 64, D), F32),
        shape((LAYERS, 64, D), F32),
        shape((LAYERS, D), F32),
        shape((LAYERS, D, FF // 2), F32),
        shape((LAYERS, FF // 2), F32),
        shape((LAYERS, FF // 2, D), F32),
        shape((LAYERS, D), F32),
        shape((D, AC), F32),
        shape((AC,), F32),
    ]
    out_specs = [vmem] * len(outs)
    out_specs[2] = pl.BlockSpec(memory_space=pl.ANY)
    result = pl.pallas_call(
        split_kernel,
        out_shape=outs,
        in_specs=[pl.BlockSpec(memory_space=pl.ANY)] + [vmem] * 7,
        out_specs=out_specs,
        scratch_shapes=[pltpu.SemaphoreType.DMA],
        compiler_params=pltpu.CompilerParams(vmem_limit_bytes=20 * 2**20),
        name="split_results",
    )(*main)
    result = list(result)
    result[1] = result[1][0]
    result[5] = jnp.transpose(result[5])
    result[6] = jnp.transpose(result[6], (0, 2, 1))
    result[9] = jnp.transpose(result[9], (0, 1, 3, 2))
    return tuple(result)


def solution(mesh):
    radices = radices_of(mesh.shape["dp"])
    in_specs = (
        P(("dp", "mp"), None),
        P(),
        P(),
        P(None, "mp"),
        P(None, None, "mp"),
        P("mp", None),
        P(),
        P(None, None, None, "mp"),
        P(None, "mp", None),
        P(),
        P(None, None, "mp"),
        P(None, "mp"),
        P(None, "mp", None),
        P(),
        P(),
        P(),
        P(("dp", "mp")),
        P(("dp", "mp"), None),
        P(("dp", "mp"), None),
    )
    out_specs = (
        P(("dp", "mp"), None),
        P(),
        P(("dp", "mp"), None),
        P(),
        P(),
        P(None, "mp"),
        P(None, None, "mp"),
        P("mp", None),
        P(),
        P(None, None, None, "mp"),
        P(None, "mp", None),
        P(),
        P(None, None, "mp"),
        P(None, "mp"),
        P(None, "mp", None),
        P(),
        P(),
        P(),
    )
    return jax.shard_map(
        functools.partial(on_device, radices),
        mesh=mesh,
        in_specs=in_specs,
        out_specs=out_specs,
        check_vma=False,
    )
```

```python
import functools

import jax
import jax.numpy as jnp
from jax import lax
from jax.experimental import pallas as pl
from jax.experimental.pallas import tpu as pltpu
from jax.sharding import PartitionSpec as P

HD = 16
LAT = 16
SEQ_LEN = 256
SPAN = 16
JOINTS = 8
HEADS = 8
D = 128
FF = 512
AC = 128
LAYERS = 2

F32 = jnp.float32
BF = jnp.bfloat16
MESH = pl.DeviceIdType.MESH
epsilon = 1e-05
highest = lax.Precision.HIGHEST

CHUNKS = (640, 256, 512, 384)
TAIL = 112


def nn(left, right):
    return jnp.dot(left, right, preferred_element_type=F32)


def nt(left, right):
    return lax.dot_general(left, right, (((1,), (1,)), ((), ())), preferred_element_type=F32)


def tn(left, right):
    return lax.dot_general(left, right, (((0,), (0,)), ((), ())), preferred_element_type=F32)


def iota(shape, axis):
    return lax.broadcasted_iota(jnp.int32, shape, axis)


def radices_of(count):
    found = []
    while count > 1:
        radix = 4 if count % 4 == 0 else 2
        found.append(radix)
        count //= radix
    return found


def flip(digit, offset):
    if offset == 1:
        return digit + 1 - 2 * (digit % 2)
    if offset == 2:
        return (digit + 2) % 4
    return 3 - digit


def norm_rows(values_in, gain_vec):
    mean_rows = jnp.mean(values_in, axis=-1, keepdims=True)
    centred = values_in - mean_rows
    variance = jnp.mean(centred * centred, axis=-1, keepdims=True)
    inv_rows = lax.rsqrt(variance + epsilon)
    unit_rows = centred * inv_rows
    return unit_rows * gain_vec, unit_rows, inv_rows


def norm_back(upstream, unit_rows, inv_rows, gain_vec):
    scaled = upstream * gain_vec
    inner = (
        scaled
        - jnp.mean(scaled, axis=-1, keepdims=True)
        - unit_rows * jnp.mean(scaled * unit_rows, axis=-1, keepdims=True)
    )
    return inv_rows * inner


def split_rows(values_in):
    first = values_in.astype(BF).astype(F32)
    rest = values_in - first
    second = rest.astype(BF).astype(F32)
    return jnp.concatenate([first, second, rest - second], axis=0).astype(BF)


def main_kernel(
    radices,
    tokens_h,
    stem_norm_h,
    stem_latent_h,
    stem_wq_h,
    stem_wkv_h,
    stem_wo_h,
    norm_attn_h,
    w_qkv_h,
    w_out_h,
    norm_mlp_h,
    w_up_h,
    b_up_h,
    w_down_h,
    b_down_h,
    w_act_h,
    b_act_h,
    span_len_h,
    joint_mask_h,
    targets_h,
    grad_tokens,
    fin_a,
    fin_b,
    fin_c,
    fin_d,
    tail_out,
    wq_out,
    head_out,
    x_v,
    stem_norm_v,
    stem_latent_v,
    wq_v,
    wkv_v,
    wo_v,
    norm_attn_v,
    wqkv_v,
    wout_v,
    norm_mlp_v,
    wup_v,
    bup_v,
    wdn_v,
    b_down_v,
    w_act_v,
    b_act_v,
    span_s,
    joint_v,
    targets_v,
    next_v,
    unit_v,
    inv_v,
    e_v,
    ds_v,
    small_v,
    ent_v,
    ent_r,
    own,
    oth,
    rcv,
    snd,
    rs_r,
    part,
    full_r,
    tail_s,
    tail_r,
    in_sem,
    send_sem,
    recv_sem,
):
    dp, mp = lax.axis_index("dp"), lax.axis_index("mp")
    own_seqs = targets_h.shape[0]
    rows = own_seqs * LAT
    fins = (fin_a, fin_b, fin_c, fin_d)
    core = (dp, 1 - mp)
    strides, digits = [], []
    stride = 1
    for radix in radices:
        strides.append(stride)
        digits.append((dp // stride) % radix)
        stride *= radix

    def partner(level, offset):
        digit = digits[level]
        return (dp + (flip(digit, offset) - digit) * strides[level], mp)

    barrier = pltpu.get_barrier_semaphore()
    greeted = [core]
    for level, radix in enumerate(radices):
        greeted += [partner(level, offset) for offset in range(1, radix)]
    for device in greeted:
        pl.semaphore_signal(barrier, inc=1, device_id=device, device_id_type=MESH)

    slots = [0]
    sends = []

    def remote(src, dst, device):
        slot = slots[0]
        slots[0] += 1
        copy = pltpu.make_async_remote_copy(
            src_ref=src,
            dst_ref=dst,
            send_sem=send_sem.at[slot],
            recv_sem=recv_sem.at[slot],
            device_id=device,
            device_id_type=MESH,
        )
        copy.start()
        sends.append(copy)
        return copy

    local = {}
    pairs = (
        ("tokens", tokens_h, x_v),
        ("stem_norm", stem_norm_h, stem_norm_v),
        ("stem_latent", stem_latent_h, stem_latent_v),
        ("wq", stem_wq_h, wq_v.at[0]),
        ("wkv", stem_wkv_h, wkv_v.at[0]),
        ("wo", stem_wo_h, wo_v.at[0]),
        ("wqkv", w_qkv_h, wqkv_v.at[0]),
        ("wout", w_out_h, wout_v.at[0]),
        ("wup", w_up_h, wup_v.at[0]),
        ("wdn", w_down_h, wdn_v.at[0]),
        ("norm_attn", norm_attn_h, norm_attn_v),
        ("norm_mlp", norm_mlp_h, norm_mlp_v),
        ("bup", b_up_h, bup_v.at[0]),
        ("b_down", b_down_h, b_down_v),
        ("w_act", w_act_h, w_act_v),
        ("b_act", b_act_h, b_act_v),
        ("span", span_len_h, span_s),
        ("joint", joint_mask_h, joint_v),
        ("targets", targets_h, targets_v),
    )
    for place, (name, src, dst) in enumerate(pairs):
        local[name] = pltpu.make_async_copy(src, dst, in_sem.at[place])
        local[name].start()

    head_mask = (
        (iota((HEADS, D, D), 2) // HD == iota((HEADS, D, D), 0)).astype(F32).astype(BF)
    )
    row_mask = (iota((HEADS, D, D), 1) // HD == iota((HEADS, D, D), 0)).astype(F32).astype(BF)
    diag_heads = (iota((D, D), 0) // LAT == iota((D, D), 1) // HD).astype(F32)
    block_add = jnp.where(iota((rows, rows), 0) // LAT == iota((rows, rows), 1) // LAT, 0.0, -1e30)
    mean_mat = jnp.full((D, D), 1.0 / D, BF)
    mean_twice = jnp.full((2 * D, D), 1.0 / D, BF)

    pl.semaphore_wait(barrier, len(greeted))
    gathered = {}
    for name, src, dst in (
        ("wq", stem_wq_h, wq_v.at[1]),
        ("wkv", stem_wkv_h, wkv_v.at[1]),
        ("wo", stem_wo_h, wo_v.at[1]),
        ("wqkv", w_qkv_h, wqkv_v.at[1]),
        ("wout", w_out_h, wout_v.at[1]),
        ("wup", w_up_h, wup_v.at[1]),
        ("wdn", w_down_h, wdn_v.at[1]),
        ("bup", b_up_h, bup_v.at[1]),
    ):
        gathered[name] = remote(src, dst, core)

    local["span"].wait()
    local["joint"].wait()
    spans = jnp.zeros((own_seqs, AC), jnp.int32)
    for seq in range(own_seqs):
        spans = jnp.where(iota((own_seqs, AC), 0) == seq, span_s[seq], spans)
    joints = (joint_v[...] > 0).astype(F32).astype(BF)
    spread = (iota((JOINTS, AC), 1) % JOINTS == iota((JOINTS, AC), 0)).astype(F32).astype(BF)
    valid = jnp.where(iota((own_seqs, AC), 1) // JOINTS < spans, nn(joints, spread), 0.0)
    ent_v[0] = jnp.broadcast_to(jnp.sum(valid, axis=0, keepdims=True), (8, AC))
    pending = [remote(ent_v.at[0], ent_r.at[0], core)]

    def entries_step(level):
        for copy in pending:
            copy.wait_recv()
        if level == 0:
            total = ent_v[0] + ent_r[0]
        else:
            total = tree(ent_v[level], [ent_r[at] for at in ent_slots[-1]])
        if level == len(radices):
            return total
        ent_v[level + 1] = total
        pending.clear()
        places = []
        for offset in range(1, radices[level]):
            place = 1 + sum(radices[:level]) - level + offset - 1
            places.append(place)
            pending.append(remote(ent_v.at[level + 1], ent_r.at[place], partner(level, offset)))
        ent_slots.append(places)
        return None

    ent_slots = []

    def tree(mine, others):
        if len(others) == 1:
            return mine + others[0]
        return (mine + others[0]) + (others[1] + others[2])

    local["tokens"].wait()
    local["stem_norm"].wait()
    stem_gain = stem_norm_v[...].astype(F32).reshape(1, D)
    half = own_seqs * SEQ_LEN // 2
    for start in (0, half):
        at = pl.ds(start, half)
        raw = x_v[at, :]
        centred = raw.astype(F32) - nn(raw, mean_mat)
        square = centred * centred
        upper = square.astype(BF)
        lower = (square - upper.astype(F32)).astype(BF)
        inv = lax.rsqrt(nn(jnp.concatenate([upper, lower], axis=1), mean_twice) + epsilon)
        unit = centred * inv
        inv_v[at, :] = inv
        unit_v[at, :] = unit
        next_v[at, 0:D] = (unit * stem_gain).astype(BF)
        next_v[at, D : 2 * D] = jnp.ones((half, D), BF)

    def both(ref, *index):
        return jnp.concatenate([ref[(0,) + index], ref[(1,) + index]], axis=0)

    entries_step(0)
    local["stem_latent"].wait()
    for name in ("wq", "wkv"):
        local[name].wait()
        gathered[name].wait_recv()
    latent = stem_latent_v[...]
    wq_t = both(wq_v)
    wk_t, wv_t = both(wkv_v, 0), both(wkv_v, 1)
    stem_q = (nt(latent, wq_t).astype(BF).astype(F32) * HD ** (-0.5)).astype(BF)
    q_diag = (jnp.concatenate([stem_q] * HEADS, axis=0).astype(F32) * diag_heads).astype(BF)
    fold = nn(q_diag, wk_t)
    fold_b = fold.astype(BF)
    mixed, shares, tops = [], [], []
    for seq in range(own_seqs):
        at = pl.ds(seq * SEQ_LEN, SEQ_LEN)
        scores = nt(fold_b, next_v[at, 0:D])
        probs = jnp.exp(scores - jnp.max(scores, axis=1, keepdims=True)).astype(BF)
        e_v[:, seq * SEQ_LEN : (seq + 1) * SEQ_LEN] = probs
        both_sums = nn(probs, next_v[at, :])
        share = 1.0 / both_sums[:, D:]
        shares.append(share)
        mixed.append((both_sums[:, :D] * share).astype(BF))
    mixed_all = jnp.concatenate(mixed, axis=0)
    heads_out = nt(mixed_all, wv_t).reshape(own_seqs, D, D) * diag_heads[None]
    stem_out = jnp.sum(heads_out.reshape(own_seqs, HEADS, LAT, D), axis=1).reshape(rows, D)
    stem_out = stem_out.astype(BF)
    local["wo"].wait()
    gathered["wo"].wait_recv()
    stem_wo = both(wo_v)
    latent_f = latent.astype(F32)
    hidden = jnp.concatenate([latent_f] * own_seqs, axis=0) + nn(stem_out, stem_wo)
    entries_step(1)

    for name in ("norm_attn", "norm_mlp", "b_down", "w_act", "b_act", "targets"):
        local[name].wait()
    for name in ("wqkv", "wout", "wup", "wdn", "bup"):
        local[name].wait()
        gathered[name].wait_recv()
    gain_attn = norm_attn_v[...].astype(F32)
    gain_mlp = norm_mlp_v[...].astype(F32)
    down_bias = b_down_v[...].astype(F32)
    up_bias = jnp.concatenate([bup_v[0], bup_v[1]], axis=1).astype(F32)

    def heads_below(matrix):
        return (matrix[None] * head_mask).reshape(HEADS * rows, D)

    def heads_beside(matrix):
        return jnp.concatenate([matrix * row_mask[head] for head in range(HEADS)], axis=1)

    def lanes_beside(cube):
        return jnp.concatenate([cube[head] for head in range(HEADS)], axis=1)

    def trunk_forward(residual, layer):
        gain_a, gain_m = gain_attn[layer : layer + 1], gain_mlp[layer : layer + 1]
        qkv = jnp.concatenate([both(wqkv_v, layer, part_at) for part_at in range(3)], axis=0)
        out_mat = both(wout_v, layer)
        up_mat = jnp.concatenate([wup_v[0, layer], wup_v[1, layer]], axis=1)
        down_mat = both(wdn_v, layer)
        normed, unit_a, inv_a = norm_rows(residual, gain_a)
        rows_a = normed.astype(BF)
        flat = nt(rows_a, qkv).astype(BF)
        queries = flat[:, :D] * jnp.asarray(HD ** (-0.5), BF)
        keys, values = flat[:, D : 2 * D], flat[:, 2 * D :]
        keys_t = nt(qkv[D : 2 * D], rows_a).astype(BF) * jnp.asarray(HD ** (-0.5), BF)
        values_t = nt(qkv[2 * D :], rows_a).astype(BF)
        scores = nt(heads_below(keys), queries).reshape(HEADS, rows, rows) + block_add[None]
        exped = jnp.exp(scores - jnp.max(scores, axis=1, keepdims=True))
        probs = exped / jnp.sum(exped, axis=1, keepdims=True)
        probs_b = probs.astype(BF)
        out_t = nn(heads_beside(values_t), probs_b.reshape(HEADS * rows, rows))
        attended = out_t.T.astype(BF)
        middle = residual + nn(attended, out_mat)
        normed_m, unit_m, inv_m = norm_rows(middle, gain_m)
        rows_m = normed_m.astype(BF)
        up_rows = nn(rows_m, up_mat) + up_bias[layer : layer + 1]
        cdf = 0.5 + 0.5 * lax.erf(up_rows * (0.5**0.5))
        slope = cdf + up_rows * (jnp.exp(-0.5 * up_rows * up_rows) * 0.3989422804014327)
        hidden_act = (up_rows * cdf).astype(BF)
        output = middle + nn(hidden_act, down_mat) + down_bias[layer : layer + 1]
        saved = dict(
            gain_a=gain_a, gain_m=gain_m, qkv=qkv, out_mat=out_mat, up_mat=up_mat,
            down_mat=down_mat, unit_a=unit_a, inv_a=inv_a, rows_a=rows_a, queries=queries,
            keys_t=keys_t, values=values, probs=probs, probs_b=probs_b, attended=attended,
            unit_m=unit_m, inv_m=inv_m, rows_m=rows_m, slope=slope, hidden_act=hidden_act,
        )
        return output, saved

    kept = []
    for layer in range(LAYERS):
        hidden, saved = trunk_forward(hidden, layer)
        kept.append(saved)
        if layer + 2 < len(radices):
            entries_step(layer + 2)

    entries = jnp.sum(entries_step(len(radices))[0:1], axis=1, keepdims=True)
    total_seqs = own_seqs * lax.axis_size("dp") * lax.axis_size("mp")
    pooled = jnp.sum(hidden.reshape(own_seqs, LAT, D), axis=1)
    act_mat = w_act_v[...]

    def summed3(stacked):
        return stacked[0:own_seqs] + stacked[own_seqs : 2 * own_seqs] + stacked[2 * own_seqs :]

    pred = summed3(nn(split_rows(pooled), act_mat)) + b_act_v[...].astype(F32).reshape(1, AC)
    errors = pred - targets_v[...]
    squares = jnp.sum(valid * errors * errors, axis=0, keepdims=True)
    d_pred = (total_seqs * AC / entries) * (valid * errors)
    head_out[0:own_seqs] = valid * pred
    head_out[own_seqs : own_seqs + 8] = jnp.broadcast_to(entries, (8, AC))
    d_act = lax.dot_general(
        pooled, d_pred, (((0,), (0,)), ((), ())), precision=highest, preferred_element_type=F32
    ).astype(BF)
    d_pooled = summed3(nt(split_rows(d_pred), act_mat))
    upstream = jnp.broadcast_to(d_pooled[:, None, :], (own_seqs, LAT, D)).reshape(rows, D)

    first_row = [sum(CHUNKS[:chunk]) for chunk in range(len(CHUNKS))]
    first_piece = [begin // radices[0] for begin in first_row]
    live = [[] for _ in CHUNKS]

    def put(chunk, offset, mine, others):
        at = pl.ds(first_row[chunk] + offset, mine.shape[0])
        own[at, :] = mine.astype(BF)
        oth[at, :] = others.astype(BF)

    def core_send(chunk):
        at = pl.ds(first_row[chunk], CHUNKS[chunk])
        live[chunk] = [remote(oth.at[at], rcv.at[at], core)]

    def received(chunk):
        for copy in live[chunk]:
            copy.wait_recv()
        live[chunk] = []

    def scatter(chunk):
        received(chunk)
        at = pl.ds(first_row[chunk], CHUNKS[chunk])
        snd[at, :] = (own[at, :].astype(F32) + rcv[at, :].astype(F32)).astype(BF)
        size = CHUNKS[chunk] // radices[0]
        here = pl.ds(first_piece[chunk], size)
        for offset in range(1, radices[0]):
            begin = first_row[chunk] + flip(digits[0], offset) * size
            src = snd.at[pl.ds(pl.multiple_of(begin, 16), size)]
            live[chunk].append(remote(src, rs_r.at[offset - 1, here], partner(0, offset)))

    def share_on(chunk, level):
        received(chunk)
        size = CHUNKS[chunk] // radices[0]
        here = pl.ds(first_piece[chunk], size)
        if level == 1:
            begin = pl.multiple_of(first_row[chunk] + digits[0] * size, 16)
            mine = snd[pl.ds(begin, size), :].astype(F32)
            got = [rs_r[at, here, :].astype(F32) for at in range(radices[0] - 1)]
        else:
            mine = part[level - 2, here, :].astype(F32)
            got = [full_r[level - 2, at, here, :].astype(F32) for at in range(radices[level - 1] - 1)]
        total = tree(mine, got).astype(BF)
        if level < len(radices):
            part[level - 1, here, :] = total
            for offset in range(1, radices[level]):
                dst = full_r.at[level - 1, offset - 1, here]
                live[chunk].append(remote(part.at[level - 1, here], dst, partner(level, offset)))
            return
        mine_at = pl.ds(pl.multiple_of(digits[0] * size, 16), size)
        fins[chunk][mine_at, :] = total
        for offset in range(1, radices[0]):
            piece = fins[chunk].at[mine_at]
            live[chunk].append(remote(piece, piece, partner(0, offset)))

    last = len(radices)

    def back_mlp(upstream, layer, chunk):
        kv = kept[layer]
        grad_top = upstream.astype(BF)
        small_v[16 + 5 + layer : 16 + 6 + layer, :] = jnp.sum(
            grad_top.astype(F32), axis=0, keepdims=True
        )
        d_hidden = nt(grad_top, kv["down_mat"])
        d_upper = (kv["slope"] * d_hidden).astype(BF)
        d_rows = nt(d_upper, kv["up_mat"])
        d_middle = upstream + norm_back(d_rows, kv["unit_m"], kv["inv_m"], kv["gain_m"])
        small_v[16 + 3 + layer : 16 + 4 + layer, :] = jnp.sum(
            d_rows * kv["unit_m"], axis=0, keepdims=True
        )
        d_bias = jnp.sum(d_upper.astype(F32), axis=0, keepdims=True)
        for block in range(4):
            row = 32 + 4 * layer + block
            small_v[row : row + 1, :] = d_bias[:, block * D : (block + 1) * D]
        d_down = tn(kv["hidden_act"], grad_top)
        d_up = tn(kv["rows_m"], d_upper)
        put(chunk, 0, d_up[:, 0:128], d_up[:, 256:384])
        put(chunk, 128, d_up[:, 128:256], d_up[:, 384:512])
        put(chunk, 256, d_down[0:256], d_down[256:512])
        return d_middle

    def back_attn(d_middle, layer, chunk):
        kv = kept[layer]
        grad_attn = d_middle.astype(BF)
        d_mixed = nt(grad_attn, kv["out_mat"]).astype(BF)
        d_probs = nt(heads_below(kv["values"]), d_mixed).reshape(HEADS, rows, rows)
        probs = kv["probs"]
        weighted = probs * d_probs
        inner = jnp.sum(weighted, axis=1, keepdims=True)
        d_scores = (weighted - probs * inner).astype(BF)
        d_q_t = nn(heads_beside(kv["keys_t"]), d_scores.reshape(HEADS * rows, rows))
        d_keys = nn(lanes_beside(d_scores), heads_below(kv["queries"])).astype(BF)
        d_values = nn(lanes_beside(kv["probs_b"]), heads_below(d_mixed)).astype(BF)
        grads = jnp.concatenate([d_q_t.T.astype(BF), d_keys, d_values], axis=1)
        d_rows = nn(grads, kv["qkv"])
        small_v[16 + 1 + layer : 16 + 2 + layer, :] = jnp.sum(
            d_rows * kv["unit_a"], axis=0, keepdims=True
        )
        d_input = d_middle + norm_back(d_rows, kv["unit_a"], kv["inv_a"], kv["gain_a"])
        d_out = tn(kv["attended"], grad_attn)
        d_qkv = tn(grads, kv["rows_a"])
        for place in range(3):
            begin = place * D
            put(chunk, place * 64, d_qkv[begin : begin + 64], d_qkv[begin + 64 : begin + 128])
        put(chunk, 192, d_out[0:64], d_out[64:128])
        return d_input

    put(0, 512, d_act, d_act)
    upstream = back_mlp(upstream, 1, 0)
    core_send(0)
    upstream = back_attn(upstream, 1, 1)
    core_send(1)
    scatter(0)
    upstream = back_mlp(upstream, 0, 2)
    core_send(2)
    scatter(1)
    upstream = back_attn(upstream, 0, 3)
    share_on(0, 1)
    scatter(2)

    grad_stem = upstream.astype(BF)
    d_out_t = nt(stem_wo, grad_stem).astype(BF)
    d_out = nt(grad_stem, stem_wo).astype(BF)
    d_stem_wo = tn(stem_out, grad_stem)
    put(3, 256, d_stem_wo[0:64], d_stem_wo[64:128])
    mixed_heads = jnp.transpose(
        mixed_all.reshape(own_seqs, HEADS, LAT, D), (1, 0, 2, 3)
    ).reshape(HEADS * rows, D)
    d_wv = nn(heads_beside(d_out_t), mixed_heads)
    put(3, 320, d_wv[0:64], d_wv[64:128])
    core_send(3)
    diag_b = diag_heads.astype(BF).reshape(1, HEADS, LAT, D)
    d_diag = (d_out.reshape(own_seqs, 1, LAT, D) * diag_b).reshape(own_seqs, D, D)
    back_v = nn(d_diag.reshape(own_seqs * D, D), wv_t).reshape(own_seqs, D, D)
    d_fold = jnp.zeros((D, D), F32)
    gain_sum = jnp.zeros((D, D), F32)
    folds_v = []
    for seq in range(own_seqs):
        at = pl.ds(seq * SEQ_LEN, SEQ_LEN)
        lanes = slice(seq * SEQ_LEN, (seq + 1) * SEQ_LEN)
        gain_sum += back_v[seq] * mixed[seq].astype(F32)
        scaled_v = back_v[seq] * shares[seq]
        scaled_b = scaled_v.astype(BF)
        folds_v.append(scaled_b)
        d_probs = nt(scaled_b, next_v[at, 0:D])
        probs = e_v[:, lanes].astype(F32)
        weighted = probs * d_probs
        inner = jnp.sum(weighted, axis=1, keepdims=True) * shares[seq][:, 0:1]
        d_scores = (weighted - probs * inner).astype(BF)
        ds_v[:, lanes] = d_scores
        d_fold += nn(d_scores, next_v[at, 0:D])

    d_fold_b = d_fold.astype(BF)
    d_wk = nn(q_diag.astype(F32).T.astype(BF), d_fold_b)
    d_q = nt(d_fold_b, wk_t) * diag_heads
    d_q = jnp.sum(d_q.reshape(HEADS, LAT, D), axis=0) * HD ** (-0.5)
    d_latent = jnp.sum(upstream.reshape(own_seqs, LAT, D), axis=0) + nn(d_q.astype(BF), wq_t)
    small_v[0:16, :] = d_latent
    gain_rows = jnp.sum(gain_sum + d_fold * fold, axis=0, keepdims=True)
    small_v[16:17, :] = gain_rows / stem_gain
    small_v[23:24, :] = jnp.sum(d_pred, axis=0, keepdims=True)
    square_top = squares.astype(BF).astype(F32)
    small_v[24:25, :] = square_top
    small_v[25:26, :] = squares - square_top
    tail_s[0, 0:64, :] = d_wk[0:64].astype(BF)
    tail_s[0, 64:80, :] = d_q.astype(BF)
    tail_s[1, 0:64, :] = d_wk[64:128].astype(BF)
    tail_s[1, 64:80, :] = jnp.concatenate([d_q[:, 64:], d_q[:, :64]], axis=1).astype(BF)
    for place, begin in ((0, 0), (1, 2)):
        for layer in range(LAYERS):
            row = 26 + 2 * layer
            src = 32 + 4 * layer + begin
            small_v[row : row + 2, :] = small_v[src : src + 2, :]
        small_v[30:32, :] = jnp.zeros((2, D), F32)
        tail_s[place, 80:112, :] = small_v[0:32, :].astype(BF)
    tail_live = [remote(tail_s.at[1], tail_r.at[0], core)]

    def tail_step(level):
        for copy in tail_live:
            copy.wait_recv()
        tail_live.clear()
        first = 1 + sum(radices[: level - 1]) - (level - 1)
        count = 1 if level == 0 else radices[level - 1] - 1
        begin = 0 if level == 0 else first
        mine = tail_s[0 if level == 0 else level + 1].astype(F32)
        total = tree(mine, [tail_r[begin + at].astype(F32) for at in range(count)])
        if level == last:
            return total
        tail_s[level + 2] = total.astype(BF)
        nxt = 1 + sum(radices[:level]) - level
        for offset in range(1, radices[level]):
            dst = tail_r.at[nxt + offset - 1]
            tail_live.append(remote(tail_s.at[level + 2], dst, partner(level, offset)))
        return None

    fold_g = (fold * stem_gain).astype(BF)
    fold_side = jnp.concatenate([fold_g, nn(fold_g, mean_mat).astype(BF)], axis=1)

    def token_grads(seq):
        at = pl.ds(seq * SEQ_LEN, SEQ_LEN)
        lanes = slice(seq * SEQ_LEN, (seq + 1) * SEQ_LEN)
        left = jnp.concatenate([ds_v[:, lanes], e_v[:, lanes]], axis=0)
        value_g = (folds_v[seq].astype(F32) * stem_gain).astype(BF)
        value_side = jnp.concatenate([value_g, nn(value_g, mean_mat).astype(BF)], axis=1)
        both_grads = tn(left, jnp.concatenate([fold_side, value_side], axis=0))
        scaled = both_grads[:, :D]
        unit = unit_v[at, :]
        slope_mean = nn((scaled * unit).astype(BF), mean_mat)
        grad_tokens[at, :] = inv_v[at, :] * (scaled - both_grads[:, D:] - unit * slope_mean)

    steps = [
        lambda: share_on(1, 1),
        lambda: scatter(3),
        lambda: tail_step(0),
        lambda: share_on(2, 1),
        lambda: share_on(0, 2),
        lambda: share_on(3, 1),
        lambda: tail_step(1),
        lambda: share_on(1, 2),
    ]
    for seq in range(own_seqs):
        token_grads(seq)
        if seq < len(steps):
            steps[seq]()
    for step in steps[own_seqs:]:
        step()
    share_on(2, 2)
    share_on(3, 2)
    for level in range(3, last + 1):
        for chunk in range(len(CHUNKS)):
            share_on(chunk, level)
    for level in range(2, last):
        tail_step(level)
    total = tail_step(last)
    tail_out[...] = total
    wq_out[...] = tn(total[64:80, 0:64].astype(BF), latent)
    for chunk in range(len(CHUNKS)):
        received(chunk)
    for copy in sends:
        copy.wait_send()


def split_kernel(
    grad_tokens,
    fin_a,
    fin_b,
    fin_c,
    fin_d,
    tail,
    wq_in,
    head,
    actions,
    masked_loss,
    d_tokens,
    d_stem_norm,
    d_latent,
    d_stem_wq,
    d_stem_wkv,
    d_stem_wo,
    d_norm_attn,
    d_qkv,
    d_out,
    d_norm_mlp,
    d_up,
    d_b_up,
    d_down,
    d_b_down,
    d_act,
    d_b_act,
    sem,
):
    copy = pltpu.make_async_copy(grad_tokens, d_tokens, sem)
    copy.start()
    own_seqs = actions.shape[0]
    for layer, mlp, attn in ((1, fin_a, fin_b), (0, fin_c, fin_d)):
        d_up[layer, :, 0:128] = mlp[0:128, :].astype(F32)
        d_up[layer, :, 128:256] = mlp[128:256, :].astype(F32)
        d_down[layer] = mlp[256:512, :].astype(F32)
        for place in range(3):
            d_qkv[layer, place] = attn[64 * place : 64 * place + 64, :].astype(F32)
        d_out[layer] = attn[192:256, :].astype(F32)
        d_b_up[layer : layer + 1, 0:128] = tail[106 + 2 * layer : 107 + 2 * layer, :]
        d_b_up[layer : layer + 1, 128:256] = tail[107 + 2 * layer : 108 + 2 * layer, :]
    d_act[...] = fin_a[512:640, :].astype(F32)
    d_stem_wo[...] = fin_d[256:320, :].astype(F32)
    d_stem_wkv[1] = fin_d[320:384, :].astype(F32)
    d_stem_wkv[0] = tail[0:64, :]
    d_stem_wq[...] = wq_in[...]
    d_latent[...] = tail[80:96, :]
    d_stem_norm[...] = tail[96:97, :].reshape(D)
    d_norm_attn[...] = tail[97:99, :]
    d_norm_mlp[...] = tail[99:101, :]
    d_b_down[...] = tail[101:103, :]
    d_b_act[...] = tail[103:104, :].reshape(D)
    actions[...] = head[0:own_seqs, :]
    squares = jnp.sum(tail[104:105, :] + tail[105:106, :], axis=1, keepdims=True)
    loss = squares / head[own_seqs : own_seqs + 1, :]
    masked_loss[...] = loss.reshape(D)
    copy.wait()


def on_device(radices, *args):
    (
        tokens,
        stem_norm,
        stem_latent,
        stem_wq,
        stem_wkv,
        stem_wo,
        norm_attn,
        w_qkv,
        w_out,
        norm_mlp,
        w_up,
        b_up,
        w_down,
        b_down,
        w_act,
        b_act,
        span_len,
        joint_mask,
        targets,
    ) = args
    own_seqs = targets.shape[0]
    count = own_seqs * SEQ_LEN
    rows = own_seqs * LAT
    last = len(radices)
    spread = sum(radices) - last
    vmem = pl.BlockSpec(memory_space=pltpu.VMEM)
    hbm = pl.BlockSpec(memory_space=pltpu.HBM)
    total_rows = sum(CHUNKS)
    pieces = total_rows // radices[0]
    wide = max(radices) - 1
    n_remote = 8 + 1 + spread + len(CHUNKS) * (1 + spread + radices[0] - 1) + 1 + spread
    shape = jax.ShapeDtypeStruct
    main = pl.pallas_call(
        functools.partial(main_kernel, radices),
        out_shape=[
            shape((count, D), F32),
            *[shape((size, D), BF) for size in CHUNKS],
            shape((TAIL, D), F32),
            shape((64, D), F32),
            shape((own_seqs + 8, AC), F32),
        ],
        in_specs=[hbm] * len(args),
        out_specs=[vmem] * 8,
        scratch_shapes=[
            pltpu.VMEM((count, D), BF),
            pltpu.VMEM((D,), BF),
            pltpu.VMEM((LAT, D), BF),
            pltpu.VMEM((2, 64, D), BF),
            pltpu.VMEM((2, 2, 64, D), BF),
            pltpu.VMEM((2, 64, D), BF),
            pltpu.VMEM((LAYERS, D), BF),
            pltpu.VMEM((2, LAYERS, 3, 64, D), BF),
            pltpu.VMEM((2, LAYERS, 64, D), BF),
            pltpu.VMEM((LAYERS, D), BF),
            pltpu.VMEM((2, LAYERS, D, FF // 2), BF),
            pltpu.VMEM((2, LAYERS, FF // 2), BF),
            pltpu.VMEM((2, LAYERS, FF // 2, D), BF),
            pltpu.VMEM((LAYERS, D), BF),
            pltpu.VMEM((D, AC), BF),
            pltpu.VMEM((AC,), BF),
            pltpu.SMEM((own_seqs,), jnp.int32),
            pltpu.VMEM((own_seqs, JOINTS), jnp.int32),
            pltpu.VMEM((own_seqs, AC), F32),
            pltpu.VMEM((count, 2 * D), BF),
            pltpu.VMEM((count, D), F32),
            pltpu.VMEM((count, D), F32),
            pltpu.VMEM((D, count), BF),
            pltpu.VMEM((D, count), BF),
            pltpu.VMEM((40, D), F32),
            pltpu.VMEM((1 + last, 8, AC), F32),
            pltpu.VMEM((1 + spread, 8, AC), F32),
            pltpu.VMEM((total_rows, D), BF),
            pltpu.VMEM((total_rows, D), BF),
            pltpu.VMEM((total_rows, D), BF),
            pltpu.VMEM((total_rows, D), BF),
            pltpu.VMEM((wide, pieces, D), BF),
            pltpu.VMEM((last - 1, pieces, D), BF),
            pltpu.VMEM((last - 1, wide, pieces, D), BF),
            pltpu.VMEM((2 + last, TAIL, D), BF),
            pltpu.VMEM((1 + spread, TAIL, D), BF),
            pltpu.SemaphoreType.DMA((len(args),)),
            pltpu.SemaphoreType.DMA((n_remote,)),
            pltpu.SemaphoreType.DMA((n_remote,)),
        ],
        compiler_params=pltpu.CompilerParams(
            collective_id=0, has_side_effects=True, vmem_limit_bytes=40 * 2**20
        ),
        name="stem_trunk_head",
    )(
        *[
            pltpu.with_memory_space_constraint(arg, pltpu.HBM)
            for arg in (
                tokens,
                stem_norm,
                stem_latent,
                jnp.transpose(stem_wq),
                jnp.transpose(stem_wkv, (0, 2, 1)),
                stem_wo,
                norm_attn,
                jnp.transpose(w_qkv, (0, 1, 3, 2)),
                w_out,
                norm_mlp,
                w_up,
                b_up,
                w_down,
                b_down,
                w_act,
                b_act,
                span_len,
                joint_mask,
                targets,
            )
        ]
    )
    outs = [
        shape((own_seqs, AC), F32),
        shape((D,), F32),
        shape((count, D), F32),
        shape((D,), F32),
        shape((LAT, D), F32),
        shape((64, D), F32),
        shape((2, 64, D), F32),
        shape((64, D), F32),
        shape((LAYERS, D), F32),
        shape((LAYERS, 3, 64, D), F32),
        shape((LAYERS, 64, D), F32),
        shape((LAYERS, D), F32),
        shape((LAYERS, D, FF // 2), F32),
        shape((LAYERS, FF // 2), F32),
        shape((LAYERS, FF // 2, D), F32),
        shape((LAYERS, D), F32),
        shape((D, AC), F32),
        shape((AC,), F32),
    ]
    out_specs = [vmem] * len(outs)
    out_specs[2] = pl.BlockSpec(memory_space=pl.ANY)
    result = pl.pallas_call(
        split_kernel,
        out_shape=outs,
        in_specs=[pl.BlockSpec(memory_space=pl.ANY)] + [vmem] * 7,
        out_specs=out_specs,
        scratch_shapes=[pltpu.SemaphoreType.DMA],
        compiler_params=pltpu.CompilerParams(vmem_limit_bytes=20 * 2**20),
        name="split_results",
    )(*main)
    result = list(result)
    result[1] = result[1][0]
    result[5] = jnp.transpose(result[5])
    result[6] = jnp.transpose(result[6], (0, 2, 1))
    result[9] = jnp.transpose(result[9], (0, 1, 3, 2))
    return tuple(result)


def solution(mesh):
    radices = radices_of(mesh.shape["dp"])
    in_specs = (
        P(("dp", "mp"), None),
        P(),
        P(),
        P(None, "mp"),
        P(None, None, "mp"),
        P("mp", None),
        P(),
        P(None, None, None, "mp"),
        P(None, "mp", None),
        P(),
        P(None, None, "mp"),
        P(None, "mp"),
        P(None, "mp", None),
        P(),
        P(),
        P(),
        P(("dp", "mp")),
        P(("dp", "mp"), None),
        P(("dp", "mp"), None),
    )
    out_specs = (
        P(("dp", "mp"), None),
        P(),
        P(("dp", "mp"), None),
        P(),
        P(),
        P(None, "mp"),
        P(None, None, "mp"),
        P("mp", None),
        P(),
        P(None, None, None, "mp"),
        P(None, "mp", None),
        P(),
        P(None, None, "mp"),
        P(None, "mp"),
        P(None, "mp", None),
        P(),
        P(),
        P(),
    )
    return jax.shard_map(
        functools.partial(on_device, radices),
        mesh=mesh,
        in_specs=in_specs,
        out_specs=out_specs,
        check_vma=False,
    )
```

```python
import functools
import math

import jax
import jax.numpy as jnp
from jax import lax
from jax.experimental import pallas as pl
from jax.experimental.pallas import tpu as pltpu
from jax.sharding import PartitionSpec as P

HD = 16
LAT = 16
SEQ_LEN = 256
SPAN = 16
JOINTS = 8
HEADS = 8
D = 128
FF = 512
AC = 128
LAYERS = 2

F32 = jnp.float32
BF = jnp.bfloat16
MESH = pl.DeviceIdType.MESH
epsilon = 1e-05
highest = lax.Precision.HIGHEST

CHUNKS = (256, 256, 256, 256, 256, 256, 256, 128)


def nn(left, right):
    return jnp.dot(left, right, preferred_element_type=F32)


def nt(left, right):
    return lax.dot_general(left, right, (((1,), (1,)), ((), ())), preferred_element_type=F32)


def tn(left, right):
    return lax.dot_general(left, right, (((0,), (0,)), ((), ())), preferred_element_type=F32)


def iota(shape, axis):
    return lax.broadcasted_iota(jnp.int32, shape, axis)


def radices_of(count):
    found = []
    while count > 1:
        radix = 8 if count % 8 == 0 else 4 if count % 4 == 0 else 2
        found.append(radix)
        count //= radix
    return found


def flip(digit, offset):
    flipped = digit
    for bit in (1, 2, 4):
        if offset & bit:
            flipped = flipped + bit - 2 * bit * ((digit // bit) % 2)
    return flipped


def far_first(radix):
    return sorted(range(1, radix), key=lambda offset: -bin(offset).count("1"))


def norm_rows(values_in, gain_vec):
    mean_rows = jnp.mean(values_in, axis=-1, keepdims=True)
    centred = values_in - mean_rows
    variance = jnp.mean(centred * centred, axis=-1, keepdims=True)
    inv_rows = lax.rsqrt(variance + epsilon)
    unit_rows = centred * inv_rows
    return unit_rows * gain_vec, unit_rows, inv_rows


def norm_back(upstream, unit_rows, inv_rows, gain_vec):
    scaled = upstream * gain_vec
    inner = (
        scaled
        - jnp.mean(scaled, axis=-1, keepdims=True)
        - unit_rows * jnp.mean(scaled * unit_rows, axis=-1, keepdims=True)
    )
    return inv_rows * inner


def split_rows(values_in):
    first = values_in.astype(BF).astype(F32)
    rest = values_in - first
    second = rest.astype(BF).astype(F32)
    return jnp.concatenate([first, second, rest - second], axis=0).astype(BF)


def main_kernel(
    radices,
    tokens_h,
    stem_norm_h,
    stem_latent_h,
    stem_wq_h,
    stem_wkv_h,
    stem_wo_h,
    norm_attn_h,
    w_qkv_h,
    w_out_h,
    norm_mlp_h,
    w_up_h,
    b_up_h,
    w_down_h,
    b_down_h,
    w_act_h,
    b_act_h,
    span_len_h,
    joint_mask_h,
    targets_h,
    grad_tokens,
    fin_a,
    fin_b,
    fin_c,
    fin_d,
    fin_e,
    fin_f,
    fin_g,
    fin_h,
    wq_out,
    head_out,
    x_v,
    stem_norm_v,
    stem_latent_v,
    wq_v,
    wkv_v,
    wo_v,
    norm_attn_v,
    wqkv_v,
    wout_v,
    norm_mlp_v,
    wup_v,
    bup_v,
    wdn_v,
    b_down_v,
    w_act_v,
    b_act_v,
    span_s,
    joint_v,
    targets_v,
    next_v,
    unit_v,
    inv_v,
    e_v,
    ds_v,
    small_v,
    ent_v,
    ent_r,
    own,
    oth,
    rcv,
    snd,
    rs_r,
    part,
    full_r,
    in_sem,
    send_sem,
    recv_sem,
):
    dp, mp = lax.axis_index("dp"), lax.axis_index("mp")
    own_seqs = targets_h.shape[0]
    rows = own_seqs * LAT
    fins = (fin_a, fin_b, fin_c, fin_d, fin_e, fin_f, fin_g, fin_h)
    core = (dp, 1 - mp)
    digits = [(dp // math.prod(radices[:level])) % radix for level, radix in enumerate(radices)]

    places = {}

    def partner(level, offset):
        stride = math.prod(radices[:level])
        if (level, offset) not in places:
            digit = digits[level]
            places[level, offset] = (dp + (flip(digit, offset) - digit) * stride, mp)
        return places[level, offset]

    def apart(step, *given):
        pl.when(dp >= 0)(functools.partial(step, *given))

    barrier = pltpu.get_barrier_semaphore()
    greeted = [core]
    for level, radix in enumerate(radices):
        greeted += [partner(level, offset) for offset in range(1, radix)]
    for device in greeted:
        pl.semaphore_signal(barrier, inc=1, device_id=device, device_id_type=MESH)

    piece_of = {}
    for size in sorted({chunk // radices[0] for chunk in CHUNKS}):
        piece_of[size] = [
            pl.multiple_of(flip(digits[0], offset) * size, size) for offset in range(radices[0])
        ]
    slots = [0]
    sends = []

    def remote(ends, device):
        slot = slots[0]
        slots[0] += 1

        def copy():
            src, dst = ends()
            return pltpu.make_async_remote_copy(
                src_ref=src,
                dst_ref=dst,
                send_sem=send_sem.at[slot],
                recv_sem=recv_sem.at[slot],
                device_id=device,
                device_id_type=MESH,
            )

        copy().start()
        sends.append(copy)
        return copy

    local = {}
    pairs = (
        ("tokens", tokens_h, x_v),
        ("stem_norm", stem_norm_h, stem_norm_v),
        ("stem_latent", stem_latent_h, stem_latent_v),
        ("wq", stem_wq_h, wq_v),
        ("wkv", stem_wkv_h, wkv_v),
        ("wo", stem_wo_h, wo_v),
        ("wqkv", w_qkv_h, wqkv_v),
        ("wout", w_out_h, wout_v),
        ("wup", w_up_h, wup_v),
        ("wdn", w_down_h, wdn_v),
        ("norm_attn", norm_attn_h, norm_attn_v),
        ("norm_mlp", norm_mlp_h, norm_mlp_v),
        ("bup", b_up_h, bup_v),
        ("b_down", b_down_h, b_down_v),
        ("w_act", w_act_h, w_act_v),
        ("b_act", b_act_h, b_act_v),
        ("span", span_len_h, span_s),
        ("joint", joint_mask_h, joint_v),
        ("targets", targets_h, targets_v),
    )
    halves = ("wq", "wkv", "wo", "wqkv", "wout", "wup", "wdn", "bup")

    def load(place, name, src, dst):
        here = dst.at[0] if name in halves else dst
        return pltpu.make_async_copy(src, here, in_sem.at[place])

    for place, (name, src, dst) in enumerate(pairs):
        local[name] = functools.partial(load, place, name, src, dst)
        local[name]().start()

    head_mask = (
        (iota((HEADS, D, D), 2) // HD == iota((HEADS, D, D), 0)).astype(F32).astype(BF)
    )
    row_mask = (iota((HEADS, D, D), 1) // HD == iota((HEADS, D, D), 0)).astype(F32).astype(BF)
    diag_heads = (iota((D, D), 0) // LAT == iota((D, D), 1) // HD).astype(F32)
    block_add = jnp.where(iota((rows, rows), 0) // LAT == iota((rows, rows), 1) // LAT, 0.0, -1e30)
    mean_mat = jnp.full((D, D), 1.0 / D, BF)
    mean_twice = jnp.full((2 * D, D), 1.0 / D, BF)

    gathered = {}

    def entries_step(level):
        for copy in pending:
            copy().wait_recv()
        if level == 0:
            total = ent_v[0] + ent_r[0]
        else:
            total = tree(ent_v[level], [ent_r[at] for at in ent_slots[-1]])
        if level == len(radices):
            return total
        ent_v[level + 1] = total
        pending.clear()
        places = []
        for offset in range(1, radices[level]):
            place = 1 + sum(radices[:level]) - level + offset - 1
            places.append(place)
            pending.append(
                remote(
                    lambda place=place: (ent_v.at[level + 1], ent_r.at[place]),
                    partner(level, offset),
                )
            )
        ent_slots.append(places)
        return None

    ent_slots = []

    def tree(mine, others):
        terms = [mine] + list(others)
        while len(terms) > 1:
            terms = [terms[at] + terms[at + 1] for at in range(0, len(terms), 2)]
        return terms[0]

    def wait_for(*names):
        for name in names:
            local[name]().wait()

    def wait_gathered(*names):
        for name in names:
            gathered[name]().wait_recv()

    def meet():
        pl.semaphore_wait(barrier, len(greeted))
        for name, src, dst in pairs:
            if name in halves:
                gathered[name] = remote(lambda src=src, dst=dst: (src, dst.at[1]), core)

    apart(meet)

    apart(wait_for, "tokens", "stem_norm")
    stem_gain = stem_norm_v[...].astype(F32).reshape(1, D)
    half = own_seqs * SEQ_LEN // 2
    for start in (0, half):
        at = pl.ds(start, half)
        raw = x_v[at, :]
        centred = raw.astype(F32) - nn(raw, mean_mat)
        square = centred * centred
        upper = square.astype(BF)
        lower = (square - upper.astype(F32)).astype(BF)
        inv = lax.rsqrt(nn(jnp.concatenate([upper, lower], axis=1), mean_twice) + epsilon)
        unit = centred * inv
        inv_v[at, :] = inv
        unit_v[at, :] = unit
        next_v[at, 0:D] = (unit * stem_gain).astype(BF)
        next_v[at, D : 2 * D] = jnp.ones((half, D), BF)

    def both(ref, *index):
        return jnp.concatenate([ref[(0,) + index], ref[(1,) + index]], axis=0)

    apart(wait_for, "span", "joint")
    spans = jnp.zeros((own_seqs, AC), jnp.int32)
    for seq in range(own_seqs):
        spans = jnp.where(iota((own_seqs, AC), 0) == seq, span_s[seq], spans)
    joints = (joint_v[...] > 0).astype(F32).astype(BF)
    spread = (iota((JOINTS, AC), 1) % JOINTS == iota((JOINTS, AC), 0)).astype(F32).astype(BF)
    valid = jnp.where(iota((own_seqs, AC), 1) // JOINTS < spans, nn(joints, spread), 0.0)
    ent_v[0] = jnp.broadcast_to(jnp.sum(valid, axis=0, keepdims=True), (8, AC))
    pending = []

    def entries_begin():
        pending.append(remote(lambda: (ent_v.at[0], ent_r.at[0]), core))

    apart(entries_begin)

    apart(wait_for, "stem_latent", "wq", "wkv")
    apart(wait_gathered, "wq", "wkv")
    latent = stem_latent_v[...]
    wq_t = both(wq_v)
    wk_t, wv_t = both(wkv_v, 0), both(wkv_v, 1)
    stem_q = nt(latent, wq_t).astype(BF).astype(F32) * HD ** (-0.5)
    q_diag = (jnp.concatenate([stem_q] * HEADS, axis=0) * diag_heads).astype(BF)
    fold = nn(q_diag, wk_t)
    fold_b = fold.astype(BF)
    mixed, shares = [], []
    for seq in range(own_seqs):
        at = pl.ds(seq * SEQ_LEN, SEQ_LEN)
        scores = nt(fold_b, next_v[at, 0:D])
        probs = jnp.exp(scores - jnp.max(scores, axis=1, keepdims=True)).astype(BF)
        e_v[:, seq * SEQ_LEN : (seq + 1) * SEQ_LEN] = probs
        both_sums = nn(probs, next_v[at, :])
        share = 1.0 / both_sums[:, D:]
        shares.append(share)
        mixed.append((both_sums[:, :D] * share).astype(BF))
    apart(entries_step, 0)
    mixed_all = jnp.concatenate(mixed, axis=0)
    heads_out = nt(mixed_all, wv_t).reshape(own_seqs, D, D) * diag_heads[None]
    stem_out = jnp.sum(heads_out.reshape(own_seqs, HEADS, LAT, D), axis=1).reshape(rows, D)
    stem_out = stem_out.astype(BF)
    apart(wait_for, "wo")
    apart(wait_gathered, "wo")
    stem_wo = both(wo_v)
    latent_f = latent.astype(F32)
    hidden = jnp.concatenate([latent_f] * own_seqs, axis=0) + nn(stem_out, stem_wo)

    apart(wait_for, "norm_attn", "norm_mlp", "b_down", "w_act", "b_act", "targets")
    apart(wait_for, "wqkv", "wout", "wup", "wdn", "bup")
    apart(wait_gathered, "wqkv", "wout", "wup", "wdn", "bup")
    gain_attn = norm_attn_v[...].astype(F32)
    gain_mlp = norm_mlp_v[...].astype(F32)
    down_bias = b_down_v[...].astype(F32)
    up_bias = jnp.concatenate([bup_v[0], bup_v[1]], axis=1).astype(F32)

    def heads_below(matrix):
        return (matrix[None] * head_mask).reshape(HEADS * rows, D)

    def heads_beside(matrix):
        return jnp.concatenate([matrix * row_mask[head] for head in range(HEADS)], axis=1)

    def lanes_beside(cube):
        return jnp.concatenate([cube[head] for head in range(HEADS)], axis=1)

    def trunk_forward(residual, layer):
        gain_a, gain_m = gain_attn[layer : layer + 1], gain_mlp[layer : layer + 1]
        qkv = jnp.concatenate([both(wqkv_v, layer, part_at) for part_at in range(3)], axis=0)
        out_mat = both(wout_v, layer)
        up_mat = jnp.concatenate([wup_v[0, layer], wup_v[1, layer]], axis=1)
        down_mat = both(wdn_v, layer)
        normed, unit_a, inv_a = norm_rows(residual, gain_a)
        rows_a = normed.astype(BF)
        flat = nt(rows_a, qkv).astype(BF)
        queries = flat[:, :D] * jnp.asarray(HD ** (-0.5), BF)
        keys, values = flat[:, D : 2 * D], flat[:, 2 * D :]
        keys_t = nt(qkv[D : 2 * D], rows_a).astype(BF) * jnp.asarray(HD ** (-0.5), BF)
        values_t = nt(qkv[2 * D :], rows_a).astype(BF)
        scores = nt(heads_below(keys), queries).reshape(HEADS, rows, rows) + block_add[None]
        exped = jnp.exp(scores - jnp.max(scores, axis=1, keepdims=True))
        probs = exped / jnp.sum(exped, axis=1, keepdims=True)
        probs_b = probs.astype(BF)
        out_t = nn(heads_beside(values_t), probs_b.reshape(HEADS * rows, rows))
        attended = out_t.T.astype(BF)
        middle = residual + nn(attended, out_mat)
        normed_m, unit_m, inv_m = norm_rows(middle, gain_m)
        rows_m = normed_m.astype(BF)
        up_rows = nn(rows_m, up_mat) + up_bias[layer : layer + 1]
        cdf = 0.5 + 0.5 * lax.erf(up_rows * (0.5**0.5))
        slope = cdf + up_rows * (jnp.exp(-0.5 * up_rows * up_rows) * 0.3989422804014327)
        hidden_act = (up_rows * cdf).astype(BF)
        output = middle + nn(hidden_act, down_mat) + down_bias[layer : layer + 1]
        saved = dict(
            gain_a=gain_a, gain_m=gain_m, qkv=qkv, out_mat=out_mat, up_mat=up_mat,
            down_mat=down_mat, unit_a=unit_a, inv_a=inv_a, rows_a=rows_a, queries=queries,
            keys_t=keys_t, values=values, probs=probs, probs_b=probs_b, attended=attended,
            unit_m=unit_m, inv_m=inv_m, rows_m=rows_m, slope=slope, hidden_act=hidden_act,
        )
        return output, saved

    kept = []
    for layer in range(LAYERS):
        hidden, saved = trunk_forward(hidden, layer)
        kept.append(saved)

    pooled = jnp.sum(hidden.reshape(own_seqs, LAT, D), axis=1)
    act_mat = w_act_v[...]

    def summed3(stacked):
        return stacked[0:own_seqs] + stacked[own_seqs : 2 * own_seqs] + stacked[2 * own_seqs :]

    pred = summed3(nn(split_rows(pooled), act_mat)) + b_act_v[...].astype(F32).reshape(1, AC)
    errors = pred - targets_v[...]
    squares = jnp.sum(valid * errors * errors, axis=0, keepdims=True)
    d_pred = valid * errors
    head_out[0:own_seqs] = valid * pred
    d_act = lax.dot_general(
        pooled, d_pred, (((0,), (0,)), ((), ())), precision=highest, preferred_element_type=F32
    ).astype(BF)
    d_pooled = summed3(nt(split_rows(d_pred), act_mat))
    upstream = jnp.broadcast_to(d_pooled[:, None, :], (own_seqs, LAT, D)).reshape(rows, D)

    first_row = [sum(CHUNKS[:chunk]) for chunk in range(len(CHUNKS))]
    first_piece = [begin // radices[0] for begin in first_row]
    live = [[] for _ in CHUNKS]

    def put(chunk, offset, mine, others):
        at = pl.ds(first_row[chunk] + offset, mine.shape[0])
        own[at, :] = mine.astype(BF)
        oth[at, :] = others.astype(BF)

    def core_send(chunk):
        at = pl.ds(first_row[chunk], CHUNKS[chunk])
        live[chunk] = [remote(lambda: (oth.at[at], rcv.at[at]), core)]

    def received(chunk):
        for copy in live[chunk]:
            copy().wait_recv()
        live[chunk] = []

    def scatter(chunk):
        received(chunk)
        at = pl.ds(first_row[chunk], CHUNKS[chunk])
        snd[at, :] = (own[at, :].astype(F32) + rcv[at, :].astype(F32)).astype(BF)
        size = CHUNKS[chunk] // radices[0]
        here = pl.ds(first_piece[chunk], size)
        for offset in far_first(radices[0]):
            piece = pl.ds(piece_of[size][offset], size)

            def ends(piece=piece, offset=offset):
                return snd.at[at].at[piece], rs_r.at[offset - 1, here]

            live[chunk].append(remote(ends, partner(0, offset)))

    def share_on(chunk, level):
        received(chunk)
        size = CHUNKS[chunk] // radices[0]
        here = pl.ds(first_piece[chunk], size)
        if level == 1:
            whole = snd.at[pl.ds(first_row[chunk], CHUNKS[chunk])]
            mine = whole[pl.ds(piece_of[size][0], size), :].astype(F32)
            got = [rs_r[at, here, :].astype(F32) for at in range(radices[0] - 1)]
        else:
            mine = part[level - 2, here, :].astype(F32)
            got = [full_r[level - 2, at, here, :].astype(F32) for at in range(radices[level - 1] - 1)]
        total = tree(mine, got).astype(BF)
        if level < len(radices):
            part[level - 1, here, :] = total
            for offset in range(1, radices[level]):

                def ends(offset=offset):
                    return part.at[level - 1, here], full_r.at[level - 1, offset - 1, here]

                live[chunk].append(remote(ends, partner(level, offset)))
            return
        mine_at = pl.ds(piece_of[size][0], size)
        fins[chunk][mine_at, :] = total
        for offset in far_first(radices[0]):
            live[chunk].append(
                remote(lambda: (fins[chunk].at[mine_at], fins[chunk].at[mine_at]), partner(0, offset))
            )

    last = len(radices)

    def back_mlp(upstream, layer, chunk):
        kv = kept[layer]
        grad_top = upstream.astype(BF)
        small_v[16 + 5 + layer : 16 + 6 + layer, :] = jnp.sum(
            grad_top.astype(F32), axis=0, keepdims=True
        )
        d_hidden = nt(grad_top, kv["down_mat"])
        d_upper = (kv["slope"] * d_hidden).astype(BF)
        d_rows = nt(d_upper, kv["up_mat"])
        d_middle = upstream + norm_back(d_rows, kv["unit_m"], kv["inv_m"], kv["gain_m"])
        small_v[16 + 3 + layer : 16 + 4 + layer, :] = jnp.sum(
            d_rows * kv["unit_m"], axis=0, keepdims=True
        )
        d_bias = jnp.sum(d_upper.astype(F32), axis=0, keepdims=True)
        for block in range(4):
            row = 32 + 4 * layer + block
            small_v[row : row + 1, :] = d_bias[:, block * D : (block + 1) * D]
        d_down = tn(kv["hidden_act"], grad_top)
        d_up = tn(kv["rows_m"], d_upper)
        put(chunk, 0, d_up[:, 0:128], d_up[:, 256:384])
        put(chunk, 128, d_up[:, 128:256], d_up[:, 384:512])
        put(chunk + 1, 0, d_down[0:256], d_down[256:512])
        return d_middle

    def back_attn(d_middle, layer, chunk):
        kv = kept[layer]
        grad_attn = d_middle.astype(BF)
        d_mixed = nt(grad_attn, kv["out_mat"]).astype(BF)
        d_probs = nt(heads_below(kv["values"]), d_mixed).reshape(HEADS, rows, rows)
        probs = kv["probs"]
        weighted = probs * d_probs
        inner = jnp.sum(weighted, axis=1, keepdims=True)
        d_scores = (weighted - probs * inner).astype(BF)
        d_q_t = nn(heads_beside(kv["keys_t"]), d_scores.reshape(HEADS * rows, rows))
        d_keys = nn(lanes_beside(d_scores), heads_below(kv["queries"])).astype(BF)
        d_values = nn(lanes_beside(kv["probs_b"]), heads_below(d_mixed)).astype(BF)
        grads = jnp.concatenate([d_q_t.T.astype(BF), d_keys, d_values], axis=1)
        d_rows = nn(grads, kv["qkv"])
        small_v[16 + 1 + layer : 16 + 2 + layer, :] = jnp.sum(
            d_rows * kv["unit_a"], axis=0, keepdims=True
        )
        d_input = d_middle + norm_back(d_rows, kv["unit_a"], kv["inv_a"], kv["gain_a"])
        d_out = tn(kv["attended"], grad_attn)
        d_qkv = tn(grads, kv["rows_a"])
        for place in range(3):
            begin = place * D
            put(chunk, place * 64, d_qkv[begin : begin + 64], d_qkv[begin + 64 : begin + 128])
        put(chunk, 192, d_out[0:64], d_out[64:128])
        return d_input

    put(6, 128, d_act, d_act)
    upstream = back_mlp(upstream, 1, 0)
    apart(core_send, 0)
    apart(core_send, 1)
    apart(entries_step, 1)
    upstream = back_attn(upstream, 1, 2)
    apart(core_send, 2)
    apart(scatter, 0)
    upstream = back_mlp(upstream, 0, 3)
    apart(core_send, 3)
    apart(core_send, 4)
    apart(scatter, 1)
    upstream = back_attn(upstream, 0, 5)
    apart(core_send, 5)
    for chunk in (2, 3, 4):
        apart(scatter, chunk)

    grad_stem = upstream.astype(BF)
    d_out_t = nt(stem_wo, grad_stem).astype(BF)
    d_out = nt(grad_stem, stem_wo).astype(BF)
    d_stem_wo = tn(stem_out, grad_stem)
    put(6, 0, d_stem_wo[0:64], d_stem_wo[64:128])
    mixed_heads = jnp.transpose(
        mixed_all.reshape(own_seqs, HEADS, LAT, D), (1, 0, 2, 3)
    ).reshape(HEADS * rows, D)
    d_wv = nn(heads_beside(d_out_t), mixed_heads)
    put(6, 64, d_wv[0:64], d_wv[64:128])
    apart(core_send, 6)
    diag_b = diag_heads.astype(BF).reshape(1, HEADS, LAT, D)
    d_diag = (d_out.reshape(own_seqs, 1, LAT, D) * diag_b).reshape(own_seqs, D, D)
    back_v = nn(d_diag.reshape(own_seqs * D, D), wv_t).reshape(own_seqs, D, D)
    d_fold = jnp.zeros((D, D), F32)
    gain_sum = jnp.zeros((D, D), F32)
    folds_v = []
    for seq in range(own_seqs):
        at = pl.ds(seq * SEQ_LEN, SEQ_LEN)
        lanes = slice(seq * SEQ_LEN, (seq + 1) * SEQ_LEN)
        gain_sum += back_v[seq] * mixed[seq].astype(F32)
        scaled_v = back_v[seq] * shares[seq]
        scaled_b = scaled_v.astype(BF)
        folds_v.append(scaled_b)
        d_probs = nt(scaled_b, next_v[at, 0:D])
        probs = e_v[:, lanes].astype(F32)
        weighted = probs * d_probs
        inner = jnp.sum(weighted, axis=1, keepdims=True) * shares[seq][:, 0:1]
        d_scores = (weighted - probs * inner).astype(BF)
        ds_v[:, lanes] = d_scores
        d_fold += nn(d_scores, next_v[at, 0:D])

    apart(scatter, 5)
    apart(scatter, 6)

    d_fold_b = d_fold.astype(BF)
    d_wk = nn(q_diag.astype(F32).T.astype(BF), d_fold_b)
    d_q = nt(d_fold_b, wk_t) * diag_heads
    d_q = jnp.sum(d_q.reshape(HEADS, LAT, D), axis=0) * HD ** (-0.5)
    d_latent = jnp.sum(upstream.reshape(own_seqs, LAT, D), axis=0) + nn(d_q.astype(BF), wq_t)
    small_v[0:16, :] = d_latent
    gain_rows = jnp.sum(gain_sum + d_fold * fold, axis=0, keepdims=True)
    small_v[16:17, :] = gain_rows / stem_gain
    small_v[23:24, :] = jnp.sum(d_pred, axis=0, keepdims=True)
    small_v[24:25, :] = squares
    for layer in range(LAYERS):
        small_v[25 + 2 * layer : 27 + 2 * layer, :] = small_v[32 + 4 * layer : 34 + 4 * layer, :]
    small_v[29:32, :] = jnp.zeros((3, D), F32)
    shared = small_v[0:32, :]
    d_q_other = jnp.concatenate([d_q[:, 64:], d_q[:, :64]], axis=1)
    put(7, 0, d_wk[0:64], d_wk[64:128])
    put(7, 64, d_q, d_q_other)
    put(7, 80, shared, shared)
    for layer in range(LAYERS):
        small_v[25 + 2 * layer : 27 + 2 * layer, :] = small_v[34 + 4 * layer : 36 + 4 * layer, :]
    oth[first_row[7] + 96 : first_row[7] + 112, :] = small_v[16:32, :].astype(BF)
    own[first_row[7] + 112 : first_row[7] + 128, :] = jnp.zeros((16, D), BF)
    oth[first_row[7] + 112 : first_row[7] + 128, :] = jnp.zeros((16, D), BF)
    apart(core_send, 7)

    for level in range(2, last):
        apart(entries_step, level)
    entries = jnp.sum(entries_step(last)[0:1], axis=1, keepdims=True)
    total_seqs = own_seqs * lax.axis_size("dp") * lax.axis_size("mp")
    factor = total_seqs * AC / entries
    head_out[own_seqs : own_seqs + 8] = jnp.broadcast_to(entries, (8, AC))
    head_out[own_seqs + 8 : own_seqs + 16] = jnp.broadcast_to(factor, (8, AC))

    fold_g = (fold * stem_gain).astype(BF)
    fold_side = jnp.concatenate([fold_g, nn(fold_g, mean_mat).astype(BF)], axis=1)

    def token_grads(seq):
        at = pl.ds(seq * SEQ_LEN, SEQ_LEN)
        lanes = slice(seq * SEQ_LEN, (seq + 1) * SEQ_LEN)
        left = jnp.concatenate([ds_v[:, lanes], e_v[:, lanes]], axis=0)
        value_g = (folds_v[seq].astype(F32) * stem_gain).astype(BF)
        value_side = jnp.concatenate([value_g, nn(value_g, mean_mat).astype(BF)], axis=1)
        both_grads = tn(left, jnp.concatenate([fold_side, value_side], axis=0))
        scaled = both_grads[:, :D]
        unit = unit_v[at, :]
        slope_mean = nn((scaled * unit).astype(BF), mean_mat)
        grad_tokens[at, :] = (factor * inv_v[at, :]) * (scaled - both_grads[:, D:] - unit * slope_mean)

    order = (
        (1, share_on, 0, 1),
        (2, scatter, 7),
        (3, share_on, 1, 1),
        (5, share_on, 2, 1),
        (7, share_on, 3, 1),
        (8, share_on, 4, 1),
        (8, share_on, 5, 1),
        (8, share_on, 0, 2),
        (8, share_on, 6, 1),
        (8, share_on, 1, 2),
        (8, share_on, 7, 1),
        (8, share_on, 2, 2),
        (8, share_on, 3, 2),
        (8, share_on, 4, 2),
        (8, share_on, 5, 2),
        (8, share_on, 6, 2),
        (8, share_on, 7, 2),
    )
    for seq in range(own_seqs):
        for place, *step in order:
            if place == seq:
                apart(*step)
        token_grads(seq)
    for place, *step in order:
        if place >= own_seqs:
            apart(*step)
    for level in range(3, last + 1):
        for chunk in range(len(CHUNKS)):
            apart(share_on, chunk, level)
    for chunk in range(len(CHUNKS)):
        apart(received, chunk)
    wq_out[...] = tn(fin_h[64:80, 0:64], latent)
    for copy in sends:
        copy().wait_send()


def split_kernel(
    grad_tokens,
    fin_a,
    fin_b,
    fin_c,
    fin_d,
    fin_e,
    fin_f,
    fin_g,
    fin_h,
    wq_in,
    head,
    actions,
    masked_loss,
    d_tokens,
    d_stem_norm,
    d_latent,
    d_stem_wq,
    d_stem_wkv,
    d_stem_wo,
    d_norm_attn,
    d_qkv,
    d_out,
    d_norm_mlp,
    d_up,
    d_b_up,
    d_down,
    d_b_down,
    d_act,
    d_b_act,
    sem,
):
    copy = pltpu.make_async_copy(grad_tokens, d_tokens, sem)
    copy.start()
    own_seqs = actions.shape[0]
    factor = head[own_seqs + 8 : own_seqs + 9, :]
    for layer, up, down, attn in ((1, fin_a, fin_b, fin_c), (0, fin_d, fin_e, fin_f)):
        d_up[layer, :, 0:128] = up[0:128, :].astype(F32) * factor
        d_up[layer, :, 128:256] = up[128:256, :].astype(F32) * factor
        d_down[layer] = down[...].astype(F32) * factor
        for place in range(3):
            d_qkv[layer, place] = attn[64 * place : 64 * place + 64, :].astype(F32) * factor
        d_out[layer] = attn[192:256, :].astype(F32) * factor
    d_act[...] = fin_g[128:256, :].astype(F32) * factor
    d_stem_wo[...] = fin_g[0:64, :].astype(F32) * factor
    d_stem_wkv[1] = fin_g[64:128, :].astype(F32) * factor
    d_stem_wkv[0] = fin_h[0:64, :].astype(F32) * factor
    tail = fin_h[64:128, :].astype(F32) * factor
    for layer in range(LAYERS):
        d_b_up[layer : layer + 1, 0:128] = tail[41 + 2 * layer : 42 + 2 * layer, :]
        d_b_up[layer : layer + 1, 128:256] = tail[42 + 2 * layer : 43 + 2 * layer, :]
    d_stem_wq[...] = factor * wq_in[...]
    d_latent[...] = tail[16:32, :]
    d_stem_norm[...] = tail[32:33, :].reshape(D)
    d_norm_attn[...] = tail[33:35, :]
    d_norm_mlp[...] = tail[35:37, :]
    d_b_down[...] = tail[37:39, :]
    d_b_act[...] = tail[39:40, :].reshape(D)
    actions[...] = head[0:own_seqs, :]
    squares = jnp.sum(fin_h[64:128, :].astype(F32)[40:41, :], axis=1, keepdims=True)
    loss = squares / head[own_seqs : own_seqs + 1, :]
    masked_loss[...] = loss.reshape(D)
    copy.wait()


def on_device(radices, *args):
    (
        tokens,
        stem_norm,
        stem_latent,
        stem_wq,
        stem_wkv,
        stem_wo,
        norm_attn,
        w_qkv,
        w_out,
        norm_mlp,
        w_up,
        b_up,
        w_down,
        b_down,
        w_act,
        b_act,
        span_len,
        joint_mask,
        targets,
    ) = args
    own_seqs = targets.shape[0]
    count = own_seqs * SEQ_LEN
    rows = own_seqs * LAT
    last = len(radices)
    spread = sum(radices) - last
    vmem = pl.BlockSpec(memory_space=pltpu.VMEM)
    hbm = pl.BlockSpec(memory_space=pltpu.HBM)
    total_rows = sum(CHUNKS)
    wide = max(radices) - 1

    def summing(count_rows, dtype):
        pieces = count_rows // radices[0]
        return [
            *[pltpu.VMEM((count_rows, D), dtype)] * 4,
            pltpu.VMEM((wide, pieces, D), dtype),
            pltpu.VMEM((last - 1, pieces, D), dtype),
            pltpu.VMEM((last - 1, wide, pieces, D), dtype),
        ]

    n_remote = 8 + 1 + spread + len(CHUNKS) * (1 + spread + radices[0] - 1)
    shape = jax.ShapeDtypeStruct
    main = pl.pallas_call(
        functools.partial(main_kernel, radices),
        out_shape=[
            shape((count, D), F32),
            *[shape((size, D), BF) for size in CHUNKS],
            shape((64, D), F32),
            shape((own_seqs + 16, AC), F32),
        ],
        in_specs=[hbm] * len(args),
        out_specs=[vmem] * (3 + len(CHUNKS)),
        scratch_shapes=[
            pltpu.VMEM((count, D), BF),
            pltpu.VMEM((D,), BF),
            pltpu.VMEM((LAT, D), BF),
            pltpu.VMEM((2, 64, D), BF),
            pltpu.VMEM((2, 2, 64, D), BF),
            pltpu.VMEM((2, 64, D), BF),
            pltpu.VMEM((LAYERS, D), BF),
            pltpu.VMEM((2, LAYERS, 3, 64, D), BF),
            pltpu.VMEM((2, LAYERS, 64, D), BF),
            pltpu.VMEM((LAYERS, D), BF),
            pltpu.VMEM((2, LAYERS, D, FF // 2), BF),
            pltpu.VMEM((2, LAYERS, FF // 2), BF),
            pltpu.VMEM((2, LAYERS, FF // 2, D), BF),
            pltpu.VMEM((LAYERS, D), BF),
            pltpu.VMEM((D, AC), BF),
            pltpu.VMEM((AC,), BF),
            pltpu.SMEM((own_seqs,), jnp.int32),
            pltpu.VMEM((own_seqs, JOINTS), jnp.int32),
            pltpu.VMEM((own_seqs, AC), F32),
            pltpu.VMEM((count, 2 * D), BF),
            pltpu.VMEM((count, D), F32),
            pltpu.VMEM((count, D), F32),
            pltpu.VMEM((D, count), BF),
            pltpu.VMEM((D, count), BF),
            pltpu.VMEM((40, D), F32),
            pltpu.VMEM((1 + last, 8, AC), F32),
            pltpu.VMEM((1 + spread, 8, AC), F32),
            *summing(total_rows, BF),
            pltpu.SemaphoreType.DMA((len(args),)),
            pltpu.SemaphoreType.DMA((n_remote,)),
            pltpu.SemaphoreType.DMA((n_remote,)),
        ],
        compiler_params=pltpu.CompilerParams(
            collective_id=0, has_side_effects=True, vmem_limit_bytes=40 * 2**20
        ),
        name="stem_trunk_head",
    )(
        *[
            pltpu.with_memory_space_constraint(arg, pltpu.HBM)
            for arg in (
                tokens,
                stem_norm,
                stem_latent,
                jnp.transpose(stem_wq),
                jnp.transpose(stem_wkv, (0, 2, 1)),
                stem_wo,
                norm_attn,
                jnp.transpose(w_qkv, (0, 1, 3, 2)),
                w_out,
                norm_mlp,
                w_up,
                b_up,
                w_down,
                b_down,
                w_act,
                b_act,
                span_len,
                joint_mask,
                targets,
            )
        ]
    )
    outs = [
        shape((own_seqs, AC), F32),
        shape((D,), F32),
        shape((count, D), F32),
        shape((D,), F32),
        shape((LAT, D), F32),
        shape((64, D), F32),
        shape((2, 64, D), F32),
        shape((64, D), F32),
        shape((LAYERS, D), F32),
        shape((LAYERS, 3, 64, D), F32),
        shape((LAYERS, 64, D), F32),
        shape((LAYERS, D), F32),
        shape((LAYERS, D, FF // 2), F32),
        shape((LAYERS, FF // 2), F32),
        shape((LAYERS, FF // 2, D), F32),
        shape((LAYERS, D), F32),
        shape((D, AC), F32),
        shape((AC,), F32),
    ]
    out_specs = [vmem] * len(outs)
    out_specs[2] = pl.BlockSpec(memory_space=pl.ANY)
    result = pl.pallas_call(
        split_kernel,
        out_shape=outs,
        in_specs=[pl.BlockSpec(memory_space=pl.ANY)] + [vmem] * (2 + len(CHUNKS)),
        out_specs=out_specs,
        scratch_shapes=[pltpu.SemaphoreType.DMA],
        compiler_params=pltpu.CompilerParams(vmem_limit_bytes=20 * 2**20),
        name="split_results",
    )(*main)
    result = list(result)
    result[1] = result[1][0]
    result[5] = jnp.transpose(result[5])
    result[6] = jnp.transpose(result[6], (0, 2, 1))
    result[9] = jnp.transpose(result[9], (0, 1, 3, 2))
    return tuple(result)


def solution(mesh):
    radices = radices_of(mesh.shape["dp"])
    in_specs = (
        P(("dp", "mp"), None),
        P(),
        P(),
        P(None, "mp"),
        P(None, None, "mp"),
        P("mp", None),
        P(),
        P(None, None, None, "mp"),
        P(None, "mp", None),
        P(),
        P(None, None, "mp"),
        P(None, "mp"),
        P(None, "mp", None),
        P(),
        P(),
        P(),
        P(("dp", "mp")),
        P(("dp", "mp"), None),
        P(("dp", "mp"), None),
    )
    out_specs = (
        P(("dp", "mp"), None),
        P(),
        P(("dp", "mp"), None),
        P(),
        P(),
        P(None, "mp"),
        P(None, None, "mp"),
        P("mp", None),
        P(),
        P(None, None, None, "mp"),
        P(None, "mp", None),
        P(),
        P(None, None, "mp"),
        P(None, "mp"),
        P(None, "mp", None),
        P(),
        P(),
        P(),
    )
    return jax.shard_map(
        functools.partial(on_device, radices),
        mesh=mesh,
        in_specs=in_specs,
        out_specs=out_specs,
        check_vma=False,
    )
```

```python
import functools
import math

import jax
import jax.numpy as jnp
from jax import lax
from jax.experimental import pallas as pl
from jax.experimental.pallas import tpu as pltpu
from jax.sharding import PartitionSpec as P

HD = 16
LAT = 16
SEQ_LEN = 256
SPAN = 16
JOINTS = 8
HEADS = 8
D = 128
FF = 512
AC = 128
LAYERS = 2

F32 = jnp.float32
BF = jnp.bfloat16
MESH = pl.DeviceIdType.MESH
epsilon = 1e-05
highest = lax.Precision.HIGHEST

CHUNKS = (512, 256, 512, 256, 384)


def nn(left, right):
    return jnp.dot(left, right, preferred_element_type=F32)


def nt(left, right):
    return lax.dot_general(left, right, (((1,), (1,)), ((), ())), preferred_element_type=F32)


def tn(left, right):
    return lax.dot_general(left, right, (((0,), (0,)), ((), ())), preferred_element_type=F32)


def iota(shape, axis):
    return lax.broadcasted_iota(jnp.int32, shape, axis)


def radices_of(count):
    found = []
    while count > 1:
        radix = 8 if count % 8 == 0 else 4 if count % 4 == 0 else 2
        found.append(radix)
        count //= radix
    return found


def flip(digit, offset):
    flipped = digit
    for bit in (1, 2, 4):
        if offset & bit:
            flipped = flipped + bit - 2 * bit * ((digit // bit) % 2)
    return flipped


def far_first(radix):
    return sorted(range(1, radix), key=lambda offset: -bin(offset).count("1"))


def norm_rows(values_in, gain_vec):
    mean_rows = jnp.mean(values_in, axis=-1, keepdims=True)
    centred = values_in - mean_rows
    variance = jnp.mean(centred * centred, axis=-1, keepdims=True)
    inv_rows = lax.rsqrt(variance + epsilon)
    unit_rows = centred * inv_rows
    return unit_rows * gain_vec, unit_rows, inv_rows


def norm_back(upstream, unit_rows, inv_rows, gain_vec):
    scaled = upstream * gain_vec
    inner = (
        scaled
        - jnp.mean(scaled, axis=-1, keepdims=True)
        - unit_rows * jnp.mean(scaled * unit_rows, axis=-1, keepdims=True)
    )
    return inv_rows * inner


def split_rows(values_in):
    first = values_in.astype(BF).astype(F32)
    rest = values_in - first
    second = rest.astype(BF).astype(F32)
    return jnp.concatenate([first, second, rest - second], axis=0).astype(BF)


def main_kernel(
    radices,
    tokens_h,
    stem_norm_h,
    stem_latent_h,
    stem_wq_h,
    stem_wkv_h,
    stem_wo_h,
    norm_attn_h,
    w_qkv_h,
    w_out_h,
    norm_mlp_h,
    w_up_h,
    b_up_h,
    w_down_h,
    b_down_h,
    w_act_h,
    b_act_h,
    span_len_h,
    joint_mask_h,
    targets_h,
    *refs,
):
    count = 18
    results, staged = refs[:count], refs[count : 2 * count]
    (
        actions,
        masked_loss,
        grad_tokens,
        d_stem_norm,
        d_latent_out,
        d_stem_wq,
        d_stem_wkv,
        d_stem_wo_out,
        d_norm_attn,
        d_qkv_out,
        d_out_out,
        d_norm_mlp,
        d_up_out,
        d_b_up,
        d_down_out,
        d_b_down,
        d_act_out,
        d_b_act,
    ) = staged
    (
        fin,
        x_v,
        stem_norm_v,
        stem_latent_v,
        wq_v,
        wkv_v,
        wo_v,
        norm_attn_v,
        wqkv_v,
        wout_v,
        norm_mlp_v,
        wup_v,
        bup_v,
        wdn_v,
        b_down_v,
        w_act_v,
        b_act_v,
        span_s,
        joint_v,
        targets_v,
        next_v,
        inv_v,
        e_v,
        ds_v,
        small_v,
        ent_v,
        ent_r,
        own,
        oth,
        rcv,
        snd,
        rs_r,
        part,
        full_r,
        in_sem,
        send_sem,
        recv_sem,
    ) = refs[2 * count :]
    dp, mp = lax.axis_index("dp"), lax.axis_index("mp")
    own_seqs = targets_h.shape[0]
    rows = own_seqs * LAT
    core = (dp, 1 - mp)
    digits = [(dp // math.prod(radices[:level])) % radix for level, radix in enumerate(radices)]

    places = {}

    def partner(level, offset):
        stride = math.prod(radices[:level])
        if (level, offset) not in places:
            digit = digits[level]
            places[level, offset] = (dp + (flip(digit, offset) - digit) * stride, mp)
        return places[level, offset]

    def apart(step, *given):
        pl.when(dp >= 0)(functools.partial(step, *given))

    barrier = pltpu.get_barrier_semaphore()
    greeted = [core]
    for level, radix in enumerate(radices):
        greeted += [partner(level, offset) for offset in range(1, radix)]
    for device in greeted:
        pl.semaphore_signal(barrier, inc=1, device_id=device, device_id_type=MESH)

    piece_of = {}
    for size in sorted({chunk // radices[0] for chunk in CHUNKS}):
        piece_of[size] = [
            pl.multiple_of(flip(digits[0], offset) * size, size) for offset in range(radices[0])
        ]
    recv_slots = [0]
    leaving = {}

    def left(send_slot):
        if send_slot in leaving:
            leaving.pop(send_slot)()

    def group(copies, extent, send_slot):
        left(send_slot)
        recv_slot = recv_slots[0]
        recv_slots[0] += 1

        def copy(src, dst, device):
            return pltpu.make_async_remote_copy(
                src_ref=src,
                dst_ref=dst,
                send_sem=send_sem.at[send_slot],
                recv_sem=recv_sem.at[recv_slot],
                device_id=device,
                device_id_type=MESH,
            )

        for src, dst, device in copies:
            copy(src, dst, device).start()
        leaving[send_slot] = lambda: copy(extent(), extent(), core).wait_send()
        return lambda: copy(extent(), extent(), core).wait_recv()

    local = {}
    pairs = (
        ("tokens", tokens_h, x_v),
        ("stem_norm", stem_norm_h, stem_norm_v),
        ("stem_latent", stem_latent_h, stem_latent_v),
        ("wq", stem_wq_h, wq_v),
        ("wkv", stem_wkv_h, wkv_v),
        ("wo", stem_wo_h, wo_v),
        ("wqkv", w_qkv_h, wqkv_v),
        ("wout", w_out_h, wout_v),
        ("wup", w_up_h, wup_v),
        ("wdn", w_down_h, wdn_v),
        ("norm_attn", norm_attn_h, norm_attn_v),
        ("norm_mlp", norm_mlp_h, norm_mlp_v),
        ("bup", b_up_h, bup_v),
        ("b_down", b_down_h, b_down_v),
        ("w_act", w_act_h, w_act_v),
        ("b_act", b_act_h, b_act_v),
        ("span", span_len_h, span_s),
        ("joint", joint_mask_h, joint_v),
        ("targets", targets_h, targets_v),
    )
    halves = ("wq", "wkv", "wo", "wqkv", "wout", "wup", "wdn", "bup")

    def load(place, name, src, dst):
        here = dst.at[0] if name in halves else dst
        return pltpu.make_async_copy(src, here, in_sem.at[place])

    for place, (name, src, dst) in enumerate(pairs):
        local[name] = functools.partial(load, place, name, src, dst)
        local[name]().start()

    head_mask = (
        (iota((HEADS, D, D), 2) // HD == iota((HEADS, D, D), 0)).astype(F32).astype(BF)
    )
    row_mask = (iota((HEADS, D, D), 1) // HD == iota((HEADS, D, D), 0)).astype(F32).astype(BF)
    diag_heads = (iota((D, D), 0) // LAT == iota((D, D), 1) // HD).astype(F32)
    block_add = jnp.where(iota((rows, rows), 0) // LAT == iota((rows, rows), 1) // LAT, 0.0, -1e30)
    mean_mat = jnp.full((D, D), 1.0 / D, BF)
    mean_twice = jnp.full((2 * D, D), 1.0 / D, BF)

    gathered = {}

    ent_slot = len(halves)
    ent_first = [1 + sum(radices[:level]) - level for level in range(len(radices))]

    def entries_step(level):
        pending.pop()()
        if level == 0:
            total = ent_v[0] + ent_r[0]
        else:
            first = ent_first[level - 1]
            total = tree(ent_v[level], [ent_r[first + at] for at in range(radices[level - 1] - 1)])
        if level == len(radices):
            return total
        ent_v[level + 1] = total
        first, others = ent_first[level], radices[level] - 1
        copies = [
            (ent_v.at[level + 1], ent_r.at[first + at], partner(level, at + 1))
            for at in range(others)
        ]
        pending.append(group(copies, lambda: ent_r.at[pl.ds(first, others)], ent_slot))
        return None

    def tree(mine, others):
        terms = [mine] + list(others)
        while len(terms) > 1:
            terms = [terms[at] + terms[at + 1] for at in range(0, len(terms), 2)]
        return terms[0]

    def wait_for(*names):
        for name in names:
            local[name]().wait()

    def wait_gathered(*names):
        for name in names:
            gathered[name]()

    def meet():
        pl.semaphore_wait(barrier, len(greeted))
        for name, src, dst in pairs:
            if name in halves:
                copies = [(src, dst.at[1], core)]
                extent = functools.partial(dst.at.__getitem__, 1)
                gathered[name] = group(copies, extent, halves.index(name))

    apart(meet)

    apart(wait_for, "span", "joint")
    spans = jnp.zeros((own_seqs, AC), jnp.int32)
    for seq in range(own_seqs):
        spans = jnp.where(iota((own_seqs, AC), 0) == seq, span_s[seq], spans)
    joints = (joint_v[...] > 0).astype(F32).astype(BF)
    spread = (iota((JOINTS, AC), 1) % JOINTS == iota((JOINTS, AC), 0)).astype(F32).astype(BF)
    valid = jnp.where(iota((own_seqs, AC), 1) // JOINTS < spans, nn(joints, spread), 0.0)
    ent_v[0] = jnp.broadcast_to(jnp.sum(valid, axis=0, keepdims=True), (8, AC))
    pending = []

    def entries_begin():
        copies = [(ent_v.at[0], ent_r.at[0], core)]
        pending.append(group(copies, lambda: ent_r.at[0], ent_slot))

    apart(entries_begin)

    apart(wait_for, "tokens", "stem_norm")
    stem_gain = stem_norm_v[...].astype(F32).reshape(1, D)
    half = own_seqs * SEQ_LEN // 2
    for start in (0, half):
        at = pl.ds(start, half)
        raw = x_v[at, :]
        centred = raw.astype(F32) - nn(raw, mean_mat)
        square = centred * centred
        upper = square.astype(BF)
        lower = (square - upper.astype(F32)).astype(BF)
        inv = lax.rsqrt(nn(jnp.concatenate([upper, lower], axis=1), mean_twice) + epsilon)
        unit = centred * inv
        inv_v[at, :] = inv
        next_v[at, 0:D] = (unit * stem_gain).astype(BF)
        next_v[at, D : 2 * D] = jnp.ones((half, D), BF)

    def both(ref, *index):
        return jnp.concatenate([ref[(0,) + index], ref[(1,) + index]], axis=0)

    def heads_below(matrix):
        return (matrix[None] * head_mask).reshape(HEADS * D, D)

    def heads_beside(matrix):
        return jnp.concatenate([matrix * row_mask[head] for head in range(HEADS)], axis=1)

    def lanes_beside(cube):
        return jnp.concatenate([cube[head] for head in range(HEADS)], axis=1)

    apart(wait_for, "stem_latent", "wq", "wkv")
    apart(wait_for, "wo")
    apart(wait_gathered, "wq", "wkv", "wo")
    latent = stem_latent_v[...]
    wq_t = both(wq_v)
    wk_t, wv_t = both(wkv_v, 0), both(wkv_v, 1)
    stem_q = nt(latent, wq_t).astype(BF).astype(F32) * HD ** (-0.5)
    q_diag = (jnp.concatenate([stem_q] * HEADS, axis=0) * diag_heads).astype(BF)
    fold = nn(q_diag, wk_t)
    fold_b = fold.astype(BF)
    apart(entries_step, 0)
    seq_rows = [pl.ds(seq * SEQ_LEN, SEQ_LEN) for seq in range(own_seqs)]
    scores = [nt(fold_b, next_v[at, 0:D]) for at in seq_rows]
    apart_wo = both(wo_v)
    wv_cols = wv_t.T
    stem_mats = nn(heads_below(wv_cols), apart_wo).astype(BF)
    mixed, shares = [], []
    for seq, at in enumerate(seq_rows):
        tops = jnp.max(scores[seq], axis=1, keepdims=True)
        probs = jnp.exp(scores[seq] - tops).astype(BF)
        e_v[:, seq * SEQ_LEN : (seq + 1) * SEQ_LEN] = probs
        both_sums = nn(probs, next_v[at, :])
        share = 1.0 / both_sums[:, D:]
        shares.append(share)
        mixed.append((both_sums[:, :D] * share).astype(BF))

    def by_head(head):
        return jnp.concatenate([part[head * LAT : (head + 1) * LAT] for part in mixed], axis=0)

    mixed_heads = [by_head(head) for head in range(HEADS)]
    latent_f = latent.astype(F32)
    hidden = jnp.concatenate([latent_f] * own_seqs, axis=0) + nn(
        jnp.concatenate(mixed_heads, axis=1), stem_mats
    )
    stem_wo = apart_wo

    def stem_heads_out():
        below = nt(jnp.concatenate(mixed_heads, axis=0), wv_t).reshape(HEADS, rows, D)
        return jnp.sum(below * head_mask.astype(F32), axis=0).astype(BF)


    apart(wait_for, "norm_attn", "norm_mlp", "b_down", "w_act", "b_act", "targets")
    apart(wait_for, "wqkv", "wout", "wup", "wdn", "bup")
    apart(wait_gathered, "wqkv", "wout", "wup", "wdn", "bup")
    gain_attn = norm_attn_v[...].astype(F32)
    gain_mlp = norm_mlp_v[...].astype(F32)
    down_bias = b_down_v[...].astype(F32)
    up_bias = jnp.concatenate([bup_v[0], bup_v[1]], axis=1).astype(F32)

    def row_blocks_beside(matrix):
        return jnp.concatenate([matrix[head * D : (head + 1) * D] for head in range(HEADS)], axis=1)

    def lane_blocks_below(matrix):
        return jnp.concatenate(
            [matrix[:, head * D : (head + 1) * D] for head in range(HEADS)], axis=0
        )

    def trunk_forward(residual, layer):
        gain_a, gain_m = gain_attn[layer : layer + 1], gain_mlp[layer : layer + 1]
        qkv = jnp.concatenate([both(wqkv_v, layer, part_at) for part_at in range(3)], axis=0)
        out_mat = both(wout_v, layer)
        out_mats = nn(heads_below(out_mat.T), qkv[2 * D :]).astype(BF)
        up_mat = jnp.concatenate([wup_v[0, layer], wup_v[1, layer]], axis=1)
        down_mat = both(wdn_v, layer)
        normed, unit_a, inv_a = norm_rows(residual, gain_a)
        rows_a = normed.astype(BF)
        flat = nt(rows_a, qkv).astype(BF)
        queries = flat[:, :D] * jnp.asarray(HD ** (-0.5), BF)
        keys = flat[:, D : 2 * D]
        scores = nt(heads_below(keys), queries).reshape(HEADS, rows, rows) + block_add[None]
        moved_t = row_blocks_beside(nt(out_mats, rows_a).astype(BF))
        exped = jnp.exp(scores - jnp.max(scores, axis=1, keepdims=True))
        probs = exped / jnp.sum(exped, axis=1, keepdims=True)
        probs_b = probs.astype(BF)
        probs_flat = probs_b.reshape(HEADS * rows, rows)
        middle = residual + nn(moved_t, probs_flat).T
        keys_t = nt(qkv[D : 2 * D], rows_a).astype(BF) * jnp.asarray(HD ** (-0.5), BF)
        values_t = nt(qkv[2 * D :], rows_a).astype(BF)
        normed_m, unit_m, inv_m = norm_rows(middle, gain_m)
        rows_m = normed_m.astype(BF)
        up_rows = nn(rows_m, up_mat) + up_bias[layer : layer + 1]
        attended_t = nn(heads_beside(values_t), probs_flat).astype(BF)
        moved = lane_blocks_below(nt(rows_a, out_mats).astype(BF))
        cdf = 0.5 + 0.5 * lax.erf(up_rows * (0.5**0.5))
        slope = cdf + up_rows * (jnp.exp(-0.5 * up_rows * up_rows) * 0.3989422804014327)
        hidden_act = (up_rows * cdf).astype(BF)
        output = middle + nn(hidden_act, down_mat) + down_bias[layer : layer + 1]
        saved = dict(
            gain_a=gain_a, gain_m=gain_m, qkv=qkv, out_mat=out_mat, up_mat=up_mat,
            down_mat=down_mat, unit_a=unit_a, inv_a=inv_a, rows_a=rows_a, queries=queries,
            keys_t=keys_t, moved=moved, probs=probs, probs_b=probs_b, attended_t=attended_t,
            unit_m=unit_m, inv_m=inv_m, rows_m=rows_m, slope=slope, hidden_act=hidden_act,
        )
        return output, saved

    kept = []
    for layer in range(LAYERS):
        hidden, saved = trunk_forward(hidden, layer)
        kept.append(saved)
        if layer == 0:
            stem_out = stem_heads_out()

    pooled = jnp.sum(hidden.reshape(own_seqs, LAT, D), axis=1)
    act_mat = w_act_v[...]

    def summed3(stacked):
        return stacked[0:own_seqs] + stacked[own_seqs : 2 * own_seqs] + stacked[2 * own_seqs :]

    pred = summed3(nn(split_rows(pooled), act_mat)) + b_act_v[...].astype(F32).reshape(1, AC)
    errors = pred - targets_v[...]
    squares = jnp.sum(valid * errors * errors, axis=0, keepdims=True)
    d_pred = valid * errors
    actions[...] = valid * pred

    def act_grad():
        top, rest = pooled.astype(BF), d_pred.astype(BF)
        left = jnp.concatenate([top.astype(F32), pooled - top.astype(F32), top.astype(F32)], axis=0)
        right = jnp.concatenate(
            [rest.astype(F32), rest.astype(F32), d_pred - rest.astype(F32)], axis=0
        )
        return tn(left.astype(BF), right.astype(BF))

    d_pooled = summed3(nt(split_rows(d_pred), act_mat))
    upstream = jnp.broadcast_to(d_pooled[:, None, :], (own_seqs, LAT, D)).reshape(rows, D)

    first_row = [sum(CHUNKS[:chunk]) for chunk in range(len(CHUNKS))]
    first_piece = [begin // radices[0] for begin in first_row]
    live = {}

    def put(chunk, offset, mine, others):
        at = pl.ds(first_row[chunk] + offset, mine.shape[0])
        own[at, :] = mine.astype(BF)
        oth[at, :] = others.astype(BF)

    def core_send(chunk):
        at = pl.ds(first_row[chunk], CHUNKS[chunk])
        live[chunk] = group([(oth.at[at], rcv.at[at], core)], lambda: rcv.at[at], chunk)

    def received(chunk):
        live.pop(chunk)()

    def scatter(chunk):
        received(chunk)
        at = pl.ds(first_row[chunk], CHUNKS[chunk])
        snd[at, :] = (own[at, :].astype(F32) + rcv[at, :].astype(F32)).astype(BF)
        size = CHUNKS[chunk] // radices[0]
        here = pl.ds(first_piece[chunk], size)
        copies = [
            (
                snd.at[at].at[pl.ds(piece_of[size][offset], size)],
                rs_r.at[offset - 1, here],
                partner(0, offset),
            )
            for offset in far_first(radices[0])
        ]
        live[chunk] = group(copies, lambda: rs_r.at[pl.ds(0, radices[0] - 1), here], chunk)

    def share_on(chunk, level):
        received(chunk)
        size = CHUNKS[chunk] // radices[0]
        here = pl.ds(first_piece[chunk], size)
        if level == 1:
            whole = snd.at[pl.ds(first_row[chunk], CHUNKS[chunk])]
            mine = whole[pl.ds(piece_of[size][0], size), :].astype(F32)
            got = [rs_r[at, here, :].astype(F32) for at in range(radices[0] - 1)]
        else:
            mine = part[level - 2, here, :].astype(F32)
            got = [full_r[level - 2, at, here, :].astype(F32) for at in range(radices[level - 1] - 1)]
        total = tree(mine, got).astype(BF)
        if level < len(radices):
            part[level - 1, here, :] = total
            others = radices[level] - 1
            copies = [
                (part.at[level - 1, here], full_r.at[level - 1, at, here], partner(level, at + 1))
                for at in range(others)
            ]
            live[chunk] = group(
                copies, lambda: full_r.at[level - 1, pl.ds(0, others), here], chunk
            )
            return
        mine_at = pl.ds(piece_of[size][0], size)
        done = fin.at[pl.ds(first_row[chunk], CHUNKS[chunk])]
        done[mine_at, :] = total
        copies = [
            (done.at[mine_at], done.at[mine_at], partner(0, offset))
            for offset in far_first(radices[0])
        ]
        rest = pl.ds(first_row[chunk], (radices[0] - 1) * size)
        live[chunk] = group(copies, lambda: fin.at[rest], chunk)

    last = len(radices)

    def back_mlp(upstream, layer, chunk):
        kv = kept[layer]
        grad_top = upstream.astype(BF)
        small_v[16 + 5 + layer : 16 + 6 + layer, :] = jnp.sum(
            grad_top.astype(F32), axis=0, keepdims=True
        )
        d_hidden = nt(grad_top, kv["down_mat"])
        d_upper = (kv["slope"] * d_hidden).astype(BF)
        d_rows = nt(d_upper, kv["up_mat"])
        d_middle = upstream + norm_back(d_rows, kv["unit_m"], kv["inv_m"], kv["gain_m"])
        small_v[16 + 3 + layer : 16 + 4 + layer, :] = jnp.sum(
            d_rows * kv["unit_m"], axis=0, keepdims=True
        )
        d_bias = jnp.sum(d_upper.astype(F32), axis=0, keepdims=True)
        for block in range(4):
            row = 32 + 4 * layer + block
            small_v[row : row + 1, :] = d_bias[:, block * D : (block + 1) * D]
        d_down = tn(kv["hidden_act"], grad_top)
        d_up = tn(kv["rows_m"], d_upper)
        put(chunk, 0, d_up[:, 0:128], d_up[:, 256:384])
        put(chunk, 128, d_up[:, 128:256], d_up[:, 384:512])
        put(chunk, 256, d_down[0:256], d_down[256:512])
        return d_middle

    def back_attn(d_middle, layer, chunk):
        kv = kept[layer]
        grad_attn = d_middle.astype(BF)
        d_probs = nt(kv["moved"], grad_attn).reshape(HEADS, rows, rows)
        d_mixed = nt(grad_attn, kv["out_mat"]).astype(BF)
        probs = kv["probs"]
        weighted = probs * d_probs
        inner = jnp.sum(weighted, axis=1, keepdims=True)
        d_scores = (weighted - probs * inner).astype(BF)
        d_values = nn(lanes_beside(kv["probs_b"]), heads_below(d_mixed)).astype(BF)
        d_q_t = nn(heads_beside(kv["keys_t"]), d_scores.reshape(HEADS * rows, rows))
        d_keys = nn(lanes_beside(d_scores), heads_below(kv["queries"])).astype(BF)
        grads = jnp.concatenate([d_q_t.T.astype(BF), d_keys, d_values], axis=1)
        d_rows = nn(grads, kv["qkv"])
        small_v[16 + 1 + layer : 16 + 2 + layer, :] = jnp.sum(
            d_rows * kv["unit_a"], axis=0, keepdims=True
        )
        d_input = d_middle + norm_back(d_rows, kv["unit_a"], kv["inv_a"], kv["gain_a"])
        d_out = nn(kv["attended_t"], grad_attn)
        d_qkv = tn(grads, kv["rows_a"])
        for place in range(3):
            begin = place * D
            put(chunk, place * 64, d_qkv[begin : begin + 64], d_qkv[begin + 64 : begin + 128])
        put(chunk, 192, d_out[0:64], d_out[64:128])
        return d_input

    upstream = back_mlp(upstream, 1, 0)
    apart(core_send, 0)
    apart(entries_step, 1)
    upstream = back_attn(upstream, 1, 1)
    apart(core_send, 1)
    upstream = back_mlp(upstream, 0, 2)
    apart(core_send, 2)
    apart(scatter, 0)
    upstream = back_attn(upstream, 0, 3)
    apart(core_send, 3)
    apart(scatter, 1)
    apart(scatter, 2)

    grad_stem = upstream.astype(BF)
    back_flat = nt(grad_stem, stem_mats)
    back_v = [
        jnp.concatenate(
            [
                back_flat[seq * LAT : (seq + 1) * LAT, head * D : (head + 1) * D]
                for head in range(HEADS)
            ],
            axis=0,
        )
        for seq in range(own_seqs)
    ]
    gain_sum = jnp.zeros((D, D), F32)
    folds_v, d_all = [], []
    for seq, at in enumerate(seq_rows):
        gain_sum += back_v[seq] * mixed[seq].astype(F32)
        folds_v.append((back_v[seq] * shares[seq]).astype(BF))
        d_all.append(nt(folds_v[seq], next_v[at, 0:D]))
    for seq in range(own_seqs):
        lanes = slice(seq * SEQ_LEN, (seq + 1) * SEQ_LEN)
        probs = e_v[:, lanes].astype(F32)
        weighted = probs * d_all[seq]
        inner = jnp.sum(weighted, axis=1, keepdims=True) * shares[seq][:, 0:1]
        ds_v[:, lanes] = (weighted - probs * inner).astype(BF)
    d_out_t = nt(stem_wo, grad_stem).astype(BF)
    d_stem_wo = tn(stem_out, grad_stem)
    put(4, 0, d_stem_wo[0:64], d_stem_wo[64:128])
    d_wv = nn(heads_beside(d_out_t), jnp.concatenate(mixed_heads, axis=0))
    put(4, 64, d_wv[0:64], d_wv[64:128])
    d_act = act_grad()
    put(4, 128, d_act, d_act)
    d_fold = nn(ds_v[...], next_v[:, 0:D])
    apart(scatter, 3)

    d_fold_b = d_fold.astype(BF)
    d_wk = nn(q_diag.astype(F32).T.astype(BF), d_fold_b)
    d_q = nt(d_fold_b, wk_t) * diag_heads
    d_q = jnp.sum(d_q.reshape(HEADS, LAT, D), axis=0) * HD ** (-0.5)
    d_latent = jnp.sum(upstream.reshape(own_seqs, LAT, D), axis=0) + nn(d_q.astype(BF), wq_t)
    small_v[0:16, :] = d_latent
    gain_rows = jnp.sum(gain_sum + d_fold * fold, axis=0, keepdims=True)
    small_v[16:17, :] = gain_rows / stem_gain
    small_v[23:24, :] = jnp.sum(d_pred, axis=0, keepdims=True)
    small_v[24:25, :] = squares
    for layer in range(LAYERS):
        small_v[25 + 2 * layer : 27 + 2 * layer, :] = small_v[32 + 4 * layer : 34 + 4 * layer, :]
    small_v[29:32, :] = jnp.zeros((3, D), F32)
    shared = small_v[0:32, :]
    d_q_other = jnp.concatenate([d_q[:, 64:], d_q[:, :64]], axis=1)
    put(4, 256, d_wk[0:64], d_wk[64:128])
    put(4, 320, d_q, d_q_other)
    put(4, 336, shared, shared)
    for layer in range(LAYERS):
        small_v[25 + 2 * layer : 27 + 2 * layer, :] = small_v[34 + 4 * layer : 36 + 4 * layer, :]
    oth[first_row[4] + 352 : first_row[4] + 368, :] = small_v[16:32, :].astype(BF)
    own[first_row[4] + 368 : first_row[4] + 384, :] = jnp.zeros((16, D), BF)
    oth[first_row[4] + 368 : first_row[4] + 384, :] = jnp.zeros((16, D), BF)
    apart(core_send, 4)

    def hand_over(*places):
        for place in places:
            pltpu.make_async_copy(staged[place], results[place], in_sem.at[place]).start()

    fold_g = (fold * stem_gain).astype(BF)
    fold_side = jnp.concatenate([fold_g, nn(fold_g, mean_mat).astype(BF)], axis=1)

    def token_grads(seq):
        at = pl.ds(seq * SEQ_LEN, SEQ_LEN)
        lanes = slice(seq * SEQ_LEN, (seq + 1) * SEQ_LEN)
        left = jnp.concatenate([ds_v[:, lanes], e_v[:, lanes]], axis=0)
        value_g = (folds_v[seq].astype(F32) * stem_gain).astype(BF)
        value_side = jnp.concatenate([value_g, nn(value_g, mean_mat).astype(BF)], axis=1)
        both_grads = tn(left, jnp.concatenate([fold_side, value_side], axis=0))
        scaled = both_grads[:, :D]
        raw = x_v[at, :]
        unit = (raw.astype(F32) - nn(raw, mean_mat)) * inv_v[at, :]
        slope_mean = nn((scaled * unit).astype(BF), mean_mat)
        grad_tokens[at, :] = inv_v[at, :] * (scaled - both_grads[:, D:] - unit * slope_mean)

    order = (
        (2, scatter, 4),
        (3, share_on, 0, 1),
        (5, share_on, 1, 1),
        (8, share_on, 2, 1),
        (8, share_on, 3, 1),
        (8, share_on, 4, 1),
        (8, share_on, 0, 2),
    )
    for seq in range(own_seqs):
        for place, *step in order:
            if place == seq:
                apart(*step)
        token_grads(seq)
    for place, *step in order:
        if place >= own_seqs:
            apart(*step)

    for level in range(2, last):
        apart(entries_step, level)
    entries = jnp.sum(entries_step(last)[0:1], axis=1, keepdims=True)
    total_seqs = own_seqs * lax.axis_size("dp") * lax.axis_size("mp")
    factor = total_seqs * AC / entries
    grad_tokens[...] = grad_tokens[...] * factor

    apart(hand_over, 0, 2)
    for chunk, level in ((1, 2), (2, 2), (3, 2), (4, 2)):
        apart(share_on, chunk, level)
    for level in range(3, last + 1):
        for chunk in range(len(CHUNKS)):
            apart(share_on, chunk, level)

    def whole(chunk, begin, count):
        at = first_row[chunk] + begin
        return fin[at : at + count, :].astype(F32) * factor

    def finish(chunk):
        received(chunk)
        if chunk in (0, 2):
            layer = 1 if chunk == 0 else 0
            d_up_out[layer, :, 0:128] = whole(chunk, 0, 128)
            d_up_out[layer, :, 128:256] = whole(chunk, 128, 128)
            d_down_out[layer] = whole(chunk, 256, 256)
            if chunk == 2:
                hand_over(12, 14)
        if chunk in (1, 3):
            layer = 1 if chunk == 1 else 0
            for place in range(3):
                d_qkv_out[layer, place] = whole(chunk, 64 * place, 64)
            d_out_out[layer] = whole(chunk, 192, 64)
            if chunk == 3:
                hand_over(9, 10)
        if chunk == 4:
            d_stem_wo_out[...] = whole(4, 0, 64)
            d_stem_wkv[1] = whole(4, 64, 64)
            d_act_out[...] = whole(4, 128, 128)
            d_stem_wkv[0] = whole(4, 256, 64)
            d_latent_out[...] = whole(4, 336, 16)
            at = first_row[4]
            d_stem_wq[...] = tn(fin[at + 320 : at + 336, 0:64], latent) * factor
            rest = whole(4, 352, 16)
            d_stem_norm[...] = rest[0:1].reshape(D)
            d_norm_attn[...] = rest[1:3]
            d_norm_mlp[...] = rest[3:5]
            d_b_down[...] = rest[5:7]
            d_b_act[...] = rest[7:8].reshape(D)
            for layer in range(LAYERS):
                d_b_up[layer : layer + 1, 0:128] = rest[9 + 2 * layer : 10 + 2 * layer]
                d_b_up[layer : layer + 1, 128:256] = rest[10 + 2 * layer : 11 + 2 * layer]
            summed = jnp.sum(fin[at + 352 : at + 368, :].astype(F32)[8:9], axis=1, keepdims=True)
            masked_loss[...] = jnp.broadcast_to(summed / entries, (1, D)).reshape(D)
            hand_over(1, 3, 4, 5, 6, 7, 8, 11, 13, 15, 16, 17)

    def all_left(*slots):
        for send_slot in slots:
            left(send_slot)

    apart(all_left, *range(len(CHUNKS), len(halves) + 1))
    for chunk in range(len(CHUNKS)):
        apart(finish, chunk)
        apart(all_left, chunk)
    for place in range(count):
        pltpu.make_async_copy(staged[place], results[place], in_sem.at[place]).wait()


def copy_kernel(*refs):
    count = len(refs) // 2
    sem = refs[-1]
    copies = [
        pltpu.make_async_copy(refs[at], refs[count + at], sem.at[at]) for at in range(count)
    ]
    for copy in copies:
        copy.start()
    for copy in copies:
        copy.wait()


def on_device(radices, *args):
    (
        tokens,
        stem_norm,
        stem_latent,
        stem_wq,
        stem_wkv,
        stem_wo,
        norm_attn,
        w_qkv,
        w_out,
        norm_mlp,
        w_up,
        b_up,
        w_down,
        b_down,
        w_act,
        b_act,
        span_len,
        joint_mask,
        targets,
    ) = args
    own_seqs = targets.shape[0]
    count = own_seqs * SEQ_LEN
    rows = own_seqs * LAT
    last = len(radices)
    spread = sum(radices) - last
    vmem = pl.BlockSpec(memory_space=pltpu.VMEM)
    hbm = pl.BlockSpec(memory_space=pltpu.HBM)
    total_rows = sum(CHUNKS)
    wide = max(radices) - 1

    def summing(count_rows, dtype):
        pieces = count_rows // radices[0]
        return [
            *[pltpu.VMEM((count_rows, D), dtype)] * 4,
            pltpu.VMEM((wide, pieces, D), dtype),
            pltpu.VMEM((last - 1, pieces, D), dtype),
            pltpu.VMEM((last - 1, wide, pieces, D), dtype),
        ]

    n_recv = 8 + (1 + last) + len(CHUNKS) * (2 + last)
    shape = jax.ShapeDtypeStruct
    outs = [
        shape((own_seqs, AC), F32),
        shape((D,), F32),
        shape((count, D), F32),
        shape((D,), F32),
        shape((LAT, D), F32),
        shape((64, D), F32),
        shape((2, 64, D), F32),
        shape((64, D), F32),
        shape((LAYERS, D), F32),
        shape((LAYERS, 3, 64, D), F32),
        shape((LAYERS, 64, D), F32),
        shape((LAYERS, D), F32),
        shape((LAYERS, D, FF // 2), F32),
        shape((LAYERS, FF // 2), F32),
        shape((LAYERS, FF // 2, D), F32),
        shape((LAYERS, D), F32),
        shape((D, AC), F32),
        shape((AC,), F32),
    ]
    main = pl.pallas_call(
        functools.partial(main_kernel, radices),
        out_shape=outs,
        in_specs=[hbm] * len(args),
        out_specs=[pl.BlockSpec(memory_space=pl.ANY)] * len(outs),
        scratch_shapes=[
            *[pltpu.VMEM(out.shape, out.dtype) for out in outs],
            pltpu.VMEM((sum(CHUNKS), D), BF),
            pltpu.VMEM((count, D), BF),
            pltpu.VMEM((D,), BF),
            pltpu.VMEM((LAT, D), BF),
            pltpu.VMEM((2, 64, D), BF),
            pltpu.VMEM((2, 2, 64, D), BF),
            pltpu.VMEM((2, 64, D), BF),
            pltpu.VMEM((LAYERS, D), BF),
            pltpu.VMEM((2, LAYERS, 3, 64, D), BF),
            pltpu.VMEM((2, LAYERS, 64, D), BF),
            pltpu.VMEM((LAYERS, D), BF),
            pltpu.VMEM((2, LAYERS, D, FF // 2), BF),
            pltpu.VMEM((2, LAYERS, FF // 2), BF),
            pltpu.VMEM((2, LAYERS, FF // 2, D), BF),
            pltpu.VMEM((LAYERS, D), BF),
            pltpu.VMEM((D, AC), BF),
            pltpu.VMEM((AC,), BF),
            pltpu.SMEM((own_seqs,), jnp.int32),
            pltpu.VMEM((own_seqs, JOINTS), jnp.int32),
            pltpu.VMEM((own_seqs, AC), F32),
            pltpu.VMEM((count, 2 * D), BF),
            pltpu.VMEM((count, D), F32),
            pltpu.VMEM((D, count), BF),
            pltpu.VMEM((D, count), BF),
            pltpu.VMEM((40, D), F32),
            pltpu.VMEM((1 + last, 8, AC), F32),
            pltpu.VMEM((1 + spread, 8, AC), F32),
            *summing(total_rows, BF),
            pltpu.SemaphoreType.DMA((len(args),)),
            pltpu.SemaphoreType.DMA((9,)),
            pltpu.SemaphoreType.DMA((n_recv,)),
        ],
        compiler_params=pltpu.CompilerParams(
            collective_id=0, has_side_effects=True, vmem_limit_bytes=40 * 2**20
        ),
        name="stem_trunk_head",
    )(
        *[
            pltpu.with_memory_space_constraint(arg, pltpu.HBM)
            for arg in (
                tokens,
                stem_norm,
                stem_latent,
                jnp.transpose(stem_wq),
                jnp.transpose(stem_wkv, (0, 2, 1)),
                stem_wo,
                norm_attn,
                jnp.transpose(w_qkv, (0, 1, 3, 2)),
                w_out,
                norm_mlp,
                w_up,
                b_up,
                w_down,
                b_down,
                w_act,
                b_act,
                span_len,
                joint_mask,
                targets,
            )
        ]
    )
    result = pl.pallas_call(
        copy_kernel,
        out_shape=[pltpu.HBM(out.shape, out.dtype) for out in outs],
        in_specs=[vmem] * len(outs),
        out_specs=[hbm] * len(outs),
        scratch_shapes=[pltpu.SemaphoreType.DMA((len(outs),))],
        compiler_params=pltpu.CompilerParams(vmem_limit_bytes=8 * 2**20),
        name="copy_results",
    )(*main)
    result = list(result)
    result[1] = result[1][0]
    result[5] = jnp.transpose(result[5])
    result[6] = jnp.transpose(result[6], (0, 2, 1))
    result[9] = jnp.transpose(result[9], (0, 1, 3, 2))
    return tuple(result)


def solution(mesh):
    radices = radices_of(mesh.shape["dp"])
    in_specs = (
        P(("dp", "mp"), None),
        P(),
        P(),
        P(None, "mp"),
        P(None, None, "mp"),
        P("mp", None),
        P(),
        P(None, None, None, "mp"),
        P(None, "mp", None),
        P(),
        P(None, None, "mp"),
        P(None, "mp"),
        P(None, "mp", None),
        P(),
        P(),
        P(),
        P(("dp", "mp")),
        P(("dp", "mp"), None),
        P(("dp", "mp"), None),
    )
    out_specs = (
        P(("dp", "mp"), None),
        P(),
        P(("dp", "mp"), None),
        P(),
        P(),
        P(None, "mp"),
        P(None, None, "mp"),
        P("mp", None),
        P(),
        P(None, None, None, "mp"),
        P(None, "mp", None),
        P(),
        P(None, None, "mp"),
        P(None, "mp"),
        P(None, "mp", None),
        P(),
        P(),
        P(),
    )
    return jax.shard_map(
        functools.partial(on_device, radices),
        mesh=mesh,
        in_specs=in_specs,
        out_specs=out_specs,
        check_vma=False,
    )
```

```python
import functools
import math

import jax
import jax.numpy as jnp
from jax import lax
from jax.experimental import pallas as pl
from jax.experimental.pallas import tpu as pltpu
from jax.sharding import PartitionSpec as P

HD = 16
LAT = 16
SEQ_LEN = 256
SPAN = 16
JOINTS = 8
HEADS = 8
D = 128
FF = 512
AC = 128
LAYERS = 2

F32 = jnp.float32
BF = jnp.bfloat16
MESH = pl.DeviceIdType.MESH
epsilon = 1e-05
highest = lax.Precision.HIGHEST

CHUNKS = (256, 256, 384, 512, 384, 128)
DIRECT = (0, 5)


def nn(left, right):
    return jnp.dot(left, right, preferred_element_type=F32)


def nt(left, right):
    return lax.dot_general(left, right, (((1,), (1,)), ((), ())), preferred_element_type=F32)


def tn(left, right):
    return lax.dot_general(left, right, (((0,), (0,)), ((), ())), preferred_element_type=F32)


def iota(shape, axis):
    return lax.broadcasted_iota(jnp.int32, shape, axis)


def radices_of(count):
    found = []
    while count > 1:
        radix = 8 if count % 8 == 0 else 4 if count % 4 == 0 else 2
        found.append(radix)
        count //= radix
    return found


def flip(digit, offset):
    flipped = digit
    for bit in (1, 2, 4):
        if offset & bit:
            flipped = flipped + bit - 2 * bit * ((digit // bit) % 2)
    return flipped


def far_first(radix):
    return sorted(range(1, radix), key=lambda offset: -bin(offset).count("1"))


def norm_rows(values_in, gain_vec):
    mean_rows = jnp.mean(values_in, axis=-1, keepdims=True)
    centred = values_in - mean_rows
    variance = jnp.mean(centred * centred, axis=-1, keepdims=True)
    inv_rows = lax.rsqrt(variance + epsilon)
    unit_rows = centred * inv_rows
    return unit_rows * gain_vec, unit_rows, inv_rows


def norm_back(upstream, unit_rows, inv_rows, gain_vec):
    scaled = upstream * gain_vec
    inner = (
        scaled
        - jnp.mean(scaled, axis=-1, keepdims=True)
        - unit_rows * jnp.mean(scaled * unit_rows, axis=-1, keepdims=True)
    )
    return inv_rows * inner


def split_rows(values_in):
    first = values_in.astype(BF).astype(F32)
    rest = values_in - first
    second = rest.astype(BF).astype(F32)
    return jnp.concatenate([first, second, rest - second], axis=0).astype(BF)


def main_kernel(
    radices,
    tokens_h,
    stem_norm_h,
    stem_latent_h,
    stem_wq_h,
    stem_wkv_h,
    stem_wo_h,
    norm_attn_h,
    w_qkv_h,
    w_out_h,
    norm_mlp_h,
    w_up_h,
    b_up_h,
    w_down_h,
    b_down_h,
    w_act_h,
    b_act_h,
    span_len_h,
    joint_mask_h,
    targets_h,
    *refs,
):
    count = 18
    (
        actions,
        masked_loss,
        grad_tokens,
        d_stem_norm,
        d_latent_out,
        d_stem_wq,
        d_stem_wkv,
        d_stem_wo_out,
        d_norm_attn,
        d_qkv_out,
        d_out_out,
        d_norm_mlp,
        d_up_out,
        d_b_up,
        d_down_out,
        d_b_down,
        d_act_out,
        d_b_act,
    ) = refs[:count]
    (
        fin,
        x_v,
        stem_norm_v,
        stem_latent_v,
        wq_v,
        wkv_v,
        wo_v,
        norm_attn_v,
        wqkv_v,
        wout_v,
        norm_mlp_v,
        wup_v,
        bup_v,
        wdn_v,
        b_down_v,
        w_act_v,
        b_act_v,
        span_s,
        joint_v,
        targets_v,
        next_v,
        inv_v,
        e_v,
        ds_v,
        small_v,
        ent_v,
        ent_r,
        own,
        oth,
        rcv,
        snd,
        rs_r,
        direct_r,
        part,
        full_r,
        in_sem,
        send_sem,
        recv_sem,
    ) = refs[count:]
    dp, mp = lax.axis_index("dp"), lax.axis_index("mp")
    own_seqs = targets_h.shape[0]
    rows = own_seqs * LAT
    core = (dp, 1 - mp)
    digits = [(dp // math.prod(radices[:level])) % radix for level, radix in enumerate(radices)]

    places = {}

    def partner(level, offset):
        stride = math.prod(radices[:level])
        if (level, offset) not in places:
            digit = digits[level]
            places[level, offset] = (dp + (flip(digit, offset) - digit) * stride, mp)
        return places[level, offset]

    def apart(step, *given):
        pl.when(dp >= 0)(functools.partial(step, *given))

    barrier = pltpu.get_barrier_semaphore()
    greeted = [core]
    for offset in range(1, radices[0]):
        greeted.append((partner(0, offset)[0], 1 - mp))
    for level, radix in enumerate(radices):
        greeted += [partner(level, offset) for offset in range(1, radix)]
    for device in greeted:
        pl.semaphore_signal(barrier, inc=1, device_id=device, device_id_type=MESH)

    piece_of = {}
    for size in sorted({chunk // radices[0] for chunk in CHUNKS}):
        piece_of[size] = [
            pl.multiple_of(flip(digits[0], offset) * size, size) for offset in range(radices[0])
        ]
    recv_slots = [0]
    leaving = {}

    def left(send_slot):
        if send_slot in leaving:
            leaving.pop(send_slot)()

    def group(copies, extent, send_slot):
        left(send_slot)
        recv_slot = recv_slots[0]
        recv_slots[0] += 1

        def copy(src, dst, device):
            return pltpu.make_async_remote_copy(
                src_ref=src,
                dst_ref=dst,
                send_sem=send_sem.at[send_slot],
                recv_sem=recv_sem.at[recv_slot],
                device_id=device,
                device_id_type=MESH,
            )

        for src, dst, device in copies:
            copy(src, dst, device).start()
        leaving[send_slot] = lambda: copy(extent(), extent(), core).wait_send()
        return lambda: copy(extent(), extent(), core).wait_recv()

    local = {}
    pairs = (
        ("tokens", tokens_h, x_v),
        ("stem_norm", stem_norm_h, stem_norm_v),
        ("stem_latent", stem_latent_h, stem_latent_v),
        ("wq", stem_wq_h, wq_v),
        ("wkv", stem_wkv_h, wkv_v),
        ("wo", stem_wo_h, wo_v),
        ("wqkv", w_qkv_h, wqkv_v),
        ("wout", w_out_h, wout_v),
        ("wup", w_up_h, wup_v),
        ("wdn", w_down_h, wdn_v),
        ("norm_attn", norm_attn_h, norm_attn_v),
        ("norm_mlp", norm_mlp_h, norm_mlp_v),
        ("bup", b_up_h, bup_v),
        ("b_down", b_down_h, b_down_v),
        ("w_act", w_act_h, w_act_v),
        ("b_act", b_act_h, b_act_v),
        ("span", span_len_h, span_s),
        ("joint", joint_mask_h, joint_v),
        ("targets", targets_h, targets_v),
    )
    halves = ("wq", "wkv", "wo", "wqkv", "wout", "wup", "wdn", "bup")

    def load(place, name, src, dst):
        here = dst.at[0] if name in halves else dst
        return pltpu.make_async_copy(src, here, in_sem.at[place])

    for place, (name, src, dst) in enumerate(pairs):
        local[name] = functools.partial(load, place, name, src, dst)
        local[name]().start()

    head_mask = (
        (iota((HEADS, D, D), 2) // HD == iota((HEADS, D, D), 0)).astype(F32).astype(BF)
    )
    row_mask = (iota((HEADS, D, D), 1) // HD == iota((HEADS, D, D), 0)).astype(F32).astype(BF)
    diag_heads = (iota((D, D), 0) // LAT == iota((D, D), 1) // HD).astype(F32)
    block_add = jnp.where(iota((rows, rows), 0) // LAT == iota((rows, rows), 1) // LAT, 0.0, -1e30)
    mean_mat = jnp.full((D, D), 1.0 / D, BF)
    mean_twice = jnp.full((2 * D, D), 1.0 / D, BF)

    gathered = {}

    ent_slot = len(halves)
    ent_first = [1 + sum(radices[:level]) - level for level in range(len(radices))]

    def entries_step(level):
        pending.pop()()
        if level == 0:
            total = ent_v[0] + ent_r[0]
        else:
            first = ent_first[level - 1]
            total = tree(ent_v[level], [ent_r[first + at] for at in range(radices[level - 1] - 1)])
        if level == len(radices):
            return total
        ent_v[level + 1] = total
        first, others = ent_first[level], radices[level] - 1
        copies = [
            (ent_v.at[level + 1], ent_r.at[first + at], partner(level, at + 1))
            for at in range(others)
        ]
        pending.append(group(copies, lambda: ent_r.at[pl.ds(first, others)], ent_slot))
        return None

    def tree(mine, others):
        terms = [mine] + list(others)
        while len(terms) > 1:
            terms = [terms[at] + terms[at + 1] for at in range(0, len(terms), 2)]
        return terms[0]

    def wait_for(*names):
        for name in names:
            local[name]().wait()

    def wait_gathered(*names):
        for name in names:
            gathered[name]()

    def meet():
        pl.semaphore_wait(barrier, len(greeted))
        for name, src, dst in pairs:
            if name in halves:
                copies = [(src, dst.at[1], core)]
                extent = functools.partial(dst.at.__getitem__, 1)
                gathered[name] = group(copies, extent, halves.index(name))

    apart(meet)

    apart(wait_for, "span", "joint")
    spans = jnp.zeros((own_seqs, AC), jnp.int32)
    for seq in range(own_seqs):
        spans = jnp.where(iota((own_seqs, AC), 0) == seq, span_s[seq], spans)
    joints = (joint_v[...] > 0).astype(F32).astype(BF)
    spread = (iota((JOINTS, AC), 1) % JOINTS == iota((JOINTS, AC), 0)).astype(F32).astype(BF)
    valid = jnp.where(iota((own_seqs, AC), 1) // JOINTS < spans, nn(joints, spread), 0.0)
    ent_v[0] = jnp.broadcast_to(jnp.sum(valid, axis=0, keepdims=True), (8, AC))
    pending = []

    def entries_begin():
        copies = [(ent_v.at[0], ent_r.at[0], core)]
        pending.append(group(copies, lambda: ent_r.at[0], ent_slot))

    apart(entries_begin)

    apart(wait_for, "tokens", "stem_norm")
    stem_gain = stem_norm_v[...].astype(F32).reshape(1, D)
    half = own_seqs * SEQ_LEN // 2
    for start in (0, half):
        at = pl.ds(start, half)
        raw = x_v[at, :]
        centred = raw.astype(F32) - nn(raw, mean_mat)
        square = centred * centred
        upper = square.astype(BF)
        lower = (square - upper.astype(F32)).astype(BF)
        inv = lax.rsqrt(nn(jnp.concatenate([upper, lower], axis=1), mean_twice) + epsilon)
        unit = centred * inv
        inv_v[at, :] = inv
        next_v[at, 0:D] = (unit * stem_gain).astype(BF)
        next_v[at, D : 2 * D] = jnp.ones((half, D), BF)

    def both(ref, *index):
        return jnp.concatenate([ref[(0,) + index], ref[(1,) + index]], axis=0)

    def heads_below(matrix):
        return (matrix[None] * head_mask).reshape(HEADS * D, D)

    def heads_beside(matrix):
        return jnp.concatenate([matrix * row_mask[head] for head in range(HEADS)], axis=1)

    def lanes_beside(cube):
        return jnp.concatenate([cube[head] for head in range(HEADS)], axis=1)

    apart(wait_for, "stem_latent", "wq", "wkv")
    apart(wait_for, "wo")
    apart(wait_gathered, "wq", "wkv", "wo")
    latent = stem_latent_v[...]
    wq_t = both(wq_v)
    wk_t, wv_t = both(wkv_v, 0), both(wkv_v, 1)
    stem_q = nt(latent, wq_t).astype(BF).astype(F32) * HD ** (-0.5)
    q_diag = (jnp.concatenate([stem_q] * HEADS, axis=0) * diag_heads).astype(BF)
    fold = nn(q_diag, wk_t)
    fold_b = fold.astype(BF)
    apart(entries_step, 0)
    seq_rows = [pl.ds(seq * SEQ_LEN, SEQ_LEN) for seq in range(own_seqs)]
    scores = [nt(fold_b, next_v[at, 0:D]) for at in seq_rows]
    apart_wo = both(wo_v)
    wv_cols = wv_t.T
    stem_mats = nn(heads_below(wv_cols), apart_wo).astype(BF)
    mixed, shares = [], []
    for seq, at in enumerate(seq_rows):
        tops = jnp.max(scores[seq], axis=1, keepdims=True)
        probs = jnp.exp(scores[seq] - tops).astype(BF)
        e_v[:, seq * SEQ_LEN : (seq + 1) * SEQ_LEN] = probs
        both_sums = nn(probs, next_v[at, :])
        share = 1.0 / both_sums[:, D:]
        shares.append(share)
        mixed.append((both_sums[:, :D] * share).astype(BF))

    def by_head(head):
        return jnp.concatenate([part[head * LAT : (head + 1) * LAT] for part in mixed], axis=0)

    mixed_heads = [by_head(head) for head in range(HEADS)]
    latent_f = latent.astype(F32)
    hidden = jnp.concatenate([latent_f] * own_seqs, axis=0) + nn(
        jnp.concatenate(mixed_heads, axis=1), stem_mats
    )
    stem_wo = apart_wo

    def stem_heads_out():
        below = nt(jnp.concatenate(mixed_heads, axis=0), wv_t).reshape(HEADS, rows, D)
        return jnp.sum(below * head_mask.astype(F32), axis=0).astype(BF)


    apart(wait_for, "norm_attn", "norm_mlp", "b_down", "w_act", "b_act", "targets")
    apart(wait_for, "wqkv", "wout", "wup", "wdn", "bup")
    apart(wait_gathered, "wqkv", "wout", "wup", "wdn", "bup")
    gain_attn = norm_attn_v[...].astype(F32)
    gain_mlp = norm_mlp_v[...].astype(F32)
    down_bias = b_down_v[...].astype(F32)
    up_bias = jnp.concatenate([bup_v[0], bup_v[1]], axis=1).astype(F32)

    def row_blocks_beside(matrix):
        return jnp.concatenate([matrix[head * D : (head + 1) * D] for head in range(HEADS)], axis=1)

    def lane_blocks_below(matrix):
        return jnp.concatenate(
            [matrix[:, head * D : (head + 1) * D] for head in range(HEADS)], axis=0
        )

    def trunk_forward(residual, layer):
        gain_a, gain_m = gain_attn[layer : layer + 1], gain_mlp[layer : layer + 1]
        qkv = jnp.concatenate([both(wqkv_v, layer, part_at) for part_at in range(3)], axis=0)
        out_mat = both(wout_v, layer)
        out_mats = nn(heads_below(out_mat.T), qkv[2 * D :]).astype(BF)
        up_mat = jnp.concatenate([wup_v[0, layer], wup_v[1, layer]], axis=1)
        down_mat = both(wdn_v, layer)
        normed, unit_a, inv_a = norm_rows(residual, gain_a)
        rows_a = normed.astype(BF)
        flat = nt(rows_a, qkv).astype(BF)
        queries = flat[:, :D] * jnp.asarray(HD ** (-0.5), BF)
        keys = flat[:, D : 2 * D]
        scores = nt(heads_below(keys), queries).reshape(HEADS, rows, rows) + block_add[None]
        moved_t = row_blocks_beside(nt(out_mats, rows_a).astype(BF))
        exped = jnp.exp(scores - jnp.max(scores, axis=1, keepdims=True))
        probs = exped / jnp.sum(exped, axis=1, keepdims=True)
        probs_b = probs.astype(BF)
        probs_flat = probs_b.reshape(HEADS * rows, rows)
        middle = residual + nn(moved_t, probs_flat).T
        keys_t = nt(qkv[D : 2 * D], rows_a).astype(BF) * jnp.asarray(HD ** (-0.5), BF)
        values_t = nt(qkv[2 * D :], rows_a).astype(BF)
        normed_m, unit_m, inv_m = norm_rows(middle, gain_m)
        rows_m = normed_m.astype(BF)
        up_rows = nn(rows_m, up_mat) + up_bias[layer : layer + 1]
        attended_t = nn(heads_beside(values_t), probs_flat).astype(BF)
        moved = lane_blocks_below(nt(rows_a, out_mats).astype(BF))
        cdf = 0.5 + 0.5 * lax.erf(up_rows * (0.5**0.5))
        slope = cdf + up_rows * (jnp.exp(-0.5 * up_rows * up_rows) * 0.3989422804014327)
        hidden_act = (up_rows * cdf).astype(BF)
        output = middle + nn(hidden_act, down_mat) + down_bias[layer : layer + 1]
        saved = dict(
            gain_a=gain_a, gain_m=gain_m, qkv=qkv, out_mat=out_mat, up_mat=up_mat,
            down_mat=down_mat, unit_a=unit_a, inv_a=inv_a, rows_a=rows_a, queries=queries,
            keys_t=keys_t, moved=moved, probs=probs, probs_b=probs_b, attended_t=attended_t,
            unit_m=unit_m, inv_m=inv_m, rows_m=rows_m, slope=slope, hidden_act=hidden_act,
        )
        return output, saved

    kept = []
    for layer in range(LAYERS):
        hidden, saved = trunk_forward(hidden, layer)
        kept.append(saved)
        if layer == 0:
            stem_out = stem_heads_out()

    pooled = jnp.sum(hidden.reshape(own_seqs, LAT, D), axis=1)
    act_mat = w_act_v[...]

    def summed3(stacked):
        return stacked[0:own_seqs] + stacked[own_seqs : 2 * own_seqs] + stacked[2 * own_seqs :]

    pred = summed3(nn(split_rows(pooled), act_mat)) + b_act_v[...].astype(F32).reshape(1, AC)
    errors = pred - targets_v[...]
    squares = jnp.sum(valid * errors * errors, axis=0, keepdims=True)
    d_pred = valid * errors
    actions[...] = valid * pred

    def act_grad():
        top, rest = pooled.astype(BF), d_pred.astype(BF)
        left = jnp.concatenate([top.astype(F32), pooled - top.astype(F32), top.astype(F32)], axis=0)
        right = jnp.concatenate(
            [rest.astype(F32), rest.astype(F32), d_pred - rest.astype(F32)], axis=0
        )
        return tn(left.astype(BF), right.astype(BF))

    d_pooled = summed3(nt(split_rows(d_pred), act_mat))
    upstream = jnp.broadcast_to(d_pooled[:, None, :], (own_seqs, LAT, D)).reshape(rows, D)

    first_row = [sum(CHUNKS[:chunk]) for chunk in range(len(CHUNKS))]
    first_piece = [begin // radices[0] for begin in first_row]
    live = {}
    first_direct = {
        chunk: sum(CHUNKS[before] for before in DIRECT[:at]) // radices[0]
        for at, chunk in enumerate(DIRECT)
    }

    def put(chunk, offset, mine, others):
        at = pl.ds(first_row[chunk] + offset, mine.shape[0])
        own[at, :] = mine.astype(BF)
        oth[at, :] = others.astype(BF)

    def core_send(chunk):
        at = pl.ds(first_row[chunk], CHUNKS[chunk])
        live[chunk] = group([(oth.at[at], rcv.at[at], core)], lambda: rcv.at[at], chunk)

    def scatter_both(chunk):
        size = CHUNKS[chunk] // radices[0]
        at = pl.ds(first_row[chunk], CHUNKS[chunk])
        here = pl.ds(first_direct[chunk], size)
        copies = []
        for offset in far_first(radices[0]) + [0]:
            piece = pl.ds(piece_of[size][offset], size)
            if offset:
                device, across = partner(0, offset), (partner(0, offset)[0], 1 - mp)
                copies.append((own.at[at].at[piece], direct_r.at[offset - 1, here], device))
            else:
                across = core
            dst = direct_r.at[radices[0] - 1 + offset, here]
            copies.append((oth.at[at].at[piece], dst, across))
        live[chunk] = group(copies, lambda: direct_r.at[:, here], chunk)

    def received(chunk):
        live.pop(chunk)()

    def scatter(chunk):
        received(chunk)
        at = pl.ds(first_row[chunk], CHUNKS[chunk])
        snd[at, :] = (own[at, :].astype(F32) + rcv[at, :].astype(F32)).astype(BF)
        size = CHUNKS[chunk] // radices[0]
        here = pl.ds(first_piece[chunk], size)
        copies = [
            (
                snd.at[at].at[pl.ds(piece_of[size][offset], size)],
                rs_r.at[offset - 1, here],
                partner(0, offset),
            )
            for offset in far_first(radices[0])
        ]
        live[chunk] = group(copies, lambda: rs_r.at[pl.ds(0, radices[0] - 1), here], chunk)

    def share_on(chunk, level):
        received(chunk)
        size = CHUNKS[chunk] // radices[0]
        here = pl.ds(first_piece[chunk], size)
        if level == 1 and chunk in DIRECT:
            whole = own.at[pl.ds(first_row[chunk], CHUNKS[chunk])]
            mine = whole[pl.ds(piece_of[size][0], size), :].astype(F32)
            there = pl.ds(first_direct[chunk], size)
            got = [direct_r[at, there, :].astype(F32) for at in range(2 * radices[0] - 1)]
        elif level == 1:
            whole = snd.at[pl.ds(first_row[chunk], CHUNKS[chunk])]
            mine = whole[pl.ds(piece_of[size][0], size), :].astype(F32)
            got = [rs_r[at, here, :].astype(F32) for at in range(radices[0] - 1)]
        else:
            mine = part[level - 2, here, :].astype(F32)
            got = [full_r[level - 2, at, here, :].astype(F32) for at in range(radices[level - 1] - 1)]
        total = tree(mine, got).astype(BF)
        if level < len(radices):
            part[level - 1, here, :] = total
            others = radices[level] - 1
            copies = [
                (part.at[level - 1, here], full_r.at[level - 1, at, here], partner(level, at + 1))
                for at in range(others)
            ]
            live[chunk] = group(
                copies, lambda: full_r.at[level - 1, pl.ds(0, others), here], chunk
            )
            return
        mine_at = pl.ds(piece_of[size][0], size)
        done = fin.at[pl.ds(first_row[chunk], CHUNKS[chunk])]
        done[mine_at, :] = total
        copies = [
            (done.at[mine_at], done.at[mine_at], partner(0, offset))
            for offset in far_first(radices[0])
        ]
        rest = pl.ds(first_row[chunk], (radices[0] - 1) * size)
        live[chunk] = group(copies, lambda: fin.at[rest], chunk)

    last = len(radices)

    def back_mlp(upstream, layer, chunk):
        kv = kept[layer]
        grad_top = upstream.astype(BF)
        small_v[16 + 5 + layer : 16 + 6 + layer, :] = jnp.sum(
            grad_top.astype(F32), axis=0, keepdims=True
        )
        d_hidden = nt(grad_top, kv["down_mat"])
        d_upper = (kv["slope"] * d_hidden).astype(BF)
        d_rows = nt(d_upper, kv["up_mat"])
        d_middle = upstream + norm_back(d_rows, kv["unit_m"], kv["inv_m"], kv["gain_m"])
        small_v[16 + 3 + layer : 16 + 4 + layer, :] = jnp.sum(
            d_rows * kv["unit_m"], axis=0, keepdims=True
        )
        d_bias = jnp.sum(d_upper.astype(F32), axis=0, keepdims=True)
        for block in range(4):
            row = 32 + 4 * layer + block
            small_v[row : row + 1, :] = d_bias[:, block * D : (block + 1) * D]
        d_down = tn(kv["hidden_act"], grad_top)
        d_up = tn(kv["rows_m"], d_upper)
        put(chunk, 0, d_up[:, 0:128], d_up[:, 256:384])
        put(chunk, 128, d_up[:, 128:256], d_up[:, 384:512])
        if layer == 1:
            put(chunk + 1, 0, d_down[0:256], d_down[256:512])
        else:
            put(chunk, 256, d_down[0:256], d_down[256:512])
        return d_middle

    def back_attn(d_middle, layer, chunk):
        kv = kept[layer]
        grad_attn = d_middle.astype(BF)
        d_probs = nt(kv["moved"], grad_attn).reshape(HEADS, rows, rows)
        d_mixed = nt(grad_attn, kv["out_mat"]).astype(BF)
        probs = kv["probs"]
        weighted = probs * d_probs
        inner = jnp.sum(weighted, axis=1, keepdims=True)
        d_scores = (weighted - probs * inner).astype(BF)
        d_values = nn(lanes_beside(kv["probs_b"]), heads_below(d_mixed)).astype(BF)
        d_q_t = nn(heads_beside(kv["keys_t"]), d_scores.reshape(HEADS * rows, rows))
        d_keys = nn(lanes_beside(d_scores), heads_below(kv["queries"])).astype(BF)
        grads = jnp.concatenate([d_q_t.T.astype(BF), d_keys, d_values], axis=1)
        d_rows = nn(grads, kv["qkv"])
        small_v[16 + 1 + layer : 16 + 2 + layer, :] = jnp.sum(
            d_rows * kv["unit_a"], axis=0, keepdims=True
        )
        d_input = d_middle + norm_back(d_rows, kv["unit_a"], kv["inv_a"], kv["gain_a"])
        d_out = nn(kv["attended_t"], grad_attn)
        d_qkv = tn(grads, kv["rows_a"])
        for place in range(3):
            begin = place * D
            put(chunk, place * 64, d_qkv[begin : begin + 64], d_qkv[begin + 64 : begin + 128])
        put(chunk, 192, d_out[0:64], d_out[64:128])
        return d_input

    upstream = back_mlp(upstream, 1, 0)
    apart(scatter_both, 0)
    apart(core_send, 1)
    apart(entries_step, 1)
    upstream = back_attn(upstream, 1, 2)
    d_act = act_grad()
    put(2, 256, d_act, d_act)
    apart(core_send, 2)
    upstream = back_mlp(upstream, 0, 3)
    apart(core_send, 3)
    apart(scatter, 1)
    upstream = back_attn(upstream, 0, 4)
    apart(scatter, 2)
    apart(scatter, 3)

    grad_stem = upstream.astype(BF)
    back_flat = nt(grad_stem, stem_mats)
    back_v = [
        jnp.concatenate(
            [
                back_flat[seq * LAT : (seq + 1) * LAT, head * D : (head + 1) * D]
                for head in range(HEADS)
            ],
            axis=0,
        )
        for seq in range(own_seqs)
    ]
    d_out_t = nt(stem_wo, grad_stem).astype(BF)
    d_stem_wo = tn(stem_out, grad_stem)
    put(4, 256, d_stem_wo[0:64], d_stem_wo[64:128])
    d_wv = nn(heads_beside(d_out_t), jnp.concatenate(mixed_heads, axis=0))
    put(4, 320, d_wv[0:64], d_wv[64:128])
    apart(core_send, 4)

    gain_sum = jnp.zeros((D, D), F32)
    folds_v, d_all = [], []
    for seq, at in enumerate(seq_rows):
        gain_sum += back_v[seq] * mixed[seq].astype(F32)
        folds_v.append((back_v[seq] * shares[seq]).astype(BF))
        d_all.append(nt(folds_v[seq], next_v[at, 0:D]))
    for seq in range(own_seqs):
        lanes = slice(seq * SEQ_LEN, (seq + 1) * SEQ_LEN)
        probs = e_v[:, lanes].astype(F32)
        weighted = probs * d_all[seq]
        inner = jnp.sum(weighted, axis=1, keepdims=True) * shares[seq][:, 0:1]
        ds_v[:, lanes] = (weighted - probs * inner).astype(BF)
    d_fold = nn(ds_v[...], next_v[:, 0:D])
    apart(scatter, 4)

    d_fold_b = d_fold.astype(BF)
    d_wk = nn(q_diag.astype(F32).T.astype(BF), d_fold_b)
    d_q = nt(d_fold_b, wk_t) * diag_heads
    d_q = jnp.sum(d_q.reshape(HEADS, LAT, D), axis=0) * HD ** (-0.5)
    d_latent = jnp.sum(upstream.reshape(own_seqs, LAT, D), axis=0) + nn(d_q.astype(BF), wq_t)
    small_v[0:16, :] = d_latent
    gain_rows = jnp.sum(gain_sum + d_fold * fold, axis=0, keepdims=True)
    small_v[16:17, :] = gain_rows / stem_gain
    small_v[23:24, :] = jnp.sum(d_pred, axis=0, keepdims=True)
    small_v[24:25, :] = squares
    for layer in range(LAYERS):
        small_v[25 + 2 * layer : 27 + 2 * layer, :] = small_v[32 + 4 * layer : 34 + 4 * layer, :]
    small_v[29:32, :] = jnp.zeros((3, D), F32)
    shared = small_v[0:32, :]
    d_q_other = jnp.concatenate([d_q[:, 64:], d_q[:, :64]], axis=1)
    put(5, 0, d_wk[0:64], d_wk[64:128])
    put(5, 64, d_q, d_q_other)
    put(5, 80, shared, shared)
    for layer in range(LAYERS):
        small_v[25 + 2 * layer : 27 + 2 * layer, :] = small_v[34 + 4 * layer : 36 + 4 * layer, :]
    oth[first_row[5] + 96 : first_row[5] + 112, :] = small_v[16:32, :].astype(BF)
    own[first_row[5] + 112 : first_row[5] + 128, :] = jnp.zeros((16, D), BF)
    oth[first_row[5] + 112 : first_row[5] + 128, :] = jnp.zeros((16, D), BF)
    apart(scatter_both, 5)

    fold_g = (fold * stem_gain).astype(BF)
    fold_side = jnp.concatenate([fold_g, nn(fold_g, mean_mat).astype(BF)], axis=1)

    def token_grads(seq):
        at = pl.ds(seq * SEQ_LEN, SEQ_LEN)
        lanes = slice(seq * SEQ_LEN, (seq + 1) * SEQ_LEN)
        left = jnp.concatenate([ds_v[:, lanes], e_v[:, lanes]], axis=0)
        value_g = (folds_v[seq].astype(F32) * stem_gain).astype(BF)
        value_side = jnp.concatenate([value_g, nn(value_g, mean_mat).astype(BF)], axis=1)
        both_grads = tn(left, jnp.concatenate([fold_side, value_side], axis=0))
        scaled = both_grads[:, :D]
        raw = x_v[at, :]
        unit = (raw.astype(F32) - nn(raw, mean_mat)) * inv_v[at, :]
        slope_mean = nn((scaled * unit).astype(BF), mean_mat)
        grad_tokens[at, :] = inv_v[at, :] * (scaled - both_grads[:, D:] - unit * slope_mean)

    order = (
        (1, share_on, 0, 1),
        (3, share_on, 1, 1),
        (5, share_on, 2, 1),
        (8, share_on, 3, 1),
        (8, share_on, 4, 1),
        (8, share_on, 0, 2),
        (8, share_on, 5, 1),
        (8, share_on, 1, 2),
    )
    for seq in range(own_seqs):
        for place, *step in order:
            if place == seq:
                apart(*step)
        token_grads(seq)
    for place, *step in order:
        if place >= own_seqs:
            apart(*step)

    for level in range(2, last):
        apart(entries_step, level)
    entries = jnp.sum(entries_step(last)[0:1], axis=1, keepdims=True)
    total_seqs = own_seqs * lax.axis_size("dp") * lax.axis_size("mp")
    factor = total_seqs * AC / entries
    grad_tokens[...] = grad_tokens[...] * factor

    for chunk, level in ((2, 2), (3, 2), (4, 2), (5, 2)):
        apart(share_on, chunk, level)
    for level in range(3, last + 1):
        for chunk in range(len(CHUNKS)):
            apart(share_on, chunk, level)

    def whole(chunk, begin, count):
        at = first_row[chunk] + begin
        return fin[at : at + count, :].astype(F32) * factor

    def finish(chunk):
        received(chunk)
        if chunk in (0, 3):
            layer = 1 if chunk == 0 else 0
            d_up_out[layer, :, 0:128] = whole(chunk, 0, 128)
            d_up_out[layer, :, 128:256] = whole(chunk, 128, 128)
        if chunk == 1:
            d_down_out[1] = whole(1, 0, 256)
        if chunk == 3:
            d_down_out[0] = whole(3, 256, 256)
        if chunk in (2, 4):
            layer = 1 if chunk == 2 else 0
            for place in range(3):
                d_qkv_out[layer, place] = whole(chunk, 64 * place, 64)
            d_out_out[layer] = whole(chunk, 192, 64)
        if chunk == 2:
            d_act_out[...] = whole(2, 256, 128)
        if chunk == 4:
            d_stem_wo_out[...] = whole(4, 256, 64)
            d_stem_wkv[1] = whole(4, 320, 64)
        if chunk == 5:
            d_stem_wkv[0] = whole(5, 0, 64)
            d_latent_out[...] = whole(5, 80, 16)
            at = first_row[5]
            d_stem_wq[...] = tn(fin[at + 64 : at + 80, 0:64], latent) * factor
            rest = whole(5, 96, 16)
            d_stem_norm[...] = rest[0:1].reshape(D)
            d_norm_attn[...] = rest[1:3]
            d_norm_mlp[...] = rest[3:5]
            d_b_down[...] = rest[5:7]
            d_b_act[...] = rest[7:8].reshape(D)
            for layer in range(LAYERS):
                d_b_up[layer : layer + 1, 0:128] = rest[9 + 2 * layer : 10 + 2 * layer]
                d_b_up[layer : layer + 1, 128:256] = rest[10 + 2 * layer : 11 + 2 * layer]
            summed = jnp.sum(fin[at + 96 : at + 112, :].astype(F32)[8:9], axis=1, keepdims=True)
            masked_loss[...] = jnp.broadcast_to(summed / entries, (1, D)).reshape(D)

    def all_left(*slots):
        for send_slot in slots:
            left(send_slot)

    apart(all_left, *range(len(CHUNKS), len(halves) + 1))
    for chunk in range(len(CHUNKS)):
        apart(finish, chunk)
        apart(all_left, chunk)


def copy_kernel(*refs):
    count = len(refs) // 2
    sem = refs[-1]
    copies = [
        pltpu.make_async_copy(refs[at], refs[count + at], sem.at[at]) for at in range(count)
    ]
    for copy in copies:
        copy.start()
    for copy in copies:
        copy.wait()


def on_device(radices, *args):
    (
        tokens,
        stem_norm,
        stem_latent,
        stem_wq,
        stem_wkv,
        stem_wo,
        norm_attn,
        w_qkv,
        w_out,
        norm_mlp,
        w_up,
        b_up,
        w_down,
        b_down,
        w_act,
        b_act,
        span_len,
        joint_mask,
        targets,
    ) = args
    own_seqs = targets.shape[0]
    count = own_seqs * SEQ_LEN
    rows = own_seqs * LAT
    last = len(radices)
    spread = sum(radices) - last
    vmem = pl.BlockSpec(memory_space=pltpu.VMEM)
    hbm = pl.BlockSpec(memory_space=pltpu.HBM)
    total_rows = sum(CHUNKS)
    wide = max(radices) - 1

    def summing(count_rows, dtype):
        pieces = count_rows // radices[0]
        direct_pieces = sum(CHUNKS[chunk] for chunk in DIRECT) // radices[0]
        return [
            *[pltpu.VMEM((count_rows, D), dtype)] * 4,
            pltpu.VMEM((wide, pieces, D), dtype),
            pltpu.VMEM((2 * radices[0] - 1, direct_pieces, D), dtype),
            pltpu.VMEM((last - 1, pieces, D), dtype),
            pltpu.VMEM((last - 1, wide, pieces, D), dtype),
        ]

    n_recv = 8 + (1 + last) + len(CHUNKS) * (2 + last)
    shape = jax.ShapeDtypeStruct
    outs = [
        shape((own_seqs, AC), F32),
        shape((D,), F32),
        shape((count, D), F32),
        shape((D,), F32),
        shape((LAT, D), F32),
        shape((64, D), F32),
        shape((2, 64, D), F32),
        shape((64, D), F32),
        shape((LAYERS, D), F32),
        shape((LAYERS, 3, 64, D), F32),
        shape((LAYERS, 64, D), F32),
        shape((LAYERS, D), F32),
        shape((LAYERS, D, FF // 2), F32),
        shape((LAYERS, FF // 2), F32),
        shape((LAYERS, FF // 2, D), F32),
        shape((LAYERS, D), F32),
        shape((D, AC), F32),
        shape((AC,), F32),
    ]
    main = pl.pallas_call(
        functools.partial(main_kernel, radices),
        out_shape=outs,
        in_specs=[hbm] * len(args),
        out_specs=[vmem] * len(outs),
        scratch_shapes=[
            pltpu.VMEM((sum(CHUNKS), D), BF),
            pltpu.VMEM((count, D), BF),
            pltpu.VMEM((D,), BF),
            pltpu.VMEM((LAT, D), BF),
            pltpu.VMEM((2, 64, D), BF),
            pltpu.VMEM((2, 2, 64, D), BF),
            pltpu.VMEM((2, 64, D), BF),
            pltpu.VMEM((LAYERS, D), BF),
            pltpu.VMEM((2, LAYERS, 3, 64, D), BF),
            pltpu.VMEM((2, LAYERS, 64, D), BF),
            pltpu.VMEM((LAYERS, D), BF),
            pltpu.VMEM((2, LAYERS, D, FF // 2), BF),
            pltpu.VMEM((2, LAYERS, FF // 2), BF),
            pltpu.VMEM((2, LAYERS, FF // 2, D), BF),
            pltpu.VMEM((LAYERS, D), BF),
            pltpu.VMEM((D, AC), BF),
            pltpu.VMEM((AC,), BF),
            pltpu.SMEM((own_seqs,), jnp.int32),
            pltpu.VMEM((own_seqs, JOINTS), jnp.int32),
            pltpu.VMEM((own_seqs, AC), F32),
            pltpu.VMEM((count, 2 * D), BF),
            pltpu.VMEM((count, D), F32),
            pltpu.VMEM((D, count), BF),
            pltpu.VMEM((D, count), BF),
            pltpu.VMEM((40, D), F32),
            pltpu.VMEM((1 + last, 8, AC), F32),
            pltpu.VMEM((1 + spread, 8, AC), F32),
            *summing(total_rows, BF),
            pltpu.SemaphoreType.DMA((len(args),)),
            pltpu.SemaphoreType.DMA((9,)),
            pltpu.SemaphoreType.DMA((n_recv,)),
        ],
        compiler_params=pltpu.CompilerParams(
            collective_id=0, has_side_effects=True, vmem_limit_bytes=40 * 2**20
        ),
        name="stem_trunk_head",
    )(
        *[
            pltpu.with_memory_space_constraint(arg, pltpu.HBM)
            for arg in (
                tokens,
                stem_norm,
                stem_latent,
                jnp.transpose(stem_wq),
                jnp.transpose(stem_wkv, (0, 2, 1)),
                stem_wo,
                norm_attn,
                jnp.transpose(w_qkv, (0, 1, 3, 2)),
                w_out,
                norm_mlp,
                w_up,
                b_up,
                w_down,
                b_down,
                w_act,
                b_act,
                span_len,
                joint_mask,
                targets,
            )
        ]
    )
    result = pl.pallas_call(
        copy_kernel,
        out_shape=[pltpu.HBM(out.shape, out.dtype) for out in outs],
        in_specs=[vmem] * len(outs),
        out_specs=[hbm] * len(outs),
        scratch_shapes=[pltpu.SemaphoreType.DMA((len(outs),))],
        compiler_params=pltpu.CompilerParams(vmem_limit_bytes=8 * 2**20),
        name="copy_results",
    )(*main)
    result = list(result)
    result[1] = result[1][0]
    result[5] = jnp.transpose(result[5])
    result[6] = jnp.transpose(result[6], (0, 2, 1))
    result[9] = jnp.transpose(result[9], (0, 1, 3, 2))
    return tuple(result)


def solution(mesh):
    radices = radices_of(mesh.shape["dp"])
    in_specs = (
        P(("dp", "mp"), None),
        P(),
        P(),
        P(None, "mp"),
        P(None, None, "mp"),
        P("mp", None),
        P(),
        P(None, None, None, "mp"),
        P(None, "mp", None),
        P(),
        P(None, None, "mp"),
        P(None, "mp"),
        P(None, "mp", None),
        P(),
        P(),
        P(),
        P(("dp", "mp")),
        P(("dp", "mp"), None),
        P(("dp", "mp"), None),
    )
    out_specs = (
        P(("dp", "mp"), None),
        P(),
        P(("dp", "mp"), None),
        P(),
        P(),
        P(None, "mp"),
        P(None, None, "mp"),
        P("mp", None),
        P(),
        P(None, None, None, "mp"),
        P(None, "mp", None),
        P(),
        P(None, None, "mp"),
        P(None, "mp"),
        P(None, "mp", None),
        P(),
        P(),
        P(),
    )
    return jax.shard_map(
        functools.partial(on_device, radices),
        mesh=mesh,
        in_specs=in_specs,
        out_specs=out_specs,
        check_vma=False,
    )
```

```python
import functools
import math

import jax
import jax.numpy as jnp
from jax import lax
from jax.experimental import pallas as pl
from jax.experimental.pallas import tpu as pltpu
from jax.sharding import PartitionSpec as P

HD = 16
LAT = 16
SEQ_LEN = 256
SPAN = 16
JOINTS = 8
HEADS = 8
D = 128
FF = 512
AC = 128
LAYERS = 2

F32 = jnp.float32
BF = jnp.bfloat16
MESH = pl.DeviceIdType.MESH
epsilon = 1e-05
highest = lax.Precision.HIGHEST

CHUNKS = (256, 256, 384, 512, 384, 128)
DIRECT = (0, 5)


def nn(left, right):
    return jnp.dot(left, right, preferred_element_type=F32)


def nt(left, right):
    return lax.dot_general(left, right, (((1,), (1,)), ((), ())), preferred_element_type=F32)


def tn(left, right):
    return lax.dot_general(left, right, (((0,), (0,)), ((), ())), preferred_element_type=F32)


def iota(shape, axis):
    return lax.broadcasted_iota(jnp.int32, shape, axis)


def radices_of(count):
    found = []
    while count > 1:
        radix = 8 if count % 8 == 0 else 4 if count % 4 == 0 else 2
        found.append(radix)
        count //= radix
    return found


def flip(digit, offset):
    flipped = digit
    for bit in (1, 2, 4):
        if offset & bit:
            flipped = flipped + bit - 2 * bit * ((digit // bit) % 2)
    return flipped


def far_first(radix):
    return sorted(range(1, radix), key=lambda offset: -bin(offset).count("1"))


def norm_rows(values_in, gain_vec):
    mean_rows = jnp.mean(values_in, axis=-1, keepdims=True)
    centred = values_in - mean_rows
    variance = jnp.mean(centred * centred, axis=-1, keepdims=True)
    inv_rows = lax.rsqrt(variance + epsilon)
    unit_rows = centred * inv_rows
    return unit_rows * gain_vec, unit_rows, inv_rows


def norm_back(upstream, unit_rows, inv_rows, gain_vec):
    scaled = upstream * gain_vec
    inner = (
        scaled
        - jnp.mean(scaled, axis=-1, keepdims=True)
        - unit_rows * jnp.mean(scaled * unit_rows, axis=-1, keepdims=True)
    )
    return inv_rows * inner


def split_rows(values_in):
    first = values_in.astype(BF).astype(F32)
    rest = values_in - first
    second = rest.astype(BF).astype(F32)
    return jnp.concatenate([first, second, rest - second], axis=0).astype(BF)


def main_kernel(
    radices,
    tokens_h,
    stem_norm_h,
    stem_latent_h,
    stem_wq_h,
    stem_wkv_h,
    stem_wo_h,
    norm_attn_h,
    w_qkv_h,
    w_out_h,
    norm_mlp_h,
    w_up_h,
    b_up_h,
    w_down_h,
    b_down_h,
    w_act_h,
    b_act_h,
    span_len_h,
    joint_mask_h,
    targets_h,
    *refs,
):
    count = 18
    (
        actions,
        masked_loss,
        grad_tokens,
        d_stem_norm,
        d_latent_out,
        d_stem_wq,
        d_stem_wkv,
        d_stem_wo_out,
        d_norm_attn,
        d_qkv_out,
        d_out_out,
        d_norm_mlp,
        d_up_out,
        d_b_up,
        d_down_out,
        d_b_down,
        d_act_out,
        d_b_act,
    ) = refs[:count]
    (
        fin,
        x_v,
        stem_norm_v,
        stem_latent_v,
        wq_v,
        wkv_v,
        wo_v,
        norm_attn_v,
        wqkv_v,
        wout_v,
        norm_mlp_v,
        wup_v,
        bup_v,
        wdn_v,
        b_down_v,
        w_act_v,
        b_act_v,
        span_s,
        joint_v,
        targets_v,
        next_v,
        inv_v,
        e_v,
        ds_v,
        small_v,
        ent_v,
        ent_r,
        own,
        oth,
        rcv,
        snd,
        rs_r,
        direct_r,
        part,
        full_r,
        in_sem,
        send_sem,
        recv_sem,
        meet_sem,
    ) = refs[count:]
    dp, mp = lax.axis_index("dp"), lax.axis_index("mp")
    own_seqs = targets_h.shape[0]
    rows = own_seqs * LAT
    core = (dp, 1 - mp)
    digits = [(dp // math.prod(radices[:level])) % radix for level, radix in enumerate(radices)]

    places = {}

    def partner(level, offset):
        stride = math.prod(radices[:level])
        if (level, offset) not in places:
            digit = digits[level]
            places[level, offset] = (dp + (flip(digit, offset) - digit) * stride, mp)
        return places[level, offset]

    def apart(step, *given):
        pl.when(dp >= 0)(functools.partial(step, *given))

    barrier = pltpu.get_barrier_semaphore()
    bits = [
        (level, bit) for level, radix in enumerate(radices) for bit in (1, 2, 4) if bit < radix
    ]
    greeted = [core] + [partner(level, bit) for level, bit in bits]
    passing = [core] + [partner(level, bit) for level, bit in bits if radices[level] > 2]
    for level, radix in enumerate(radices):
        for offset in range(1, radix):
            partner(level, offset)
    for device in greeted:
        pl.semaphore_signal(barrier, inc=1, device_id=device, device_id_type=MESH)

    piece_of = {}
    for size in sorted({chunk // radices[0] for chunk in CHUNKS}):
        piece_of[size] = [
            pl.multiple_of(flip(digits[0], offset) * size, size) for offset in range(radices[0])
        ]
    recv_slots = [0]
    leaving = {}

    def left(send_slot):
        if send_slot in leaving:
            leaving.pop(send_slot)()

    def group(copies, extent, send_slot):
        left(send_slot)
        recv_slot = recv_slots[0]
        recv_slots[0] += 1

        def copy(src, dst, device):
            return pltpu.make_async_remote_copy(
                src_ref=src,
                dst_ref=dst,
                send_sem=send_sem.at[send_slot],
                recv_sem=recv_sem.at[recv_slot],
                device_id=device,
                device_id_type=MESH,
            )

        for src, dst, device in copies:
            copy(src, dst, device).start()
        leaving[send_slot] = lambda: copy(extent(), extent(), core).wait_send()
        return lambda: copy(extent(), extent(), core).wait_recv()

    local = {}
    pairs = (
        ("tokens", tokens_h, x_v),
        ("stem_norm", stem_norm_h, stem_norm_v),
        ("stem_latent", stem_latent_h, stem_latent_v),
        ("wq", stem_wq_h, wq_v),
        ("wkv", stem_wkv_h, wkv_v),
        ("wo", stem_wo_h, wo_v),
        ("wqkv", w_qkv_h, wqkv_v),
        ("wout", w_out_h, wout_v),
        ("wup", w_up_h, wup_v),
        ("wdn", w_down_h, wdn_v),
        ("norm_attn", norm_attn_h, norm_attn_v),
        ("norm_mlp", norm_mlp_h, norm_mlp_v),
        ("bup", b_up_h, bup_v),
        ("b_down", b_down_h, b_down_v),
        ("w_act", w_act_h, w_act_v),
        ("b_act", b_act_h, b_act_v),
        ("span", span_len_h, span_s),
        ("joint", joint_mask_h, joint_v),
        ("targets", targets_h, targets_v),
    )
    halves = ("wq", "wkv", "wo", "wqkv", "wout", "wup", "wdn", "bup")

    def load(place, name, src, dst):
        here = dst.at[0] if name in halves else dst
        return pltpu.make_async_copy(src, here, in_sem.at[place])

    for place, (name, src, dst) in enumerate(pairs):
        local[name] = functools.partial(load, place, name, src, dst)
    at_once = ("tokens", "span", "joint", "stem_norm", "stem_latent", "wq", "wkv", "wo")
    for name in at_once:
        local[name]().start()

    head_mask = (
        (iota((HEADS, D, D), 2) // HD == iota((HEADS, D, D), 0)).astype(F32).astype(BF)
    )
    row_mask = (iota((HEADS, D, D), 1) // HD == iota((HEADS, D, D), 0)).astype(F32).astype(BF)
    diag_heads = (iota((D, D), 0) // LAT == iota((D, D), 1) // HD).astype(F32)
    block_add = jnp.where(iota((rows, rows), 0) // LAT == iota((rows, rows), 1) // LAT, 0.0, -1e30)
    mean_mat = jnp.full((D, D), 1.0 / D, BF)
    mean_twice = jnp.full((2 * D, D), 1.0 / D, BF)

    gathered = {}

    ent_slot = len(halves)
    ent_first = [1 + sum(radices[:level]) - level for level in range(len(radices))]

    def entries_step(level):
        pending.pop()()
        if level == 0:
            total = ent_v[0] + ent_r[0]
        else:
            first = ent_first[level - 1]
            total = tree(ent_v[level], [ent_r[first + at] for at in range(radices[level - 1] - 1)])
        if level == len(radices):
            return total
        ent_v[level + 1] = total
        first, others = ent_first[level], radices[level] - 1
        copies = [
            (ent_v.at[level + 1], ent_r.at[first + at], partner(level, at + 1))
            for at in range(others)
        ]
        pending.append(group(copies, lambda: ent_r.at[pl.ds(first, others)], ent_slot))
        return None

    def tree(mine, others):
        terms = [mine] + list(others)
        while len(terms) > 1:
            terms = [terms[at] + terms[at + 1] for at in range(0, len(terms), 2)]
        return terms[0]

    def wait_for(*names):
        for name in names:
            local[name]().wait()

    def wait_gathered(*names):
        for name in names:
            gathered[name]()

    def gather(*names):
        for name, _, dst in pairs:
            if name in names:
                local[name]().wait()
                copies = [(dst.at[0], dst.at[1], core)]
                extent = functools.partial(dst.at.__getitem__, 1)
                gathered[name] = group(copies, extent, halves.index(name))

    def pass_on(turn):
        if turn:
            pl.semaphore_wait(meet_sem.at[turn - 1], len(passing))
        if turn < 3:
            for device in passing:
                pl.semaphore_signal(
                    meet_sem.at[turn], inc=1, device_id=device, device_id_type=MESH
                )

    def meet():
        pl.semaphore_wait(barrier, len(greeted))
        pass_on(0)
        gather("wq", "wkv", "wo")
        for name in local:
            if name not in at_once:
                local[name]().start()

    apart(meet)

    apart(wait_for, "span", "joint")
    spans = jnp.zeros((own_seqs, AC), jnp.int32)
    for seq in range(own_seqs):
        spans = jnp.where(iota((own_seqs, AC), 0) == seq, span_s[seq], spans)
    joints = (joint_v[...] > 0).astype(F32).astype(BF)
    spread = (iota((JOINTS, AC), 1) % JOINTS == iota((JOINTS, AC), 0)).astype(F32).astype(BF)
    valid = jnp.where(iota((own_seqs, AC), 1) // JOINTS < spans, nn(joints, spread), 0.0)
    ent_v[0] = jnp.broadcast_to(jnp.sum(valid, axis=0, keepdims=True), (8, AC))
    pending = []

    def entries_begin():
        copies = [(ent_v.at[0], ent_r.at[0], core)]
        pending.append(group(copies, lambda: ent_r.at[0], ent_slot))

    apart(entries_begin)

    apart(wait_for, "tokens", "stem_norm")
    stem_gain = stem_norm_v[...].astype(F32).reshape(1, D)
    half = own_seqs * SEQ_LEN // 2
    for start in (0, half):
        at = pl.ds(start, half)
        raw = x_v[at, :]
        centred = raw.astype(F32) - nn(raw, mean_mat)
        square = centred * centred
        upper = square.astype(BF)
        lower = (square - upper.astype(F32)).astype(BF)
        inv = lax.rsqrt(nn(jnp.concatenate([upper, lower], axis=1), mean_twice) + epsilon)
        unit = centred * inv
        inv_v[at, :] = inv
        next_v[at, 0:D] = (unit * stem_gain).astype(BF)
        next_v[at, D : 2 * D] = jnp.ones((half, D), BF)

    def both(ref, *index):
        return jnp.concatenate([ref[(0,) + index], ref[(1,) + index]], axis=0)

    def heads_below(matrix):
        return (matrix[None] * head_mask).reshape(HEADS * D, D)

    def heads_beside(matrix):
        return jnp.concatenate([matrix * row_mask[head] for head in range(HEADS)], axis=1)

    def lanes_beside(cube):
        return jnp.concatenate([cube[head] for head in range(HEADS)], axis=1)

    apart(gather, "wqkv", "wout")
    apart(wait_for, "stem_latent")
    apart(wait_gathered, "wq", "wkv", "wo")
    latent = stem_latent_v[...]
    wq_t = both(wq_v)
    wk_t, wv_t = both(wkv_v, 0), both(wkv_v, 1)
    stem_q = nt(latent, wq_t).astype(BF).astype(F32) * HD ** (-0.5)
    q_diag = (jnp.concatenate([stem_q] * HEADS, axis=0) * diag_heads).astype(BF)
    fold = nn(q_diag, wk_t)
    fold_b = fold.astype(BF)
    apart(gather, "wup", "wdn", "bup")
    seq_rows = [pl.ds(seq * SEQ_LEN, SEQ_LEN) for seq in range(own_seqs)]
    scores = [nt(fold_b, next_v[at, 0:D]) for at in seq_rows]
    apart_wo = both(wo_v)
    wv_cols = wv_t.T
    stem_mats = nn(heads_below(wv_cols), apart_wo).astype(BF)
    mixed, shares, sums = [], [], []
    for seq, at in enumerate(seq_rows):
        tops = jnp.max(scores[seq], axis=1, keepdims=True)
        probs = jnp.exp(scores[seq] - tops).astype(BF)
        e_v[:, seq * SEQ_LEN : (seq + 1) * SEQ_LEN] = probs
        both_sums = nn(probs, next_v[at, :])
        share = 1.0 / both_sums[:, D:]
        shares.append(share)
        sums.append(both_sums[:, :D])
        mixed.append((both_sums[:, :D] * share).astype(BF))

    def by_head(head):
        return jnp.concatenate([part[head * LAT : (head + 1) * LAT] for part in mixed], axis=0)

    mixed_heads = [by_head(head) for head in range(HEADS)]
    latent_f = latent.astype(F32)
    hidden = jnp.concatenate([latent_f] * own_seqs, axis=0) + nn(
        jnp.concatenate(mixed_heads, axis=1), stem_mats
    )
    stem_wo = apart_wo

    def stem_heads_out():
        below = nt(jnp.concatenate(mixed_heads, axis=0), wv_t).reshape(HEADS, rows, D)
        return jnp.sum(below * head_mask.astype(F32), axis=0).astype(BF)


    apart(wait_for, "norm_attn", "norm_mlp", "b_down", "w_act", "b_act", "targets")
    apart(wait_gathered, "wqkv", "wout")
    apart(pass_on, 1)
    gain_attn = norm_attn_v[...].astype(F32)
    gain_mlp = norm_mlp_v[...].astype(F32)
    down_bias = b_down_v[...].astype(F32)

    def row_blocks_beside(matrix):
        return jnp.concatenate([matrix[head * D : (head + 1) * D] for head in range(HEADS)], axis=1)

    def lane_blocks_below(matrix):
        return jnp.concatenate(
            [matrix[:, head * D : (head + 1) * D] for head in range(HEADS)], axis=0
        )

    def trunk_forward(residual, layer):
        gain_a, gain_m = gain_attn[layer : layer + 1], gain_mlp[layer : layer + 1]
        qkv = jnp.concatenate([both(wqkv_v, layer, part_at) for part_at in range(3)], axis=0)
        out_mat = both(wout_v, layer)
        out_mats = nn(heads_below(out_mat.T), qkv[2 * D :]).astype(BF)
        normed, unit_a, inv_a = norm_rows(residual, gain_a)
        rows_a = normed.astype(BF)
        flat = nt(rows_a, qkv).astype(BF)
        queries = flat[:, :D] * jnp.asarray(HD ** (-0.5), BF)
        keys = flat[:, D : 2 * D]
        scores = nt(heads_below(keys), queries).reshape(HEADS, rows, rows) + block_add[None]
        moved_t = row_blocks_beside(nt(out_mats, rows_a).astype(BF))
        exped = jnp.exp(scores - jnp.max(scores, axis=1, keepdims=True))
        probs = exped / jnp.sum(exped, axis=1, keepdims=True)
        probs_b = probs.astype(BF)
        probs_flat = probs_b.reshape(HEADS * rows, rows)
        middle = residual + nn(moved_t, probs_flat).T
        keys_t = nt(qkv[D : 2 * D], rows_a).astype(BF) * jnp.asarray(HD ** (-0.5), BF)
        values_t = nt(qkv[2 * D :], rows_a).astype(BF)
        if layer == 0:
            apart(wait_gathered, "wup", "wdn", "bup")
        up_mat = jnp.concatenate([wup_v[0, layer], wup_v[1, layer]], axis=1)
        down_mat = both(wdn_v, layer)
        up_bias = jnp.concatenate([bup_v[0], bup_v[1]], axis=1).astype(F32)
        normed_m, unit_m, inv_m = norm_rows(middle, gain_m)
        rows_m = normed_m.astype(BF)
        up_rows = nn(rows_m, up_mat) + up_bias[layer : layer + 1]
        attended_t = nn(heads_beside(values_t), probs_flat).astype(BF)
        moved = lane_blocks_below(nt(rows_a, out_mats).astype(BF))
        cdf = 0.5 + 0.5 * lax.erf(up_rows * (0.5**0.5))
        slope = cdf + up_rows * (jnp.exp(-0.5 * up_rows * up_rows) * 0.3989422804014327)
        hidden_act = (up_rows * cdf).astype(BF)
        output = middle + nn(hidden_act, down_mat) + down_bias[layer : layer + 1]
        saved = dict(
            gain_a=gain_a, gain_m=gain_m, qkv=qkv, out_mat=out_mat, up_mat=up_mat,
            down_mat=down_mat, unit_a=unit_a, inv_a=inv_a, rows_a=rows_a, queries=queries,
            keys_t=keys_t, moved=moved, probs=probs, probs_b=probs_b, attended_t=attended_t,
            unit_m=unit_m, inv_m=inv_m, rows_m=rows_m, slope=slope, hidden_act=hidden_act,
        )
        return output, saved

    kept = []
    for layer in range(LAYERS):
        hidden, saved = trunk_forward(hidden, layer)
        kept.append(saved)
        if layer == 0:
            apart(pass_on, 2)
        if layer == 0:
            stem_out = stem_heads_out()

    pooled = jnp.sum(hidden.reshape(own_seqs, LAT, D), axis=1)
    act_mat = w_act_v[...]

    def summed3(stacked):
        return stacked[0:own_seqs] + stacked[own_seqs : 2 * own_seqs] + stacked[2 * own_seqs :]

    pred = summed3(nn(split_rows(pooled), act_mat)) + b_act_v[...].astype(F32).reshape(1, AC)
    errors = pred - targets_v[...]
    squares = jnp.sum(valid * errors * errors, axis=0, keepdims=True)
    d_pred = valid * errors
    actions[...] = valid * pred

    def act_grad():
        top, rest = pooled.astype(BF), d_pred.astype(BF)
        left = jnp.concatenate([top.astype(F32), pooled - top.astype(F32), top.astype(F32)], axis=0)
        right = jnp.concatenate(
            [rest.astype(F32), rest.astype(F32), d_pred - rest.astype(F32)], axis=0
        )
        return tn(left.astype(BF), right.astype(BF))

    d_pooled = summed3(nt(split_rows(d_pred), act_mat))
    upstream = jnp.broadcast_to(d_pooled[:, None, :], (own_seqs, LAT, D)).reshape(rows, D)

    first_row = [sum(CHUNKS[:chunk]) for chunk in range(len(CHUNKS))]
    first_piece = [begin // radices[0] for begin in first_row]
    live = {}
    first_direct = {
        chunk: sum(CHUNKS[before] for before in DIRECT[:at]) // radices[0]
        for at, chunk in enumerate(DIRECT)
    }

    def put(chunk, offset, mine, others):
        at = pl.ds(first_row[chunk] + offset, mine.shape[0])
        own[at, :] = mine.astype(BF)
        oth[at, :] = others.astype(BF)

    def core_send(chunk):
        at = pl.ds(first_row[chunk], CHUNKS[chunk])
        live[chunk] = group([(oth.at[at], rcv.at[at], core)], lambda: rcv.at[at], chunk)

    def scatter_both(chunk):
        size = CHUNKS[chunk] // radices[0]
        at = pl.ds(first_row[chunk], CHUNKS[chunk])
        here = pl.ds(first_direct[chunk], size)
        copies = []
        for offset in far_first(radices[0]) + [0]:
            piece = pl.ds(piece_of[size][offset], size)
            if offset:
                device, across = partner(0, offset), (partner(0, offset)[0], 1 - mp)
                copies.append((own.at[at].at[piece], direct_r.at[offset - 1, here], device))
            else:
                across = core
            dst = direct_r.at[radices[0] - 1 + offset, here]
            copies.append((oth.at[at].at[piece], dst, across))
        live[chunk] = group(copies, lambda: direct_r.at[:, here], chunk)

    def received(chunk):
        live.pop(chunk)()

    def scatter(chunk):
        received(chunk)
        at = pl.ds(first_row[chunk], CHUNKS[chunk])
        snd[at, :] = (own[at, :].astype(F32) + rcv[at, :].astype(F32)).astype(BF)
        size = CHUNKS[chunk] // radices[0]
        here = pl.ds(first_piece[chunk], size)
        copies = [
            (
                snd.at[at].at[pl.ds(piece_of[size][offset], size)],
                rs_r.at[offset - 1, here],
                partner(0, offset),
            )
            for offset in far_first(radices[0])
        ]
        live[chunk] = group(copies, lambda: rs_r.at[pl.ds(0, radices[0] - 1), here], chunk)

    def share_on(chunk, level):
        received(chunk)
        size = CHUNKS[chunk] // radices[0]
        here = pl.ds(first_piece[chunk], size)
        if level == 1 and chunk in DIRECT:
            whole = own.at[pl.ds(first_row[chunk], CHUNKS[chunk])]
            mine = whole[pl.ds(piece_of[size][0], size), :].astype(F32)
            there = pl.ds(first_direct[chunk], size)
            got = [direct_r[at, there, :].astype(F32) for at in range(2 * radices[0] - 1)]
        elif level == 1:
            whole = snd.at[pl.ds(first_row[chunk], CHUNKS[chunk])]
            mine = whole[pl.ds(piece_of[size][0], size), :].astype(F32)
            got = [rs_r[at, here, :].astype(F32) for at in range(radices[0] - 1)]
        else:
            mine = part[level - 2, here, :].astype(F32)
            got = [full_r[level - 2, at, here, :].astype(F32) for at in range(radices[level - 1] - 1)]
        total = tree(mine, got).astype(BF)
        if level < len(radices):
            part[level - 1, here, :] = total
            others = radices[level] - 1
            copies = [
                (part.at[level - 1, here], full_r.at[level - 1, at, here], partner(level, at + 1))
                for at in range(others)
            ]
            live[chunk] = group(
                copies, lambda: full_r.at[level - 1, pl.ds(0, others), here], chunk
            )
            return
        mine_at = pl.ds(piece_of[size][0], size)
        done = fin.at[pl.ds(first_row[chunk], CHUNKS[chunk])]
        done[mine_at, :] = total
        copies = [
            (done.at[mine_at], done.at[mine_at], partner(0, offset))
            for offset in far_first(radices[0])
        ]
        rest = pl.ds(first_row[chunk], (radices[0] - 1) * size)
        live[chunk] = group(copies, lambda: fin.at[rest], chunk)

    last = len(radices)

    def back_mlp(upstream, layer, chunk):
        kv = kept[layer]
        grad_top = upstream.astype(BF)
        small_v[16 + 5 + layer : 16 + 6 + layer, :] = jnp.sum(
            grad_top.astype(F32), axis=0, keepdims=True
        )
        d_hidden = nt(grad_top, kv["down_mat"])
        d_upper = (kv["slope"] * d_hidden).astype(BF)
        d_rows = nt(d_upper, kv["up_mat"])
        d_middle = upstream + norm_back(d_rows, kv["unit_m"], kv["inv_m"], kv["gain_m"])
        small_v[16 + 3 + layer : 16 + 4 + layer, :] = jnp.sum(
            d_rows * kv["unit_m"], axis=0, keepdims=True
        )
        d_bias = jnp.sum(d_upper.astype(F32), axis=0, keepdims=True)
        for block in range(4):
            row = 32 + 4 * layer + block
            small_v[row : row + 1, :] = d_bias[:, block * D : (block + 1) * D]
        d_down = tn(kv["hidden_act"], grad_top)
        d_up = tn(kv["rows_m"], d_upper)
        put(chunk, 0, d_up[:, 0:128], d_up[:, 256:384])
        put(chunk, 128, d_up[:, 128:256], d_up[:, 384:512])
        if layer == 1:
            put(chunk + 1, 0, d_down[0:256], d_down[256:512])
        else:
            put(chunk, 256, d_down[0:256], d_down[256:512])
        return d_middle

    def back_attn(d_middle, layer, chunk):
        kv = kept[layer]
        grad_attn = d_middle.astype(BF)
        d_probs = nt(kv["moved"], grad_attn).reshape(HEADS, rows, rows)
        d_mixed = nt(grad_attn, kv["out_mat"]).astype(BF)
        probs = kv["probs"]
        weighted = probs * d_probs
        inner = jnp.sum(weighted, axis=1, keepdims=True)
        d_scores = (weighted - probs * inner).astype(BF)
        d_values = nn(lanes_beside(kv["probs_b"]), heads_below(d_mixed)).astype(BF)
        d_q_t = nn(heads_beside(kv["keys_t"]), d_scores.reshape(HEADS * rows, rows))
        d_keys = nn(lanes_beside(d_scores), heads_below(kv["queries"])).astype(BF)
        grads = jnp.concatenate([d_q_t.T.astype(BF), d_keys, d_values], axis=1)
        d_rows = nn(grads, kv["qkv"])
        small_v[16 + 1 + layer : 16 + 2 + layer, :] = jnp.sum(
            d_rows * kv["unit_a"], axis=0, keepdims=True
        )
        d_input = d_middle + norm_back(d_rows, kv["unit_a"], kv["inv_a"], kv["gain_a"])
        d_out = nn(kv["attended_t"], grad_attn)
        d_qkv = tn(grads, kv["rows_a"])
        for place in range(3):
            begin = place * D
            put(chunk, place * 64, d_qkv[begin : begin + 64], d_qkv[begin + 64 : begin + 128])
        put(chunk, 192, d_out[0:64], d_out[64:128])
        return d_input

    apart(pass_on, 3)
    apart(entries_step, 0)
    upstream = back_mlp(upstream, 1, 0)
    apart(scatter_both, 0)
    apart(core_send, 1)
    upstream = back_attn(upstream, 1, 2)
    d_act = act_grad()
    put(2, 256, d_act, d_act)
    apart(core_send, 2)
    upstream = back_mlp(upstream, 0, 3)
    apart(core_send, 3)
    apart(scatter, 1)
    upstream = back_attn(upstream, 0, 4)
    apart(scatter, 2)

    grad_stem = upstream.astype(BF)
    back_flat = nt(grad_stem, stem_mats)
    back_v = [
        jnp.concatenate(
            [
                back_flat[seq * LAT : (seq + 1) * LAT, head * D : (head + 1) * D]
                for head in range(HEADS)
            ],
            axis=0,
        )
        for seq in range(own_seqs)
    ]
    d_out_t = nt(stem_wo, grad_stem).astype(BF)
    d_stem_wo = tn(stem_out, grad_stem)
    put(4, 256, d_stem_wo[0:64], d_stem_wo[64:128])
    d_wv = nn(heads_beside(d_out_t), jnp.concatenate(mixed_heads, axis=0))
    put(4, 320, d_wv[0:64], d_wv[64:128])
    apart(core_send, 4)
    apart(scatter, 3)

    gain_sum = jnp.zeros((D, D), F32)
    folds_v, inners = [], []
    for seq in range(own_seqs):
        gain_sum += back_v[seq] * mixed[seq].astype(F32)
        folded = (back_v[seq] * shares[seq]).astype(BF)
        folds_v.append(folded)
        inner = jnp.sum(folded.astype(F32) * sums[seq], axis=1, keepdims=True)
        inners.append(inner * shares[seq][:, 0:1])
    for seq, at in enumerate(seq_rows):
        lanes = slice(seq * SEQ_LEN, (seq + 1) * SEQ_LEN)
        d_probs = nt(folds_v[seq], next_v[at, 0:D])
        ds_v[:, lanes] = (e_v[:, lanes].astype(F32) * (d_probs - inners[seq])).astype(BF)
    d_fold = nn(ds_v[...], next_v[:, 0:D])
    apart(scatter, 4)

    d_fold_b = d_fold.astype(BF)
    d_wk = nn(q_diag.astype(F32).T.astype(BF), d_fold_b)
    d_q = nt(d_fold_b, wk_t) * diag_heads
    d_q = jnp.sum(d_q.reshape(HEADS, LAT, D), axis=0) * HD ** (-0.5)
    d_latent = jnp.sum(upstream.reshape(own_seqs, LAT, D), axis=0) + nn(d_q.astype(BF), wq_t)
    small_v[0:16, :] = d_latent
    gain_rows = jnp.sum(gain_sum + d_fold * fold, axis=0, keepdims=True)
    small_v[16:17, :] = gain_rows / stem_gain
    small_v[23:24, :] = jnp.sum(d_pred, axis=0, keepdims=True)
    small_v[24:25, :] = squares
    for layer in range(LAYERS):
        small_v[25 + 2 * layer : 27 + 2 * layer, :] = small_v[32 + 4 * layer : 34 + 4 * layer, :]
    small_v[29:32, :] = jnp.zeros((3, D), F32)
    shared = small_v[0:32, :]
    d_q_other = jnp.concatenate([d_q[:, 64:], d_q[:, :64]], axis=1)
    put(5, 0, d_wk[0:64], d_wk[64:128])
    put(5, 64, d_q, d_q_other)
    put(5, 80, shared, shared)
    for layer in range(LAYERS):
        small_v[25 + 2 * layer : 27 + 2 * layer, :] = small_v[34 + 4 * layer : 36 + 4 * layer, :]
    oth[first_row[5] + 96 : first_row[5] + 112, :] = small_v[16:32, :].astype(BF)
    own[first_row[5] + 112 : first_row[5] + 128, :] = jnp.zeros((16, D), BF)
    oth[first_row[5] + 112 : first_row[5] + 128, :] = jnp.zeros((16, D), BF)
    apart(scatter_both, 5)
    apart(entries_step, 1)

    fold_g = (fold * stem_gain).astype(BF)
    fold_side = jnp.concatenate([fold_g, nn(fold_g, mean_mat).astype(BF)], axis=1)

    def token_grads(seq):
        at = pl.ds(seq * SEQ_LEN, SEQ_LEN)
        lanes = slice(seq * SEQ_LEN, (seq + 1) * SEQ_LEN)
        left = jnp.concatenate([ds_v[:, lanes], e_v[:, lanes]], axis=0)
        value_g = (folds_v[seq].astype(F32) * stem_gain).astype(BF)
        value_side = jnp.concatenate([value_g, nn(value_g, mean_mat).astype(BF)], axis=1)
        both_grads = tn(left, jnp.concatenate([fold_side, value_side], axis=0))
        scaled = both_grads[:, :D]
        raw = x_v[at, :]
        unit = (raw.astype(F32) - nn(raw, mean_mat)) * inv_v[at, :]
        slope_mean = nn((scaled * unit).astype(BF), mean_mat)
        grad_tokens[at, :] = inv_v[at, :] * (scaled - both_grads[:, D:] - unit * slope_mean)

    order = (
        (1, share_on, 0, 1),
        (3, share_on, 1, 1),
        (5, share_on, 2, 1),
        (8, share_on, 3, 1),
        (8, share_on, 0, 2),
        (8, share_on, 4, 1),
        (8, share_on, 5, 1),
        (8, share_on, 1, 2),
    )
    for seq in range(own_seqs):
        for place, *step in order:
            if place == seq:
                apart(*step)
        token_grads(seq)
    for place, *step in order:
        if place >= own_seqs:
            apart(*step)

    for level in range(2, last):
        apart(entries_step, level)
    entries = jnp.sum(entries_step(last)[0:1], axis=1, keepdims=True)
    total_seqs = own_seqs * lax.axis_size("dp") * lax.axis_size("mp")
    factor = total_seqs * AC / entries
    grad_tokens[...] = grad_tokens[...] * factor

    for chunk, level in ((2, 2), (3, 2), (4, 2), (5, 2)):
        apart(share_on, chunk, level)
    for level in range(3, last + 1):
        for chunk in range(len(CHUNKS)):
            apart(share_on, chunk, level)

    def whole(chunk, begin, count):
        at = first_row[chunk] + begin
        return fin[at : at + count, :].astype(F32) * factor

    def finish(chunk):
        received(chunk)
        if chunk in (0, 3):
            layer = 1 if chunk == 0 else 0
            d_up_out[layer, :, 0:128] = whole(chunk, 0, 128)
            d_up_out[layer, :, 128:256] = whole(chunk, 128, 128)
        if chunk == 1:
            d_down_out[1] = whole(1, 0, 256)
        if chunk == 3:
            d_down_out[0] = whole(3, 256, 256)
        if chunk in (2, 4):
            layer = 1 if chunk == 2 else 0
            for place in range(3):
                d_qkv_out[layer, place] = whole(chunk, 64 * place, 64)
            d_out_out[layer] = whole(chunk, 192, 64)
        if chunk == 2:
            d_act_out[...] = whole(2, 256, 128)
        if chunk == 4:
            d_stem_wo_out[...] = whole(4, 256, 64)
            d_stem_wkv[1] = whole(4, 320, 64)
        if chunk == 5:
            d_stem_wkv[0] = whole(5, 0, 64)
            d_latent_out[...] = whole(5, 80, 16)
            at = first_row[5]
            d_stem_wq[...] = tn(fin[at + 64 : at + 80, 0:64], latent) * factor
            rest = whole(5, 96, 16)
            d_stem_norm[...] = rest[0:1].reshape(D)
            d_norm_attn[...] = rest[1:3]
            d_norm_mlp[...] = rest[3:5]
            d_b_down[...] = rest[5:7]
            d_b_act[...] = rest[7:8].reshape(D)
            for layer in range(LAYERS):
                d_b_up[layer : layer + 1, 0:128] = rest[9 + 2 * layer : 10 + 2 * layer]
                d_b_up[layer : layer + 1, 128:256] = rest[10 + 2 * layer : 11 + 2 * layer]
            summed = jnp.sum(fin[at + 96 : at + 112, :].astype(F32)[8:9], axis=1, keepdims=True)
            masked_loss[...] = jnp.broadcast_to(summed / entries, (1, D)).reshape(D)

    def all_left(*slots):
        for send_slot in slots:
            left(send_slot)

    apart(all_left, *range(len(CHUNKS), len(halves) + 1))
    for chunk in range(len(CHUNKS)):
        apart(finish, chunk)
        apart(all_left, chunk)


def copy_kernel(*refs):
    count = len(refs) // 2
    sem = refs[-1]
    copies = [
        pltpu.make_async_copy(refs[at], refs[count + at], sem.at[at]) for at in range(count)
    ]
    for copy in copies:
        copy.start()
    for copy in copies:
        copy.wait()


def on_device(radices, *args):
    (
        tokens,
        stem_norm,
        stem_latent,
        stem_wq,
        stem_wkv,
        stem_wo,
        norm_attn,
        w_qkv,
        w_out,
        norm_mlp,
        w_up,
        b_up,
        w_down,
        b_down,
        w_act,
        b_act,
        span_len,
        joint_mask,
        targets,
    ) = args
    own_seqs = targets.shape[0]
    count = own_seqs * SEQ_LEN
    rows = own_seqs * LAT
    last = len(radices)
    spread = sum(radices) - last
    vmem = pl.BlockSpec(memory_space=pltpu.VMEM)
    hbm = pl.BlockSpec(memory_space=pltpu.HBM)
    total_rows = sum(CHUNKS)
    wide = max(radices) - 1

    def summing(count_rows, dtype):
        pieces = count_rows // radices[0]
        direct_pieces = sum(CHUNKS[chunk] for chunk in DIRECT) // radices[0]
        return [
            *[pltpu.VMEM((count_rows, D), dtype)] * 4,
            pltpu.VMEM((wide, pieces, D), dtype),
            pltpu.VMEM((2 * radices[0] - 1, direct_pieces, D), dtype),
            pltpu.VMEM((last - 1, pieces, D), dtype),
            pltpu.VMEM((last - 1, wide, pieces, D), dtype),
        ]

    n_recv = 8 + (1 + last) + len(CHUNKS) * (2 + last)
    shape = jax.ShapeDtypeStruct
    outs = [
        shape((own_seqs, AC), F32),
        shape((D,), F32),
        shape((count, D), F32),
        shape((D,), F32),
        shape((LAT, D), F32),
        shape((64, D), F32),
        shape((2, 64, D), F32),
        shape((64, D), F32),
        shape((LAYERS, D), F32),
        shape((LAYERS, 3, 64, D), F32),
        shape((LAYERS, 64, D), F32),
        shape((LAYERS, D), F32),
        shape((LAYERS, D, FF // 2), F32),
        shape((LAYERS, FF // 2), F32),
        shape((LAYERS, FF // 2, D), F32),
        shape((LAYERS, D), F32),
        shape((D, AC), F32),
        shape((AC,), F32),
    ]
    main = pl.pallas_call(
        functools.partial(main_kernel, radices),
        out_shape=outs,
        in_specs=[hbm] * len(args),
        out_specs=[vmem] * len(outs),
        scratch_shapes=[
            pltpu.VMEM((sum(CHUNKS), D), BF),
            pltpu.VMEM((count, D), BF),
            pltpu.VMEM((D,), BF),
            pltpu.VMEM((LAT, D), BF),
            pltpu.VMEM((2, 64, D), BF),
            pltpu.VMEM((2, 2, 64, D), BF),
            pltpu.VMEM((2, 64, D), BF),
            pltpu.VMEM((LAYERS, D), BF),
            pltpu.VMEM((2, LAYERS, 3, 64, D), BF),
            pltpu.VMEM((2, LAYERS, 64, D), BF),
            pltpu.VMEM((LAYERS, D), BF),
            pltpu.VMEM((2, LAYERS, D, FF // 2), BF),
            pltpu.VMEM((2, LAYERS, FF // 2), BF),
            pltpu.VMEM((2, LAYERS, FF // 2, D), BF),
            pltpu.VMEM((LAYERS, D), BF),
            pltpu.VMEM((D, AC), BF),
            pltpu.VMEM((AC,), BF),
            pltpu.SMEM((own_seqs,), jnp.int32),
            pltpu.VMEM((own_seqs, JOINTS), jnp.int32),
            pltpu.VMEM((own_seqs, AC), F32),
            pltpu.VMEM((count, 2 * D), BF),
            pltpu.VMEM((count, D), F32),
            pltpu.VMEM((D, count), BF),
            pltpu.VMEM((D, count), BF),
            pltpu.VMEM((40, D), F32),
            pltpu.VMEM((1 + last, 8, AC), F32),
            pltpu.VMEM((1 + spread, 8, AC), F32),
            *summing(total_rows, BF),
            pltpu.SemaphoreType.DMA((len(args),)),
            pltpu.SemaphoreType.DMA((9,)),
            pltpu.SemaphoreType.DMA((n_recv,)),
            pltpu.SemaphoreType.REGULAR((3,)),
        ],
        compiler_params=pltpu.CompilerParams(
            collective_id=0, has_side_effects=True, vmem_limit_bytes=40 * 2**20
        ),
        name="stem_trunk_head",
    )(
        *[
            pltpu.with_memory_space_constraint(arg, pltpu.HBM)
            for arg in (
                tokens,
                stem_norm,
                stem_latent,
                jnp.transpose(stem_wq),
                jnp.transpose(stem_wkv, (0, 2, 1)),
                stem_wo,
                norm_attn,
                jnp.transpose(w_qkv, (0, 1, 3, 2)),
                w_out,
                norm_mlp,
                w_up,
                b_up,
                w_down,
                b_down,
                w_act,
                b_act,
                span_len,
                joint_mask,
                targets,
            )
        ]
    )
    result = pl.pallas_call(
        copy_kernel,
        out_shape=[pltpu.HBM(out.shape, out.dtype) for out in outs],
        in_specs=[vmem] * len(outs),
        out_specs=[hbm] * len(outs),
        scratch_shapes=[pltpu.SemaphoreType.DMA((len(outs),))],
        compiler_params=pltpu.CompilerParams(vmem_limit_bytes=8 * 2**20),
        name="copy_results",
    )(*main)
    result = list(result)
    result[1] = result[1][0]
    result[5] = jnp.transpose(result[5])
    result[6] = jnp.transpose(result[6], (0, 2, 1))
    result[9] = jnp.transpose(result[9], (0, 1, 3, 2))
    return tuple(result)


def solution(mesh):
    radices = radices_of(mesh.shape["dp"])
    in_specs = (
        P(("dp", "mp"), None),
        P(),
        P(),
        P(None, "mp"),
        P(None, None, "mp"),
        P("mp", None),
        P(),
        P(None, None, None, "mp"),
        P(None, "mp", None),
        P(),
        P(None, None, "mp"),
        P(None, "mp"),
        P(None, "mp", None),
        P(),
        P(),
        P(),
        P(("dp", "mp")),
        P(("dp", "mp"), None),
        P(("dp", "mp"), None),
    )
    out_specs = (
        P(("dp", "mp"), None),
        P(),
        P(("dp", "mp"), None),
        P(),
        P(),
        P(None, "mp"),
        P(None, None, "mp"),
        P("mp", None),
        P(),
        P(None, None, None, "mp"),
        P(None, "mp", None),
        P(),
        P(None, None, "mp"),
        P(None, "mp"),
        P(None, "mp", None),
        P(),
        P(),
        P(),
    )
    return jax.shard_map(
        functools.partial(on_device, radices),
        mesh=mesh,
        in_specs=in_specs,
        out_specs=out_specs,
        check_vma=False,
    )
```

```python
import functools
import math

import jax
import jax.numpy as jnp
from jax import lax
from jax.experimental import pallas as pl
from jax.experimental.pallas import tpu as pltpu
from jax.sharding import PartitionSpec as P

HD = 16
LAT = 16
SEQ_LEN = 256
SPAN = 16
JOINTS = 8
HEADS = 8
D = 128
FF = 512
AC = 128
LAYERS = 2

F32 = jnp.float32
BF = jnp.bfloat16
MESH = pl.DeviceIdType.MESH
epsilon = 1e-05
highest = lax.Precision.HIGHEST

CHUNKS = (256, 256, 384, 512, 384, 128)
DIRECT = (0, 5)


def nn(left, right):
    return jnp.dot(left, right, preferred_element_type=F32)


def nt(left, right):
    return lax.dot_general(left, right, (((1,), (1,)), ((), ())), preferred_element_type=F32)


def tn(left, right):
    return lax.dot_general(left, right, (((0,), (0,)), ((), ())), preferred_element_type=F32)


def iota(shape, axis):
    return lax.broadcasted_iota(jnp.int32, shape, axis)


def radices_of(count):
    found = []
    while count > 1:
        radix = 8 if count % 8 == 0 else 4 if count % 4 == 0 else 2
        found.append(radix)
        count //= radix
    return found


def flip(digit, offset):
    flipped = digit
    for bit in (1, 2, 4):
        if offset & bit:
            flipped = flipped + bit - 2 * bit * ((digit // bit) % 2)
    return flipped


def far_first(radix):
    return sorted(range(1, radix), key=lambda offset: -bin(offset).count("1"))


def norm_rows(values_in, gain_vec):
    mean_rows = jnp.mean(values_in, axis=-1, keepdims=True)
    centred = values_in - mean_rows
    variance = jnp.mean(centred * centred, axis=-1, keepdims=True)
    inv_rows = lax.rsqrt(variance + epsilon)
    unit_rows = centred * inv_rows
    return unit_rows * gain_vec, unit_rows, inv_rows


def norm_back(upstream, unit_rows, inv_rows, gain_vec):
    scaled = upstream * gain_vec
    inner = (
        scaled
        - jnp.mean(scaled, axis=-1, keepdims=True)
        - unit_rows * jnp.mean(scaled * unit_rows, axis=-1, keepdims=True)
    )
    return inv_rows * inner


def split_rows(values_in):
    first = values_in.astype(BF).astype(F32)
    rest = values_in - first
    second = rest.astype(BF).astype(F32)
    return jnp.concatenate([first, second, rest - second], axis=0).astype(BF)


def main_kernel(
    radices,
    tokens_h,
    stem_norm_h,
    stem_latent_h,
    stem_wq_h,
    stem_wkv_h,
    stem_wo_h,
    norm_attn_h,
    w_qkv_h,
    w_out_h,
    norm_mlp_h,
    w_up_h,
    b_up_h,
    w_down_h,
    b_down_h,
    w_act_h,
    b_act_h,
    span_len_h,
    joint_mask_h,
    targets_h,
    *refs,
):
    count = 18
    (
        actions,
        masked_loss,
        grad_tokens,
        d_stem_norm,
        d_latent_out,
        d_stem_wq,
        d_stem_wkv,
        d_stem_wo_out,
        d_norm_attn,
        d_qkv_out,
        d_out_out,
        d_norm_mlp,
        d_up_out,
        d_b_up,
        d_down_out,
        d_b_down,
        d_act_out,
        d_b_act,
    ) = refs[:count]
    (
        fin,
        x_v,
        stem_norm_v,
        stem_latent_v,
        wq_v,
        wkv_v,
        wo_v,
        norm_attn_v,
        wqkv_v,
        wout_v,
        norm_mlp_v,
        wup_v,
        bup_v,
        wdn_v,
        b_down_v,
        w_act_v,
        b_act_v,
        span_s,
        joint_v,
        targets_v,
        next_v,
        inv_v,
        e_v,
        ds_v,
        small_v,
        ent_v,
        ent_r,
        own,
        oth,
        rcv,
        snd,
        rs_r,
        direct_r,
        part,
        full_r,
        in_sem,
        send_sem,
        recv_sem,
        meet_sem,
    ) = refs[count:]
    dp, mp = lax.axis_index("dp"), lax.axis_index("mp")
    own_seqs = targets_h.shape[0]
    rows = own_seqs * LAT
    core = (dp, 1 - mp)
    digits = [(dp // math.prod(radices[:level])) % radix for level, radix in enumerate(radices)]

    places = {}

    def partner(level, offset):
        stride = math.prod(radices[:level])
        if (level, offset) not in places:
            digit = digits[level]
            places[level, offset] = (dp + (flip(digit, offset) - digit) * stride, mp)
        return places[level, offset]

    def apart(step, *given):
        pl.when(dp >= 0)(functools.partial(step, *given))

    barrier = pltpu.get_barrier_semaphore()
    count_below = math.prod(radices[:-1])
    bits = [
        (level, bit) for level, radix in enumerate(radices) for bit in (1, 2, 4) if bit < radix
    ]
    greeted = [core] + [partner(level, bit) for level, bit in bits if radices[level] > 2]
    split = len(radices) > 1 and radices[-1] == 2
    if split:
        low = (dp // (count_below // 2)) % 2
        high = dp // count_below
        inner = (low + high) % 2
        across = (dp + (1 - 2 * high) * count_below + (1 - 2 * low) * (count_below // 2), mp)
    else:
        inner = 0

    def signal_all(semaphore):
        for device in greeted:
            pl.semaphore_signal(semaphore, inc=1, device_id=device, device_id_type=MESH)
        if split:

            @pl.when(inner == 1)
            def _():
                pl.semaphore_signal(semaphore, inc=1, device_id=across, device_id_type=MESH)

    for level, radix in enumerate(radices):
        for offset in range(1, radix):
            partner(level, offset)
    signal_all(barrier)

    piece_of = {}
    for size in sorted({chunk // radices[0] for chunk in CHUNKS}):
        piece_of[size] = [
            pl.multiple_of(flip(digits[0], offset) * size, size) for offset in range(radices[0])
        ]
    recv_slots = [0]
    leaving = {}

    def left(send_slot):
        if send_slot in leaving:
            leaving.pop(send_slot)()

    def group(copies, extent, send_slot):
        left(send_slot)
        recv_slot = recv_slots[0]
        recv_slots[0] += 1

        def copy(src, dst, device):
            return pltpu.make_async_remote_copy(
                src_ref=src,
                dst_ref=dst,
                send_sem=send_sem.at[send_slot],
                recv_sem=recv_sem.at[recv_slot],
                device_id=device,
                device_id_type=MESH,
            )

        for src, dst, device in copies:
            copy(src, dst, device).start()
        leaving[send_slot] = lambda: copy(extent(), extent(), core).wait_send()
        return lambda: copy(extent(), extent(), core).wait_recv()

    local = {}
    pairs = (
        ("tokens", tokens_h, x_v),
        ("stem_norm", stem_norm_h, stem_norm_v),
        ("stem_latent", stem_latent_h, stem_latent_v),
        ("wq", stem_wq_h, wq_v),
        ("wkv", stem_wkv_h, wkv_v),
        ("wo", stem_wo_h, wo_v),
        ("wqkv", w_qkv_h, wqkv_v),
        ("wout", w_out_h, wout_v),
        ("wup", w_up_h, wup_v),
        ("wdn", w_down_h, wdn_v),
        ("norm_attn", norm_attn_h, norm_attn_v),
        ("norm_mlp", norm_mlp_h, norm_mlp_v),
        ("bup", b_up_h, bup_v),
        ("b_down", b_down_h, b_down_v),
        ("w_act", w_act_h, w_act_v),
        ("b_act", b_act_h, b_act_v),
        ("span", span_len_h, span_s),
        ("joint", joint_mask_h, joint_v),
        ("targets", targets_h, targets_v),
    )
    halves = ("wq", "wkv", "wo", "wqkv", "wout", "wup", "wdn", "bup")

    def load(place, name, src, dst):
        here = dst.at[0] if name in halves else dst
        return pltpu.make_async_copy(src, here, in_sem.at[place])

    for place, (name, src, dst) in enumerate(pairs):
        local[name] = functools.partial(load, place, name, src, dst)
    at_once = ("tokens", "span", "joint", "stem_norm", "stem_latent", "wq", "wkv", "wo")
    for name in at_once:
        local[name]().start()

    head_mask = (
        (iota((HEADS, D, D), 2) // HD == iota((HEADS, D, D), 0)).astype(F32).astype(BF)
    )
    row_mask = (iota((HEADS, D, D), 1) // HD == iota((HEADS, D, D), 0)).astype(F32).astype(BF)
    diag_heads = (iota((D, D), 0) // LAT == iota((D, D), 1) // HD).astype(F32)
    block_add = jnp.where(iota((rows, rows), 0) // LAT == iota((rows, rows), 1) // LAT, 0.0, -1e30)
    mean_mat = jnp.full((D, D), 1.0 / D, BF)
    mean_twice = jnp.full((2 * D, D), 1.0 / D, BF)

    gathered = {}

    ent_slot = len(halves)
    ent_first = [1 + sum(radices[:level]) - level for level in range(len(radices))]

    def entries_step(level):
        pending.pop()()
        if level == 0:
            total = ent_v[0] + ent_r[0]
        else:
            first = ent_first[level - 1]
            total = tree(ent_v[level], [ent_r[first + at] for at in range(radices[level - 1] - 1)])
        if level == len(radices):
            return total
        ent_v[level + 1] = total
        first, others = ent_first[level], radices[level] - 1
        copies = [
            (ent_v.at[level + 1], ent_r.at[first + at], partner(level, at + 1))
            for at in range(others)
        ]
        pending.append(group(copies, lambda: ent_r.at[pl.ds(first, others)], ent_slot))
        return None

    def tree(mine, others):
        terms = [mine] + list(others)
        while len(terms) > 1:
            terms = [terms[at] + terms[at + 1] for at in range(0, len(terms), 2)]
        return terms[0]

    def wait_for(*names):
        for name in names:
            local[name]().wait()

    def wait_gathered(*names):
        for name in names:
            gathered[name]()

    def gather(*names):
        for name, _, dst in pairs:
            if name in names:
                local[name]().wait()
                copies = [(dst.at[0], dst.at[1], core)]
                extent = functools.partial(dst.at.__getitem__, 1)
                gathered[name] = group(copies, extent, halves.index(name))

    def pass_on(turn):
        if turn:
            pl.semaphore_wait(meet_sem.at[turn - 1], len(greeted) + inner)
        if turn < 3:
            signal_all(meet_sem.at[turn])

    def meet():
        pl.semaphore_wait(barrier, len(greeted) + inner)
        pass_on(0)
        gather("wq", "wkv", "wo")
        for name in local:
            if name not in at_once:
                local[name]().start()

    apart(meet)

    apart(wait_for, "span", "joint")
    spans = jnp.zeros((own_seqs, AC), jnp.int32)
    for seq in range(own_seqs):
        spans = jnp.where(iota((own_seqs, AC), 0) == seq, span_s[seq], spans)
    joints = (joint_v[...] > 0).astype(F32).astype(BF)
    spread = (iota((JOINTS, AC), 1) % JOINTS == iota((JOINTS, AC), 0)).astype(F32).astype(BF)
    valid = jnp.where(iota((own_seqs, AC), 1) // JOINTS < spans, nn(joints, spread), 0.0)
    ent_v[0] = jnp.broadcast_to(jnp.sum(valid, axis=0, keepdims=True), (8, AC))
    pending = []

    def entries_begin():
        copies = [(ent_v.at[0], ent_r.at[0], core)]
        pending.append(group(copies, lambda: ent_r.at[0], ent_slot))

    apart(entries_begin)

    apart(wait_for, "tokens", "stem_norm")
    stem_gain = stem_norm_v[...].astype(F32).reshape(1, D)
    half = own_seqs * SEQ_LEN // 2
    for start in (0, half):
        at = pl.ds(start, half)
        raw = x_v[at, :]
        centred = raw.astype(F32) - nn(raw, mean_mat)
        square = centred * centred
        upper = square.astype(BF)
        lower = (square - upper.astype(F32)).astype(BF)
        inv = lax.rsqrt(nn(jnp.concatenate([upper, lower], axis=1), mean_twice) + epsilon)
        unit = centred * inv
        inv_v[at, :] = inv
        next_v[at, 0:D] = (unit * stem_gain).astype(BF)
        next_v[at, D : 2 * D] = jnp.ones((half, D), BF)

    def both(ref, *index):
        return jnp.concatenate([ref[(0,) + index], ref[(1,) + index]], axis=0)

    def heads_below(matrix):
        return (matrix[None] * head_mask).reshape(HEADS * D, D)

    def heads_beside(matrix):
        return jnp.concatenate([matrix * row_mask[head] for head in range(HEADS)], axis=1)

    def lanes_beside(cube):
        return jnp.concatenate([cube[head] for head in range(HEADS)], axis=1)

    apart(gather, "wqkv", "wout")
    apart(wait_for, "stem_latent")
    apart(wait_gathered, "wq", "wkv", "wo")
    latent = stem_latent_v[...]
    wq_t = both(wq_v)
    wk_t, wv_t = both(wkv_v, 0), both(wkv_v, 1)
    stem_q = nt(latent, wq_t).astype(BF).astype(F32) * HD ** (-0.5)
    q_diag = (jnp.concatenate([stem_q] * HEADS, axis=0) * diag_heads).astype(BF)
    fold = nn(q_diag, wk_t)
    fold_b = fold.astype(BF)
    apart(gather, "wup", "wdn", "bup")
    seq_rows = [pl.ds(seq * SEQ_LEN, SEQ_LEN) for seq in range(own_seqs)]
    scores = [nt(fold_b, next_v[at, 0:D]) for at in seq_rows]
    apart_wo = both(wo_v)
    wv_cols = wv_t.T
    stem_mats = nn(heads_below(wv_cols), apart_wo).astype(BF)
    mixed, shares, sums = [], [], []
    for seq, at in enumerate(seq_rows):
        tops = jnp.max(scores[seq], axis=1, keepdims=True)
        probs = jnp.exp(scores[seq] - tops).astype(BF)
        e_v[:, seq * SEQ_LEN : (seq + 1) * SEQ_LEN] = probs
        both_sums = nn(probs, next_v[at, :])
        share = 1.0 / both_sums[:, D:]
        shares.append(share)
        sums.append(both_sums[:, :D])
        mixed.append((both_sums[:, :D] * share).astype(BF))

    def by_head(head):
        return jnp.concatenate([part[head * LAT : (head + 1) * LAT] for part in mixed], axis=0)

    mixed_heads = [by_head(head) for head in range(HEADS)]
    latent_f = latent.astype(F32)
    hidden = jnp.concatenate([latent_f] * own_seqs, axis=0) + nn(
        jnp.concatenate(mixed_heads, axis=1), stem_mats
    )
    stem_wo = apart_wo

    def stem_heads_out():
        below = nt(jnp.concatenate(mixed_heads, axis=0), wv_t).reshape(HEADS, rows, D)
        return jnp.sum(below * head_mask.astype(F32), axis=0).astype(BF)


    apart(wait_for, "norm_attn", "norm_mlp", "b_down", "w_act", "b_act", "targets")
    apart(wait_gathered, "wqkv", "wout")
    apart(pass_on, 1)
    gain_attn = norm_attn_v[...].astype(F32)
    gain_mlp = norm_mlp_v[...].astype(F32)
    down_bias = b_down_v[...].astype(F32)

    def row_blocks_beside(matrix):
        return jnp.concatenate([matrix[head * D : (head + 1) * D] for head in range(HEADS)], axis=1)

    def lane_blocks_below(matrix):
        return jnp.concatenate(
            [matrix[:, head * D : (head + 1) * D] for head in range(HEADS)], axis=0
        )

    def trunk_forward(residual, layer):
        gain_a, gain_m = gain_attn[layer : layer + 1], gain_mlp[layer : layer + 1]
        qkv = jnp.concatenate([both(wqkv_v, layer, part_at) for part_at in range(3)], axis=0)
        out_mat = both(wout_v, layer)
        out_mats = nn(heads_below(out_mat.T), qkv[2 * D :]).astype(BF)
        normed, unit_a, inv_a = norm_rows(residual, gain_a)
        rows_a = normed.astype(BF)
        flat = nt(rows_a, qkv).astype(BF)
        queries = flat[:, :D] * jnp.asarray(HD ** (-0.5), BF)
        keys = flat[:, D : 2 * D]
        scores = nt(heads_below(keys), queries).reshape(HEADS, rows, rows) + block_add[None]
        moved_t = row_blocks_beside(nt(out_mats, rows_a).astype(BF))
        exped = jnp.exp(scores - jnp.max(scores, axis=1, keepdims=True))
        probs = exped / jnp.sum(exped, axis=1, keepdims=True)
        probs_b = probs.astype(BF)
        probs_flat = probs_b.reshape(HEADS * rows, rows)
        middle = residual + nn(moved_t, probs_flat).T
        keys_t = nt(qkv[D : 2 * D], rows_a).astype(BF) * jnp.asarray(HD ** (-0.5), BF)
        values_t = nt(qkv[2 * D :], rows_a).astype(BF)
        if layer == 0:
            apart(wait_gathered, "wup", "wdn", "bup")
        up_mat = jnp.concatenate([wup_v[0, layer], wup_v[1, layer]], axis=1)
        down_mat = both(wdn_v, layer)
        up_bias = jnp.concatenate([bup_v[0], bup_v[1]], axis=1).astype(F32)
        normed_m, unit_m, inv_m = norm_rows(middle, gain_m)
        rows_m = normed_m.astype(BF)
        up_rows = nn(rows_m, up_mat) + up_bias[layer : layer + 1]
        attended_t = nn(heads_beside(values_t), probs_flat).astype(BF)
        moved = lane_blocks_below(nt(rows_a, out_mats).astype(BF))
        cdf = 0.5 + 0.5 * lax.erf(up_rows * (0.5**0.5))
        slope = cdf + up_rows * (jnp.exp(-0.5 * up_rows * up_rows) * 0.3989422804014327)
        hidden_act = (up_rows * cdf).astype(BF)
        output = middle + nn(hidden_act, down_mat) + down_bias[layer : layer + 1]
        saved = dict(
            gain_a=gain_a, gain_m=gain_m, qkv=qkv, out_mat=out_mat, up_mat=up_mat,
            down_mat=down_mat, unit_a=unit_a, inv_a=inv_a, rows_a=rows_a, queries=queries,
            keys_t=keys_t, moved=moved, probs=probs, probs_b=probs_b, attended_t=attended_t,
            unit_m=unit_m, inv_m=inv_m, rows_m=rows_m, slope=slope, hidden_act=hidden_act,
        )
        return output, saved

    kept = []
    for layer in range(LAYERS):
        hidden, saved = trunk_forward(hidden, layer)
        kept.append(saved)
        if layer == 0:
            apart(pass_on, 2)
        if layer == 0:
            stem_out = stem_heads_out()

    pooled = jnp.sum(hidden.reshape(own_seqs, LAT, D), axis=1)
    act_mat = w_act_v[...]

    def summed3(stacked):
        return stacked[0:own_seqs] + stacked[own_seqs : 2 * own_seqs] + stacked[2 * own_seqs :]

    pred = summed3(nn(split_rows(pooled), act_mat)) + b_act_v[...].astype(F32).reshape(1, AC)
    errors = pred - targets_v[...]
    squares = jnp.sum(valid * errors * errors, axis=0, keepdims=True)
    d_pred = valid * errors
    actions[...] = valid * pred

    def act_grad():
        top, rest = pooled.astype(BF), d_pred.astype(BF)
        left = jnp.concatenate([top.astype(F32), pooled - top.astype(F32), top.astype(F32)], axis=0)
        right = jnp.concatenate(
            [rest.astype(F32), rest.astype(F32), d_pred - rest.astype(F32)], axis=0
        )
        return tn(left.astype(BF), right.astype(BF))

    d_pooled = summed3(nt(split_rows(d_pred), act_mat))
    upstream = jnp.broadcast_to(d_pooled[:, None, :], (own_seqs, LAT, D)).reshape(rows, D)

    first_row = [sum(CHUNKS[:chunk]) for chunk in range(len(CHUNKS))]
    first_piece = [begin // radices[0] for begin in first_row]
    live = {}
    first_direct = {
        chunk: sum(CHUNKS[before] for before in DIRECT[:at]) // radices[0]
        for at, chunk in enumerate(DIRECT)
    }

    def put(chunk, offset, mine, others):
        at = pl.ds(first_row[chunk] + offset, mine.shape[0])
        own[at, :] = mine.astype(BF)
        oth[at, :] = others.astype(BF)

    def core_send(chunk):
        at = pl.ds(first_row[chunk], CHUNKS[chunk])
        live[chunk] = group([(oth.at[at], rcv.at[at], core)], lambda: rcv.at[at], chunk)

    def scatter_both(chunk):
        size = CHUNKS[chunk] // radices[0]
        at = pl.ds(first_row[chunk], CHUNKS[chunk])
        here = pl.ds(first_direct[chunk], size)
        copies = []
        for offset in far_first(radices[0]) + [0]:
            piece = pl.ds(piece_of[size][offset], size)
            if offset:
                device, across = partner(0, offset), (partner(0, offset)[0], 1 - mp)
                copies.append((own.at[at].at[piece], direct_r.at[offset - 1, here], device))
            else:
                across = core
            dst = direct_r.at[radices[0] - 1 + offset, here]
            copies.append((oth.at[at].at[piece], dst, across))
        live[chunk] = group(copies, lambda: direct_r.at[:, here], chunk)

    def received(chunk):
        live.pop(chunk)()

    def scatter(chunk):
        received(chunk)
        at = pl.ds(first_row[chunk], CHUNKS[chunk])
        snd[at, :] = (own[at, :].astype(F32) + rcv[at, :].astype(F32)).astype(BF)
        size = CHUNKS[chunk] // radices[0]
        here = pl.ds(first_piece[chunk], size)
        copies = [
            (
                snd.at[at].at[pl.ds(piece_of[size][offset], size)],
                rs_r.at[offset - 1, here],
                partner(0, offset),
            )
            for offset in far_first(radices[0])
        ]
        live[chunk] = group(copies, lambda: rs_r.at[pl.ds(0, radices[0] - 1), here], chunk)

    def share_on(chunk, level):
        received(chunk)
        size = CHUNKS[chunk] // radices[0]
        here = pl.ds(first_piece[chunk], size)
        if level == 1 and chunk in DIRECT:
            whole = own.at[pl.ds(first_row[chunk], CHUNKS[chunk])]
            mine = whole[pl.ds(piece_of[size][0], size), :].astype(F32)
            there = pl.ds(first_direct[chunk], size)
            got = [direct_r[at, there, :].astype(F32) for at in range(2 * radices[0] - 1)]
        elif level == 1:
            whole = snd.at[pl.ds(first_row[chunk], CHUNKS[chunk])]
            mine = whole[pl.ds(piece_of[size][0], size), :].astype(F32)
            got = [rs_r[at, here, :].astype(F32) for at in range(radices[0] - 1)]
        else:
            mine = part[level - 2, here, :].astype(F32)
            got = [full_r[level - 2, at, here, :].astype(F32) for at in range(radices[level - 1] - 1)]
        total = tree(mine, got).astype(BF)
        if level < len(radices):
            part[level - 1, here, :] = total
            others = radices[level] - 1
            copies = [
                (part.at[level - 1, here], full_r.at[level - 1, at, here], partner(level, at + 1))
                for at in range(others)
            ]
            live[chunk] = group(
                copies, lambda: full_r.at[level - 1, pl.ds(0, others), here], chunk
            )
            return
        mine_at = pl.ds(piece_of[size][0], size)
        done = fin.at[pl.ds(first_row[chunk], CHUNKS[chunk])]
        done[mine_at, :] = total
        copies = [
            (done.at[mine_at], done.at[mine_at], partner(0, offset))
            for offset in far_first(radices[0])
        ]
        rest = pl.ds(first_row[chunk], (radices[0] - 1) * size)
        live[chunk] = group(copies, lambda: fin.at[rest], chunk)

    last = len(radices)

    def back_mlp(upstream, layer, chunk):
        kv = kept[layer]
        grad_top = upstream.astype(BF)
        small_v[16 + 5 + layer : 16 + 6 + layer, :] = jnp.sum(
            grad_top.astype(F32), axis=0, keepdims=True
        )
        d_hidden = nt(grad_top, kv["down_mat"])
        d_upper = (kv["slope"] * d_hidden).astype(BF)
        d_rows = nt(d_upper, kv["up_mat"])
        d_middle = upstream + norm_back(d_rows, kv["unit_m"], kv["inv_m"], kv["gain_m"])
        small_v[16 + 3 + layer : 16 + 4 + layer, :] = jnp.sum(
            d_rows * kv["unit_m"], axis=0, keepdims=True
        )
        d_bias = jnp.sum(d_upper.astype(F32), axis=0, keepdims=True)
        for block in range(4):
            row = 32 + 4 * layer + block
            small_v[row : row + 1, :] = d_bias[:, block * D : (block + 1) * D]
        d_down = tn(kv["hidden_act"], grad_top)
        d_up = tn(kv["rows_m"], d_upper)
        put(chunk, 0, d_up[:, 0:128], d_up[:, 256:384])
        put(chunk, 128, d_up[:, 128:256], d_up[:, 384:512])
        if layer == 1:
            put(chunk + 1, 0, d_down[0:256], d_down[256:512])
        else:
            put(chunk, 256, d_down[0:256], d_down[256:512])
        return d_middle

    def back_attn(d_middle, layer, chunk):
        kv = kept[layer]
        grad_attn = d_middle.astype(BF)
        d_probs = nt(kv["moved"], grad_attn).reshape(HEADS, rows, rows)
        d_mixed = nt(grad_attn, kv["out_mat"]).astype(BF)
        probs = kv["probs"]
        weighted = probs * d_probs
        inner = jnp.sum(weighted, axis=1, keepdims=True)
        d_scores = (weighted - probs * inner).astype(BF)
        d_values = nn(lanes_beside(kv["probs_b"]), heads_below(d_mixed)).astype(BF)
        d_q_t = nn(heads_beside(kv["keys_t"]), d_scores.reshape(HEADS * rows, rows))
        d_keys = nn(lanes_beside(d_scores), heads_below(kv["queries"])).astype(BF)
        grads = jnp.concatenate([d_q_t.T.astype(BF), d_keys, d_values], axis=1)
        d_rows = nn(grads, kv["qkv"])
        small_v[16 + 1 + layer : 16 + 2 + layer, :] = jnp.sum(
            d_rows * kv["unit_a"], axis=0, keepdims=True
        )
        d_input = d_middle + norm_back(d_rows, kv["unit_a"], kv["inv_a"], kv["gain_a"])
        d_out = nn(kv["attended_t"], grad_attn)
        d_qkv = tn(grads, kv["rows_a"])
        for place in range(3):
            begin = place * D
            put(chunk, place * 64, d_qkv[begin : begin + 64], d_qkv[begin + 64 : begin + 128])
        put(chunk, 192, d_out[0:64], d_out[64:128])
        return d_input

    apart(pass_on, 3)
    apart(entries_step, 0)
    upstream = back_mlp(upstream, 1, 0)
    apart(scatter_both, 0)
    apart(core_send, 1)
    upstream = back_attn(upstream, 1, 2)
    d_act = act_grad()
    put(2, 256, d_act, d_act)
    apart(core_send, 2)
    upstream = back_mlp(upstream, 0, 3)
    apart(core_send, 3)
    apart(scatter, 1)
    upstream = back_attn(upstream, 0, 4)
    apart(scatter, 2)

    grad_stem = upstream.astype(BF)
    back_flat = nt(grad_stem, stem_mats)
    back_v = [
        jnp.concatenate(
            [
                back_flat[seq * LAT : (seq + 1) * LAT, head * D : (head + 1) * D]
                for head in range(HEADS)
            ],
            axis=0,
        )
        for seq in range(own_seqs)
    ]
    d_out_t = nt(stem_wo, grad_stem).astype(BF)
    d_stem_wo = tn(stem_out, grad_stem)
    put(4, 256, d_stem_wo[0:64], d_stem_wo[64:128])
    d_wv = nn(heads_beside(d_out_t), jnp.concatenate(mixed_heads, axis=0))
    put(4, 320, d_wv[0:64], d_wv[64:128])
    apart(core_send, 4)
    apart(scatter, 3)

    gain_sum = jnp.zeros((D, D), F32)
    folds_v, inners = [], []
    for seq in range(own_seqs):
        gain_sum += back_v[seq] * mixed[seq].astype(F32)
        folded = (back_v[seq] * shares[seq]).astype(BF)
        folds_v.append(folded)
        inner = jnp.sum(folded.astype(F32) * sums[seq], axis=1, keepdims=True)
        inners.append(inner * shares[seq][:, 0:1])
    for seq, at in enumerate(seq_rows):
        lanes = slice(seq * SEQ_LEN, (seq + 1) * SEQ_LEN)
        d_probs = nt(folds_v[seq], next_v[at, 0:D])
        ds_v[:, lanes] = (e_v[:, lanes].astype(F32) * (d_probs - inners[seq])).astype(BF)
    d_fold = nn(ds_v[...], next_v[:, 0:D])
    apart(scatter, 4)

    d_fold_b = d_fold.astype(BF)
    d_wk = nn(q_diag.astype(F32).T.astype(BF), d_fold_b)
    d_q = nt(d_fold_b, wk_t) * diag_heads
    d_q = jnp.sum(d_q.reshape(HEADS, LAT, D), axis=0) * HD ** (-0.5)
    d_latent = jnp.sum(upstream.reshape(own_seqs, LAT, D), axis=0) + nn(d_q.astype(BF), wq_t)
    small_v[0:16, :] = d_latent
    gain_rows = jnp.sum(gain_sum + d_fold * fold, axis=0, keepdims=True)
    small_v[16:17, :] = gain_rows / stem_gain
    small_v[23:24, :] = jnp.sum(d_pred, axis=0, keepdims=True)
    small_v[24:25, :] = squares
    for layer in range(LAYERS):
        small_v[25 + 2 * layer : 27 + 2 * layer, :] = small_v[32 + 4 * layer : 34 + 4 * layer, :]
    small_v[29:32, :] = jnp.zeros((3, D), F32)
    shared = small_v[0:32, :]
    d_q_other = jnp.concatenate([d_q[:, 64:], d_q[:, :64]], axis=1)
    put(5, 0, d_wk[0:64], d_wk[64:128])
    put(5, 64, d_q, d_q_other)
    put(5, 80, shared, shared)
    for layer in range(LAYERS):
        small_v[25 + 2 * layer : 27 + 2 * layer, :] = small_v[34 + 4 * layer : 36 + 4 * layer, :]
    oth[first_row[5] + 96 : first_row[5] + 112, :] = small_v[16:32, :].astype(BF)
    own[first_row[5] + 112 : first_row[5] + 128, :] = jnp.zeros((16, D), BF)
    oth[first_row[5] + 112 : first_row[5] + 128, :] = jnp.zeros((16, D), BF)
    apart(scatter_both, 5)
    apart(entries_step, 1)

    fold_g = (fold * stem_gain).astype(BF)
    fold_side = jnp.concatenate([fold_g, nn(fold_g, mean_mat).astype(BF)], axis=1)

    def token_grads(seq):
        at = pl.ds(seq * SEQ_LEN, SEQ_LEN)
        lanes = slice(seq * SEQ_LEN, (seq + 1) * SEQ_LEN)
        left = jnp.concatenate([ds_v[:, lanes], e_v[:, lanes]], axis=0)
        value_g = (folds_v[seq].astype(F32) * stem_gain).astype(BF)
        value_side = jnp.concatenate([value_g, nn(value_g, mean_mat).astype(BF)], axis=1)
        both_grads = tn(left, jnp.concatenate([fold_side, value_side], axis=0))
        scaled = both_grads[:, :D]
        raw = x_v[at, :]
        unit = (raw.astype(F32) - nn(raw, mean_mat)) * inv_v[at, :]
        slope_mean = nn((scaled * unit).astype(BF), mean_mat)
        grad_tokens[at, :] = inv_v[at, :] * (scaled - both_grads[:, D:] - unit * slope_mean)

    order = (
        (1, share_on, 0, 1),
        (3, share_on, 1, 1),
        (5, share_on, 2, 1),
        (8, share_on, 3, 1),
        (8, share_on, 0, 2),
        (8, share_on, 4, 1),
        (8, share_on, 5, 1),
        (8, share_on, 1, 2),
    )
    for seq in range(own_seqs):
        for place, *step in order:
            if place == seq:
                apart(*step)
        token_grads(seq)
    for place, *step in order:
        if place >= own_seqs:
            apart(*step)

    for level in range(2, last):
        apart(entries_step, level)
    entries = jnp.sum(entries_step(last)[0:1], axis=1, keepdims=True)
    total_seqs = own_seqs * lax.axis_size("dp") * lax.axis_size("mp")
    factor = total_seqs * AC / entries
    grad_tokens[...] = grad_tokens[...] * factor

    for chunk, level in ((2, 2), (3, 2), (4, 2), (5, 2)):
        apart(share_on, chunk, level)
    for level in range(3, last + 1):
        for chunk in range(len(CHUNKS)):
            apart(share_on, chunk, level)

    def whole(chunk, begin, count):
        at = first_row[chunk] + begin
        return fin[at : at + count, :].astype(F32) * factor

    def finish(chunk):
        received(chunk)
        if chunk in (0, 3):
            layer = 1 if chunk == 0 else 0
            d_up_out[layer, :, 0:128] = whole(chunk, 0, 128)
            d_up_out[layer, :, 128:256] = whole(chunk, 128, 128)
        if chunk == 1:
            d_down_out[1] = whole(1, 0, 256)
        if chunk == 3:
            d_down_out[0] = whole(3, 256, 256)
        if chunk in (2, 4):
            layer = 1 if chunk == 2 else 0
            for place in range(3):
                d_qkv_out[layer, place] = whole(chunk, 64 * place, 64)
            d_out_out[layer] = whole(chunk, 192, 64)
        if chunk == 2:
            d_act_out[...] = whole(2, 256, 128)
        if chunk == 4:
            d_stem_wo_out[...] = whole(4, 256, 64)
            d_stem_wkv[1] = whole(4, 320, 64)
        if chunk == 5:
            d_stem_wkv[0] = whole(5, 0, 64)
            d_latent_out[...] = whole(5, 80, 16)
            at = first_row[5]
            d_stem_wq[...] = tn(fin[at + 64 : at + 80, 0:64], latent) * factor
            rest = whole(5, 96, 16)
            d_stem_norm[...] = rest[0:1].reshape(D)
            d_norm_attn[...] = rest[1:3]
            d_norm_mlp[...] = rest[3:5]
            d_b_down[...] = rest[5:7]
            d_b_act[...] = rest[7:8].reshape(D)
            for layer in range(LAYERS):
                d_b_up[layer : layer + 1, 0:128] = rest[9 + 2 * layer : 10 + 2 * layer]
                d_b_up[layer : layer + 1, 128:256] = rest[10 + 2 * layer : 11 + 2 * layer]
            summed = jnp.sum(fin[at + 96 : at + 112, :].astype(F32)[8:9], axis=1, keepdims=True)
            masked_loss[...] = jnp.broadcast_to(summed / entries, (1, D)).reshape(D)

    def all_left(*slots):
        for send_slot in slots:
            left(send_slot)

    apart(all_left, *range(len(CHUNKS), len(halves) + 1))
    for chunk in range(len(CHUNKS)):
        apart(finish, chunk)
        apart(all_left, chunk)


def copy_kernel(*refs):
    count = len(refs) // 2
    sem = refs[-1]
    copies = [
        pltpu.make_async_copy(refs[at], refs[count + at], sem.at[at]) for at in range(count)
    ]
    for copy in copies:
        copy.start()
    for copy in copies:
        copy.wait()


def on_device(radices, *args):
    (
        tokens,
        stem_norm,
        stem_latent,
        stem_wq,
        stem_wkv,
        stem_wo,
        norm_attn,
        w_qkv,
        w_out,
        norm_mlp,
        w_up,
        b_up,
        w_down,
        b_down,
        w_act,
        b_act,
        span_len,
        joint_mask,
        targets,
    ) = args
    own_seqs = targets.shape[0]
    count = own_seqs * SEQ_LEN
    rows = own_seqs * LAT
    last = len(radices)
    spread = sum(radices) - last
    vmem = pl.BlockSpec(memory_space=pltpu.VMEM)
    hbm = pl.BlockSpec(memory_space=pltpu.HBM)
    total_rows = sum(CHUNKS)
    wide = max(radices) - 1

    def summing(count_rows, dtype):
        pieces = count_rows // radices[0]
        direct_pieces = sum(CHUNKS[chunk] for chunk in DIRECT) // radices[0]
        return [
            *[pltpu.VMEM((count_rows, D), dtype)] * 4,
            pltpu.VMEM((wide, pieces, D), dtype),
            pltpu.VMEM((2 * radices[0] - 1, direct_pieces, D), dtype),
            pltpu.VMEM((last - 1, pieces, D), dtype),
            pltpu.VMEM((last - 1, wide, pieces, D), dtype),
        ]

    n_recv = 8 + (1 + last) + len(CHUNKS) * (2 + last)
    shape = jax.ShapeDtypeStruct
    outs = [
        shape((own_seqs, AC), F32),
        shape((D,), F32),
        shape((count, D), F32),
        shape((D,), F32),
        shape((LAT, D), F32),
        shape((64, D), F32),
        shape((2, 64, D), F32),
        shape((64, D), F32),
        shape((LAYERS, D), F32),
        shape((LAYERS, 3, 64, D), F32),
        shape((LAYERS, 64, D), F32),
        shape((LAYERS, D), F32),
        shape((LAYERS, D, FF // 2), F32),
        shape((LAYERS, FF // 2), F32),
        shape((LAYERS, FF // 2, D), F32),
        shape((LAYERS, D), F32),
        shape((D, AC), F32),
        shape((AC,), F32),
    ]
    main = pl.pallas_call(
        functools.partial(main_kernel, radices),
        out_shape=outs,
        in_specs=[hbm] * len(args),
        out_specs=[vmem] * len(outs),
        scratch_shapes=[
            pltpu.VMEM((sum(CHUNKS), D), BF),
            pltpu.VMEM((count, D), BF),
            pltpu.VMEM((D,), BF),
            pltpu.VMEM((LAT, D), BF),
            pltpu.VMEM((2, 64, D), BF),
            pltpu.VMEM((2, 2, 64, D), BF),
            pltpu.VMEM((2, 64, D), BF),
            pltpu.VMEM((LAYERS, D), BF),
            pltpu.VMEM((2, LAYERS, 3, 64, D), BF),
            pltpu.VMEM((2, LAYERS, 64, D), BF),
            pltpu.VMEM((LAYERS, D), BF),
            pltpu.VMEM((2, LAYERS, D, FF // 2), BF),
            pltpu.VMEM((2, LAYERS, FF // 2), BF),
            pltpu.VMEM((2, LAYERS, FF // 2, D), BF),
            pltpu.VMEM((LAYERS, D), BF),
            pltpu.VMEM((D, AC), BF),
            pltpu.VMEM((AC,), BF),
            pltpu.SMEM((own_seqs,), jnp.int32),
            pltpu.VMEM((own_seqs, JOINTS), jnp.int32),
            pltpu.VMEM((own_seqs, AC), F32),
            pltpu.VMEM((count, 2 * D), BF),
            pltpu.VMEM((count, D), F32),
            pltpu.VMEM((D, count), BF),
            pltpu.VMEM((D, count), BF),
            pltpu.VMEM((40, D), F32),
            pltpu.VMEM((1 + last, 8, AC), F32),
            pltpu.VMEM((1 + spread, 8, AC), F32),
            *summing(total_rows, BF),
            pltpu.SemaphoreType.DMA((len(args),)),
            pltpu.SemaphoreType.DMA((9,)),
            pltpu.SemaphoreType.DMA((n_recv,)),
            pltpu.SemaphoreType.REGULAR((3,)),
        ],
        compiler_params=pltpu.CompilerParams(
            collective_id=0, has_side_effects=True, vmem_limit_bytes=40 * 2**20
        ),
        name="stem_trunk_head",
    )(
        *[
            pltpu.with_memory_space_constraint(arg, pltpu.HBM)
            for arg in (
                tokens,
                stem_norm,
                stem_latent,
                jnp.transpose(stem_wq),
                jnp.transpose(stem_wkv, (0, 2, 1)),
                stem_wo,
                norm_attn,
                jnp.transpose(w_qkv, (0, 1, 3, 2)),
                w_out,
                norm_mlp,
                w_up,
                b_up,
                w_down,
                b_down,
                w_act,
                b_act,
                span_len,
                joint_mask,
                targets,
            )
        ]
    )
    result = pl.pallas_call(
        copy_kernel,
        out_shape=[pltpu.HBM(out.shape, out.dtype) for out in outs],
        in_specs=[vmem] * len(outs),
        out_specs=[hbm] * len(outs),
        scratch_shapes=[pltpu.SemaphoreType.DMA((len(outs),))],
        compiler_params=pltpu.CompilerParams(vmem_limit_bytes=8 * 2**20),
        name="copy_results",
    )(*main)
    result = list(result)
    result[1] = result[1][0]
    result[5] = jnp.transpose(result[5])
    result[6] = jnp.transpose(result[6], (0, 2, 1))
    result[9] = jnp.transpose(result[9], (0, 1, 3, 2))
    return tuple(result)


def solution(mesh):
    radices = radices_of(mesh.shape["dp"])
    in_specs = (
        P(("dp", "mp"), None),
        P(),
        P(),
        P(None, "mp"),
        P(None, None, "mp"),
        P("mp", None),
        P(),
        P(None, None, None, "mp"),
        P(None, "mp", None),
        P(),
        P(None, None, "mp"),
        P(None, "mp"),
        P(None, "mp", None),
        P(),
        P(),
        P(),
        P(("dp", "mp")),
        P(("dp", "mp"), None),
        P(("dp", "mp"), None),
    )
    out_specs = (
        P(("dp", "mp"), None),
        P(),
        P(("dp", "mp"), None),
        P(),
        P(),
        P(None, "mp"),
        P(None, None, "mp"),
        P("mp", None),
        P(),
        P(None, None, None, "mp"),
        P(None, "mp", None),
        P(),
        P(None, None, "mp"),
        P(None, "mp"),
        P(None, "mp", None),
        P(),
        P(),
        P(),
    )
    return jax.shard_map(
        functools.partial(on_device, radices),
        mesh=mesh,
        in_specs=in_specs,
        out_specs=out_specs,
        check_vma=False,
    )
```
